32 devices in a mesh: dp: 4 (over z), space: 8 (over y, x, core).
Axes of the slice: x: 2, y: 2, z: 4, core: 2. Of those that a mesh axis runs over, the one named last changes fastest.
Arguments:
- activations: bfloat16 [4, 16, 180, 768], P('dp', 'space'), may hold values from -6 to 6
- cotangent: bfloat16 [4, 16, 180, 768], P('dp', 'space'), may hold values from -6 to 6
- w_first: bfloat16 [2, 768, 96], replicated, may hold values from -0.4375 to 0.4375
- w_second: bfloat16 [2, 768, 96], replicated, may hold values from -0.4375 to 0.4375
- b_first: float32 [2, 768], replicated, may hold values from -3 to 3
- lon_keep: int32 [8], replicated, may hold values from 0 to 90, as said below
- relu_mask: int32 [4, 16, 2, 8, 768], P('dp', None, None, 'space'), may hold values 0 or 1
- shrink_mask: int32 [4, 16, 2, 8, 768], P('dp', None, None, 'space'), may hold values 0 or 1
Outputs:
- grad_activations: bfloat16 [4, 16, 180, 768], P('dp', 'space')
- grad_w_first: float32 [2, 768, 96], P(None, 'dp')
- grad_w_second: float32 [2, 768, 96], P(None, 'dp')
- grad_b_first: float32 [2, 768], P(None, 'dp')
- grad_b_second: float32 [2, 768], P(None, 'dp')
The draws below stay inside these ranges and needn't reach their ends.
Inputs may be any that keep to these rules, and one draw needn't show every extreme that they name: `lon_keep`: 8 distinct longitude frequencies, 0 and 90 among them, in no particular order.
All inputs are finite; a program needn't handle non-finite values. No bound on the sum of `relu_mask` or of `shrink_mask` on one device may be relied on, other than what follows from the above.
Results may differ from the reference program's by a relative error of at most 0.011.
Values may be sent and summed in bfloat16 or wider, within the bound.
No kernel may reach another device: no remote copies, remote signals or barrier semaphores. Data moves between devices by JAX's collectives and lax.ppermute only.
A program may use at most 64 MiB of HBM per device.

```python
import math
import jax
import jax.numpy as jnp
from jax import lax

C = 768
BLOCKS = 8
LON = 180
BS = 96
SAMPLES = 4
LAT = 16
KW = 8


def draw_lon_keep(key, part):
    middle = jax.random.permutation(key, jnp.arange(1, LON // 2, dtype=jnp.int32))[:KW - 2]
    values = jnp.concatenate([jnp.array([0, LON // 2], dtype=jnp.int32), middle])
    return jax.random.permutation(jax.random.fold_in(key, 7), values)


def touch_ends(values, rng, low, largest):
    index_at = [jax.random.randint(jax.random.fold_in(rng, axis), (), 0, length) for axis, length in enumerate(values.shape)]
    main_axis = values.shape.index(max(values.shape))
    neighbour = index_at[:main_axis] + [(index_at[main_axis] + 1) % values.shape[main_axis]] + index_at[main_axis + 1:]
    return values.at[tuple(index_at)].set(low).at[tuple(neighbour)].set(largest)


def levels(rng, extent, split, smallest, top_value):
    loudness, own = 1.0, jax.random.fold_in(rng, 6)
    for axis_at, blocks in split:
        draws = jnp.exp(jax.random.uniform(jax.random.fold_in(own, axis_at), (blocks,), jnp.float32, smallest / len(split), top_value / len(split)))
        loudness = loudness * jnp.repeat(draws, extent[axis_at] // blocks).reshape([-1 if axis == axis_at else 1 for axis in range(len(extent))])
    return loudness


def noise(rng, shape, width, most, shards=(), held_as=jnp.bfloat16):
    loudness = levels(rng, shape, shards, -0.22, 0.18) if shards else 1.0
    result = jax.random.normal(rng, shape, jnp.float32) * width * loudness
    return jnp.minimum(jnp.maximum(result, -most), most).astype(held_as)


def setup_inputs(seed: int = 0) -> dict:
    key_list = jax.random.split(jax.random.key(seed), 9)
    return {
        "activations": noise(key_list[0], (SAMPLES, LAT, LON, C), 1.0, 6.0, ((0, 4), (1, 8))),
        "cotangent": noise(key_list[1], (SAMPLES, LAT, LON, C), 1.0, 6.0, ((0, 4), (1, 8))),
        "w_first": noise(key_list[2], (2, C, BS), (2 * BS) ** -0.5, 0.4375),
        "w_second": noise(key_list[3], (2, C, BS), (2 * BS) ** -0.5, 0.4375),
        "b_first": noise(key_list[4], (2, C), 0.5, 3.0, (), jnp.float32),
        "lon_keep": draw_lon_keep(jax.random.fold_in(key_list[8], 71), 0),
        "relu_mask": touch_ends((jax.random.randint(key_list[6], (SAMPLES, LAT, 2, KW, C), 0, 2) < 1).astype(jnp.int32), jax.random.fold_in(key_list[6], 1), 0, 1),
        "shrink_mask": touch_ends((jax.random.randint(key_list[7], (SAMPLES, LAT, 2, KW, C), 0, 4) < 3).astype(jnp.int32), jax.random.fold_in(key_list[7], 1), 0, 1),
    }


def build_tables(lon_keep, lat_len, lon_len):
    columns = jnp.arange(lon_len, dtype=jnp.int32)
    lon_phase = columns[:, None] * lon_keep[None, :] % lon_len
    lon_angle = lon_phase.astype(jnp.float32) * (2.0 * math.pi / lon_len)
    lon_table = jnp.stack([jnp.cos(lon_angle), -jnp.sin(lon_angle)], axis=1).astype(jnp.bfloat16)
    latitudes = jnp.arange(lat_len, dtype=jnp.int32)
    lat_phase = latitudes[:, None] * latitudes[None, :] % lat_len
    lat_angle = lat_phase.astype(jnp.float32) * (2.0 * math.pi / lat_len)
    cosine = jnp.cos(lat_angle)
    sine_part = jnp.sin(lat_angle)
    lat_table = jnp.stack([jnp.stack([cosine, sine_part], axis=-1), jnp.stack([-sine_part, cosine], axis=-1)], axis=1).astype(jnp.bfloat16)
    return (lon_table, lat_table)

def apply_blocks(operand, matrix):
    return jnp.einsum('mkbc,bcd->mkbd', operand.astype(jnp.float32), matrix.astype(jnp.float32))

def adjoint(operand, matrix):
    return jnp.einsum('mkbd,bcd->mkbc', operand.astype(jnp.float32), matrix.astype(jnp.float32))

def outer_sum(operand, other):
    return jnp.einsum('mkbc,mkbd->bcd', operand.astype(jnp.float32), other.astype(jnp.float32))

def reference(activations, cotangent, w_first, w_second, b_first, lon_keep, relu_mask, shrink_mask):
    lon_table, lat_table = build_tables(lon_keep, LAT, LON)
    lon_wide = lon_table.astype(jnp.float32)
    lat_wide = lat_table.astype(jnp.float32)
    ortho_scale = 1.0 / math.sqrt(LAT * LON)
    doubled = jnp.where((lon_keep == 0) | (2 * lon_keep == LON), 1.0, 2.0).astype(jnp.float32)
    first_blocks = w_first.reshape(2, BLOCKS, BS, BS)
    second_blocks = w_second.reshape(2, BLOCKS, BS, BS)
    bias_blocks = b_first.reshape(2, BLOCKS, BS)

    def spectrum(field_in):
        along_lon = jnp.einsum('hwc,wpk->hpkc', field_in.astype(jnp.float32), lon_wide).astype(jnp.bfloat16)
        return (jnp.einsum('mphq,hqkc->mpkc', lat_wide, along_lon.astype(jnp.float32)) * ortho_scale).astype(jnp.bfloat16)

    def blocked(array):
        return array.reshape(LAT, 2, KW, BLOCKS, BS)

    def one_sample(totals, inputs):
        field_in, tangent, relu_bits, shrink_bits = inputs
        spec_act = blocked(spectrum(field_in))
        spec_cot = spectrum(tangent)
        relu_gate = blocked(relu_bits) > 0
        grad_out = blocked(jnp.where(shrink_bits > 0, doubled[None, None, :, None] * spec_cot.astype(jnp.float32), 0.0).astype(jnp.bfloat16))
        act_real = spec_act[:, 0]
        act_imag = spec_act[:, 1]
        pre_real = apply_blocks(act_real, first_blocks[0]) - apply_blocks(act_imag, first_blocks[1]) + bias_blocks[0]
        pre_imag = apply_blocks(act_real, first_blocks[1]) + apply_blocks(act_imag, first_blocks[0]) + bias_blocks[1]
        hidden = jnp.where(relu_gate, jnp.stack([pre_real, pre_imag], axis=1), 0.0).astype(jnp.bfloat16)
        out_real = grad_out[:, 0]
        out_imag = grad_out[:, 1]
        hidden_real = adjoint(out_real, second_blocks[0]) + adjoint(out_imag, second_blocks[1])
        hidden_imag = -adjoint(out_real, second_blocks[1]) + adjoint(out_imag, second_blocks[0])
        grad_pre = jnp.where(relu_gate, jnp.stack([hidden_real, hidden_imag], axis=1), 0.0).astype(jnp.bfloat16)
        pre_grad_real = grad_pre[:, 0]
        pre_grad_imag = grad_pre[:, 1]
        spec_real = adjoint(pre_grad_real, first_blocks[0]) + adjoint(pre_grad_imag, first_blocks[1])
        spec_imag = -adjoint(pre_grad_real, first_blocks[1]) + adjoint(pre_grad_imag, first_blocks[0])
        grad_spec = jnp.stack([spec_real, spec_imag], axis=1).astype(jnp.bfloat16).reshape(LAT, 2, KW, C)
        first_grad = jnp.stack([outer_sum(act_real, pre_grad_real) + outer_sum(act_imag, pre_grad_imag), outer_sum(act_real, pre_grad_imag) - outer_sum(act_imag, pre_grad_real)])
        hid_real = hidden[:, 0]
        hid_imag = hidden[:, 1]
        second_grad = jnp.stack([outer_sum(hid_real, out_real) + outer_sum(hid_imag, out_imag), outer_sum(hid_real, out_imag) - outer_sum(hid_imag, out_real)])
        bias_first = lax.optimization_barrier(jnp.sum(grad_pre, axis=(0, 2), dtype=jnp.float32))
        bias_second = lax.optimization_barrier(jnp.sum(grad_out, axis=(0, 2), dtype=jnp.float32))
        grad_lat = jnp.einsum('mqhp,mqkc->hpkc', lat_wide, grad_spec.astype(jnp.float32)).astype(jnp.bfloat16)
        grad_field = (jnp.einsum('wpk,hpkc->hwc', lon_wide, grad_lat.astype(jnp.float32)) * ortho_scale).astype(jnp.bfloat16)
        updated = (totals[0] + first_grad, totals[1] + second_grad, totals[2] + bias_first, totals[3] + bias_second)
        return (updated, grad_field)
    start_totals = (jnp.zeros((2, BLOCKS, BS, BS), jnp.float32), jnp.zeros((2, BLOCKS, BS, BS), jnp.float32), jnp.zeros((2, BLOCKS, BS), jnp.float32), jnp.zeros((2, BLOCKS, BS), jnp.float32))
    totals, grad_fields = lax.scan(one_sample, start_totals, (activations, cotangent, relu_mask, shrink_mask))
    grad_norm = 1.0 / math.sqrt(SAMPLES * LAT * KW)
    return (grad_fields, (totals[0] * grad_norm).reshape(2, C, BS), (totals[1] * grad_norm).reshape(2, C, BS), (totals[2] * grad_norm).reshape(2, C), (totals[3] * grad_norm).reshape(2, C))
```

```python
import functools
import math

import jax
import jax.numpy as jnp
import numpy as np
from jax import lax
from jax.experimental import pallas as pl
from jax.experimental.pallas import tpu as pltpu
from jax.sharding import PartitionSpec as P

C = 768
BLOCKS = 8
LON = 180
BS = 96

BF = jnp.bfloat16
F32 = jnp.float32
VMEM_LIMIT = 32 * 1024 * 1024


def latitude_matrix(lat_len, kept):
    index = np.arange(lat_len)
    angle = ((index[:, None] * index[None, :]) % lat_len).astype(np.float32) * np.float32(
        2.0 * math.pi / lat_len
    )
    cosine, sine = np.cos(angle), np.sin(angle)
    table = np.stack([np.stack([cosine, sine], -1), np.stack([-sine, cosine], -1)], 1)
    full = np.einsum("mphq,jk->pjmhqk", table, np.eye(kept, dtype=np.float32))
    return full.reshape(2 * kept * lat_len, 2 * kept * lat_len)


def dot(lhs, rhs, lhs_axis, rhs_axis):
    return lax.dot_general(
        lhs, rhs, (((lhs_axis,), (rhs_axis,)), ((), ())), preferred_element_type=F32
    )


def forward_lon_kernel(
    place, keep, act_hbm, cot_hbm, relu, shrink, out, table_out, field, sems
):
    kept = keep.shape[0]
    rows = act_hbm.shape[1]
    copies = []
    for t, source in enumerate((act_hbm, cot_hbm)):
        for h in range(rows):
            copy = pltpu.make_async_copy(
                source.at[0, h], field.at[t * rows + h], sems.at[t * rows + h]
            )
            copy.start()
            copies.append(copy)

    line = lax.broadcasted_iota(jnp.int32, (2 * kept, LON), 0)
    column = lax.broadcasted_iota(jnp.int32, (2 * kept, LON), 1)
    frequency = jnp.zeros((2 * kept, LON), jnp.int32)
    for j in range(kept):
        frequency = jnp.where(line % kept == j, keep[j], frequency)
    phase = column * frequency + jnp.where(line >= kept, LON // 4, 0)
    phase = phase % LON
    table = jnp.cos(phase.astype(F32) * (2.0 * math.pi / LON)).astype(BF)
    table_out[...] = table

    own = keep[place[1]]
    weight = jnp.where((own == 0) | (2 * own == LON), 1.0, 2.0)
    modes = relu.shape[0]
    spectra = 2 * rows * 2 * kept
    for p in range(2):
        passed = jnp.where(relu[:, p, :] > 0, 1.0, 0.0).astype(BF)
        scaled = jnp.where(shrink[:, p, :] > 0, weight, 0.0).astype(BF)
        for b in range(BLOCKS):
            lanes = slice(b * BS, (b + 1) * BS)
            out[b, spectra + p * modes : spectra + (p + 1) * modes, :] = passed[:, lanes]
            out[b, spectra + (2 + p) * modes : spectra + (3 + p) * modes, :] = scaled[:, lanes]

    for i, copy in enumerate(copies):
        copy.wait()
        lines = dot(table, field[i], 1, 0).astype(BF)
        for b in range(BLOCKS):
            out[b, i * 2 * kept : (i + 1) * 2 * kept, :] = lines[:, b * BS : (b + 1) * BS]


def spectral_kernel(
    place, pieces, first, second, bias, lat, lat_t, grad_lat, terms, *, ortho_scale, rows, kept
):
    parts = pieces.shape[0]
    per_tensor = rows * 2 * kept
    half = parts * per_tensor // 2
    modes = half // kept
    spectra = 2 * per_tensor

    def spectrum(t):
        stacked = jnp.concatenate(
            [pieces[i, t * per_tensor : (t + 1) * per_tensor, :] for i in range(parts)], axis=0
        )
        return (dot(lat[...], stacked, 1, 0) * ortho_scale).astype(BF)

    def mask(k):
        return jnp.concatenate(
            [
                pieces[j, spectra + (2 * k + p) * modes : spectra + (2 * k + p + 1) * modes, :]
                for p in range(2)
                for j in range(kept)
            ],
            axis=0,
        ).astype(F32)

    spec_act = spectrum(0)
    spec_cot = spectrum(1)
    passed = mask(0) > 0.0
    weight = mask(1)
    grad_out = jnp.where(weight > 0.0, weight * spec_cot.astype(F32), 0.0).astype(BF)

    bias_real = jnp.zeros((1, BS), F32)
    bias_imag = jnp.zeros((1, BS), F32)
    for b in range(BLOCKS):
        mine = place[1] == b
        bias_real = jnp.where(mine, bias[0:1, b * BS : (b + 1) * BS], bias_real)
        bias_imag = jnp.where(mine, bias[1:2, b * BS : (b + 1) * BS], bias_imag)

    by_real = dot(spec_act, first[0], 1, 0)
    by_imag = dot(spec_act, first[1], 1, 0)
    pre = jnp.concatenate(
        [
            by_real[:half] - by_imag[half:] + bias_real,
            by_imag[:half] + by_real[half:] + bias_imag,
        ],
        axis=0,
    )
    hidden = jnp.where(passed, pre, 0.0).astype(BF)

    def adjoint(operand, matrix):
        real = dot(operand, matrix[0], 1, 1)
        imag = dot(operand, matrix[1], 1, 1)
        return jnp.concatenate([real[:half] + imag[half:], real[half:] - imag[:half]], axis=0)

    grad_pre = jnp.where(passed, adjoint(grad_out, second), 0.0).astype(BF)

    def turned(array):
        return jnp.concatenate([array[half:], -array[:half]], axis=0)

    for a, (left, right) in enumerate(((spec_act, grad_pre), (hidden, grad_out))):
        wide = right.astype(F32)
        for p, (other, summed) in enumerate(
            ((right, wide[:half]), (turned(right), wide[half:]))
        ):
            slot = (2 * a + p - place[0]) % 4
            terms[slot, 0:BS, :] = dot(left, other, 0, 0)
            terms[slot, BS:, :] = jnp.broadcast_to(
                jnp.sum(summed, axis=0, keepdims=True), (terms.shape[1] - BS, BS)
            )

    grad_spec = adjoint(grad_pre, first).astype(BF)
    grad_lat[...] = (
        dot(lat_t[...], grad_spec, 1, 0).astype(BF).reshape(grad_lat.shape)
    )


def inverse_lon_kernel(
    table, pieces, field, first, second, bias_first, bias_second, lines, *, ortho_scale, rows, kept
):
    per = 2 * kept
    for b in range(BLOCKS):
        lines[:, b * BS : (b + 1) * BS] = pieces[b, 0 : rows * per, :]
    for h in range(rows):
        field[0, h] = (
            dot(table[...], lines[h * per : (h + 1) * per, :], 0, 0) * ortho_scale
        ).astype(BF)
    at = rows * per
    for block in range(2):
        for a, (matrix, vector) in enumerate(((first, bias_first), (second, bias_second))):
            for p in range(2):
                source = 4 * block + 2 * a + p
                place = slice(block * BS, (block + 1) * BS)
                matrix[p, place, :] = pieces[source, at : at + BS, :].astype(F32)
                vector[p : p + 1, place] = pieces[source, at + BS : at + BS + 16, :].astype(F32)[
                    0:1, :
                ]


def whole(memory=pltpu.VMEM):
    return pl.BlockSpec(memory_space=memory)


def by_blocks(
    activations, cotangent, w_first, w_second, b_first, lon_keep, relu_mask, shrink_mask
):
    groups = lax.axis_size("dp")
    parts = lax.axis_size("space")
    rows = activations.shape[1]
    lat_len = rows * parts
    kept = lon_keep.shape[0]
    ortho_scale = 1.0 / math.sqrt(lat_len * LON)
    grad_norm = 1.0 / math.sqrt(groups * lat_len * kept)
    params = pltpu.CompilerParams(vmem_limit_bytes=VMEM_LIMIT)
    place = jnp.stack([lax.axis_index("dp"), lax.axis_index("space")]).astype(jnp.int32)
    height = 2 * rows * 2 * kept + 4 * lat_len

    sent, table = pl.pallas_call(
        forward_lon_kernel,
        out_shape=(
            jax.ShapeDtypeStruct((parts, height, BS), BF),
            jax.ShapeDtypeStruct((2 * kept, LON), BF),
        ),
        in_specs=[
            whole(pltpu.SMEM),
            whole(pltpu.SMEM),
            whole(pl.ANY),
            whole(pl.ANY),
            whole(),
            whole(),
        ],
        out_specs=(whole(), whole()),
        scratch_shapes=[
            pltpu.VMEM((2 * rows, LON, C), BF),
            pltpu.SemaphoreType.DMA((2 * rows,)),
        ],
        compiler_params=params,
        name="forward_lon",
    )(
        place,
        lon_keep,
        activations,
        cotangent,
        relu_mask.reshape(lat_len, 2, C),
        shrink_mask.reshape(lat_len, 2, C),
    )
    pieces = lax.all_to_all(sent, "space", 0, 0, tiled=True)

    lat = latitude_matrix(lat_len, kept)
    size = lat.shape[0]
    grad_lat, terms = pl.pallas_call(
        functools.partial(spectral_kernel, ortho_scale=ortho_scale, rows=rows, kept=kept),
        out_shape=(
            jax.ShapeDtypeStruct((parts, rows * 2 * kept, BS), BF),
            jax.ShapeDtypeStruct((4, BS + 8, BS), F32),
        ),
        grid_spec=pltpu.PrefetchScalarGridSpec(
            num_scalar_prefetch=1,
            grid=(1,),
            in_specs=[
                pl.BlockSpec((parts, height, BS), lambda i, place: (0, 0, 0)),
                pl.BlockSpec((2, BS, BS), lambda i, place: (0, place[1], 0)),
                pl.BlockSpec((2, BS, BS), lambda i, place: (0, place[1], 0)),
                pl.BlockSpec((2, C), lambda i, place: (0, 0)),
                pl.BlockSpec((size, size), lambda i, place: (0, 0)),
                pl.BlockSpec((size, size), lambda i, place: (0, 0)),
            ],
            out_specs=(
                pl.BlockSpec((parts, rows * 2 * kept, BS), lambda i, place: (0, 0, 0)),
                pl.BlockSpec((4, BS + 8, BS), lambda i, place: (0, 0, 0)),
            ),
        ),
        compiler_params=params,
        name="spectral",
    )(
        place,
        pieces,
        w_first,
        w_second,
        b_first,
        jnp.asarray(lat, BF),
        jnp.asarray(lat.T, BF),
    )

    total = None
    for r in range(4):
        pairs = [
            (d * parts + b, (b // 2) * parts + 4 * (b % 2) + (d + r) % 4)
            for d in range(groups)
            for b in range(parts)
        ]
        arrived = lax.ppermute(terms[r], ("dp", "space"), pairs)
        total = arrived if total is None else total + arrived
    share = (total * grad_norm).astype(BF)
    share = jnp.pad(share, ((0, 8), (0, 0)))
    returned = lax.all_to_all(
        jnp.concatenate(
            [grad_lat, jnp.broadcast_to(share[None], (parts,) + share.shape)], axis=1
        ),
        "space",
        0,
        0,
        tiled=True,
    )

    keep_rows = C // groups
    return pl.pallas_call(
        functools.partial(inverse_lon_kernel, ortho_scale=ortho_scale, rows=rows, kept=kept),
        out_shape=(
            jax.ShapeDtypeStruct((1, rows, LON, C), BF),
            jax.ShapeDtypeStruct((2, keep_rows, BS), F32),
            jax.ShapeDtypeStruct((2, keep_rows, BS), F32),
            jax.ShapeDtypeStruct((2, keep_rows), F32),
            jax.ShapeDtypeStruct((2, keep_rows), F32),
        ),
        in_specs=[whole(), whole()],
        out_specs=(whole(),) * 5,
        scratch_shapes=[pltpu.VMEM((rows * 2 * kept, C), BF)],
        compiler_params=params,
        name="inverse_lon",
    )(table, returned)


def build_tables(lon_keep, lat_len, lon_len):
    columns = jnp.arange(lon_len, dtype=jnp.int32)
    lon_phase = columns[:, None] * lon_keep[None, :] % lon_len
    lon_angle = lon_phase.astype(jnp.float32) * (2.0 * math.pi / lon_len)
    lon_table = jnp.stack([jnp.cos(lon_angle), -jnp.sin(lon_angle)], axis=1).astype(jnp.bfloat16)
    latitudes = jnp.arange(lat_len, dtype=jnp.int32)
    lat_phase = latitudes[:, None] * latitudes[None, :] % lat_len
    lat_angle = lat_phase.astype(jnp.float32) * (2.0 * math.pi / lat_len)
    cosine = jnp.cos(lat_angle)
    sine_part = jnp.sin(lat_angle)
    lat_table = jnp.stack(
        [jnp.stack([cosine, sine_part], axis=-1), jnp.stack([-sine_part, cosine], axis=-1)], axis=1
    ).astype(jnp.bfloat16)
    return (lon_table, lat_table)


def apply_blocks(operand, matrix):
    return jnp.einsum("smjbc,bcd->smjbd", operand, matrix, preferred_element_type=jnp.float32)


def adjoint(operand, matrix):
    return jnp.einsum("smjbd,bcd->smjbc", operand, matrix, preferred_element_type=jnp.float32)


def outer_sum(operand, other):
    return jnp.einsum("smjbc,smjbd->bcd", operand, other, preferred_element_type=jnp.float32)


def by_frequencies(
    activations, cotangent, w_first, w_second, b_first, lon_keep, relu_mask, shrink_mask
):
    parts = lax.axis_size("space")
    samples_dev = activations.shape[0]
    lat_len = activations.shape[1] * parts
    kept = lon_keep.shape[0]
    owned = kept // parts
    lon_table, lat_table = build_tables(lon_keep, lat_len, LON)
    ortho_scale = 1.0 / math.sqrt(lat_len * LON)
    act_lon = jnp.einsum(
        "shwc,wpk->shpkc", activations, lon_table, preferred_element_type=jnp.float32
    ).astype(jnp.bfloat16)
    cot_lon = jnp.einsum(
        "shwc,wpk->shpkc", cotangent, lon_table, preferred_element_type=jnp.float32
    ).astype(jnp.bfloat16)
    act_modes, cot_modes = (
        lax.all_to_all(act_lon, "space", split_axis=3, concat_axis=1, tiled=True),
        lax.all_to_all(cot_lon, "space", split_axis=3, concat_axis=1, tiled=True),
    )

    def latitude(modes):
        summed = jnp.einsum(
            "mphq,shqjc->smpjc", lat_table, modes, preferred_element_type=jnp.float32
        )
        return (summed * ortho_scale).astype(jnp.bfloat16)

    block_shape = (samples_dev, lat_len, 2, owned, BLOCKS, BS)
    spec_act = latitude(act_modes).reshape(block_shape)
    spec_cot = latitude(cot_modes)
    own_keep = lax.dynamic_slice_in_dim(lon_keep, lax.axis_index("space") * owned, owned)
    doubled = jnp.where((own_keep == 0) | (2 * own_keep == LON), 1.0, 2.0).astype(jnp.float32)
    grad_out = (
        jnp.where(
            shrink_mask > 0, doubled[None, None, None, :, None] * spec_cot.astype(jnp.float32), 0.0
        )
        .astype(jnp.bfloat16)
        .reshape(block_shape)
    )
    relu_gate = relu_mask.reshape(block_shape) > 0
    first_blocks = w_first.reshape(2, BLOCKS, BS, BS)
    second_blocks = w_second.reshape(2, BLOCKS, BS, BS)
    bias_blocks = b_first.reshape(2, BLOCKS, BS)
    act_real = spec_act[:, :, 0]
    act_imag = spec_act[:, :, 1]
    pre_real = (
        apply_blocks(act_real, first_blocks[0])
        - apply_blocks(act_imag, first_blocks[1])
        + bias_blocks[0]
    )
    pre_imag = (
        apply_blocks(act_real, first_blocks[1])
        + apply_blocks(act_imag, first_blocks[0])
        + bias_blocks[1]
    )
    hidden = jnp.where(relu_gate, jnp.stack([pre_real, pre_imag], axis=2), 0.0).astype(jnp.bfloat16)
    out_real = grad_out[:, :, 0]
    out_imag = grad_out[:, :, 1]
    hidden_real = adjoint(out_real, second_blocks[0]) + adjoint(out_imag, second_blocks[1])
    hidden_imag = -adjoint(out_real, second_blocks[1]) + adjoint(out_imag, second_blocks[0])
    grad_pre = jnp.where(relu_gate, jnp.stack([hidden_real, hidden_imag], axis=2), 0.0).astype(
        jnp.bfloat16
    )
    pre_grad_real = grad_pre[:, :, 0]
    pre_grad_imag = grad_pre[:, :, 1]
    spec_real = adjoint(pre_grad_real, first_blocks[0]) + adjoint(pre_grad_imag, first_blocks[1])
    spec_imag = -adjoint(pre_grad_real, first_blocks[1]) + adjoint(pre_grad_imag, first_blocks[0])
    grad_spec = (
        jnp.stack([spec_real, spec_imag], axis=2)
        .astype(jnp.bfloat16)
        .reshape(samples_dev, lat_len, 2, owned, C)
    )
    first_grad = jnp.stack(
        [
            outer_sum(act_real, pre_grad_real) + outer_sum(act_imag, pre_grad_imag),
            outer_sum(act_real, pre_grad_imag) - outer_sum(act_imag, pre_grad_real),
        ]
    ).reshape(2, C, BS)
    hid_real = hidden[:, :, 0]
    hid_imag = hidden[:, :, 1]
    second_grad = jnp.stack(
        [
            outer_sum(hid_real, out_real) + outer_sum(hid_imag, out_imag),
            outer_sum(hid_real, out_imag) - outer_sum(hid_imag, out_real),
        ]
    ).reshape(2, C, BS)
    bias_first = jnp.sum(grad_pre, axis=(0, 1, 3), dtype=jnp.float32).reshape(2, C)
    bias_second = jnp.sum(grad_out, axis=(0, 1, 3), dtype=jnp.float32).reshape(2, C)
    local_terms = (first_grad, second_grad, bias_first, bias_second)
    summed = lax.psum(
        (local_terms[0], local_terms[1], local_terms[2], local_terms[3]), ("dp", "space")
    )
    share_rows = C // lax.axis_size("dp")
    row_start = lax.axis_index("dp") * share_rows

    def take_share(array):
        return lax.dynamic_slice_in_dim(array, row_start, share_rows, 1)

    totals = jax.tree.map(take_share, summed)
    grad_norm = 1.0 / math.sqrt(samples_dev * lax.axis_size("dp") * lat_len * kept)
    grad_lat = jnp.einsum(
        "mqhp,smqjc->shpjc", lat_table, grad_spec, preferred_element_type=jnp.float32
    ).astype(jnp.bfloat16)
    returned = lax.all_to_all(grad_lat, "space", split_axis=1, concat_axis=3, tiled=True)
    grad_field = (
        jnp.einsum("wpk,shpkc->shwc", lon_table, returned, preferred_element_type=jnp.float32)
        * ortho_scale
    ).astype(jnp.bfloat16)
    return (
        grad_field,
        totals[0] * grad_norm,
        totals[1] * grad_norm,
        totals[2] * grad_norm,
        totals[3] * grad_norm,
    )


def solution(mesh):
    groups, parts = mesh.shape["dp"], mesh.shape["space"]

    def per_device(*arrays):
        activations, lon_keep = arrays[0], arrays[5]
        fits = (
            parts == BLOCKS
            and 2 * groups == BLOCKS
            and activations.shape[:2] == (1, 2)
            and lon_keep.shape[0] == parts
        )
        return by_blocks(*arrays) if fits else by_frequencies(*arrays)

    return jax.shard_map(
        per_device,
        mesh=mesh,
        in_specs=(
            P("dp", "space", None, None),
            P("dp", "space", None, None),
            P(),
            P(),
            P(),
            P(),
            P("dp", None, None, "space", None),
            P("dp", None, None, "space", None),
        ),
        out_specs=(
            P("dp", "space", None, None),
            P(None, "dp", None),
            P(None, "dp", None),
            P(None, "dp"),
            P(None, "dp"),
        ),
        check_vma=False,
    )
```

```python
import functools
import math

import jax
import jax.numpy as jnp
import numpy as np
from jax import lax
from jax.experimental import pallas as pl
from jax.experimental.pallas import tpu as pltpu
from jax.sharding import PartitionSpec as P

C = 768
BLOCKS = 8
LON = 180
BS = 96

BF = jnp.bfloat16
F32 = jnp.float32
LANES = 128
THIRD = LANES - BS
VMEM_LIMIT = 32 * 1024 * 1024
WHOLE_VMEM = 60 * 1024 * 1024


def shift_of(group):
    return 2 * (group % 2) + group // 2


def block_of(group, device):
    lane = 2 * (device // 4) + device % 2
    return 2 * ((lane + shift_of(group)) % 4) + (device // 2) % 2


def owner_of(group, block):
    lane = (block // 2 + 4 - shift_of(group)) % 4
    return 4 * (lane // 2) + 2 * (block % 2) + lane % 2


def latitude_matrix(lat_len, kept):
    index = np.arange(lat_len)
    angle = ((index[:, None] * index[None, :]) % lat_len).astype(np.float32) * np.float32(
        2.0 * math.pi / lat_len
    )
    cosine, sine = np.cos(angle), np.sin(angle)
    table = np.stack([np.stack([cosine, sine], -1), np.stack([-sine, cosine], -1)], 1)
    full = np.einsum("mphq,jk->pjmhqk", table, np.eye(kept, dtype=np.float32))
    return full.reshape(2 * kept * lat_len, 2 * kept * lat_len)


def dot(lhs, rhs, lhs_axis, rhs_axis):
    return lax.dot_general(
        lhs, rhs, (((lhs_axis,), (rhs_axis,)), ((), ())), preferred_element_type=F32
    )


def fold(array):
    rows = array.shape[0] // 4
    beside = [array[3 * rows :, g * THIRD : (g + 1) * THIRD] for g in range(3)]
    return jnp.concatenate([array[: 3 * rows], jnp.concatenate(beside, axis=0)], axis=1)


def unfold(array):
    rows = array.shape[0] // 3
    beside = [array[g * rows : (g + 1) * rows, BS:] for g in range(3)]
    return jnp.concatenate([array[:, :BS], jnp.concatenate(beside, axis=1)], axis=0)


def forward_lon_kernel(
    keep_hbm, act_hbm, cot_hbm, relu_hbm, shrink_hbm, out, table_out, field, masks, keep, sems
):
    kept = keep.shape[0]
    rows = act_hbm.shape[1]
    modes = relu_hbm.shape[0]
    tiles = C // LANES
    columns = [slice(k * LANES, (k + 1) * LANES) for k in range(tiles)]
    keep_copy = pltpu.make_async_copy(keep_hbm, keep, sems.at[0])
    keep_copy.start()
    field_copies, mask_copies = [], []
    for t, source in enumerate((act_hbm, cot_hbm)):
        for k in range(tiles):
            copy = pltpu.make_async_copy(
                source.at[:, :, columns[k]], field.at[t, k], sems.at[1 + t * tiles + k]
            )
            copy.start()
            field_copies.append(copy)
    for t, source in enumerate((relu_hbm, shrink_hbm)):
        for p in range(2):
            for k in range(tiles):
                copy = pltpu.make_async_copy(
                    source.at[:, p, :, columns[k]],
                    masks.at[t, p, k],
                    sems.at[1 + (2 + 2 * t + p) * tiles + k],
                )
                copy.start()
                mask_copies.append(copy)

    keep_copy.wait()
    shape = (rows * 2 * kept, LON * rows)
    line = lax.broadcasted_iota(jnp.int32, shape, 0)
    column = lax.broadcasted_iota(jnp.int32, shape, 1)
    frequency = jnp.zeros(shape, jnp.int32)
    for j in range(kept):
        frequency = jnp.where(line % kept == j, keep[j], frequency)
    turn = jnp.where((line // kept) % 2 == 1, LON // 4, 0)
    phase = ((column // rows) * frequency + turn) % LON
    table = jnp.cos(phase.astype(F32) * (2.0 * math.pi / LON))
    table = jnp.where(line // (2 * kept) == column % rows, table, 0.0).astype(BF)
    table_out[...] = table

    group = lax.axis_index("dp")
    own = keep[lax.axis_index("space")]
    scale = jnp.where((own == 0) | (2 * own == LON), 1.0, 2.0)
    for copy in mask_copies:
        copy.wait()

    def gate(t, value):
        return jnp.concatenate(
            [
                jnp.concatenate(
                    [
                        jnp.where(masks.at[t, p, k].reshape(modes, LANES)[...] > 0, value, 0.0)
                        for k in range(tiles)
                    ],
                    axis=1,
                )
                for p in range(2)
            ],
            axis=0,
        ).astype(BF)

    passed = gate(0, 1.0)
    scaled = gate(1, scale)

    lines = []
    for t in range(2):
        found = []
        for k in range(0, tiles, 2):
            for i in range(2):
                field_copies[t * tiles + k + i].wait()
            wide = jnp.concatenate(
                [field.at[t, k + i].reshape(LON * rows, LANES)[...] for i in range(2)], axis=1
            )
            found.append(dot(table, wide, 1, 0).astype(BF))
        lines.append(jnp.concatenate(found, axis=1))

    packed = jnp.concatenate(lines + [passed, scaled], axis=0)
    for b in range(BLOCKS):
        out[owner_of(group, b)] = fold(packed[:, b * BS : (b + 1) * BS])


def spectral_kernel(
    pieces, first_all, second_all, bias, lat, lat_t, grad_lat, terms, *, ortho_scale, rows, kept
):
    device = lax.axis_index("space")
    block = block_of(lax.axis_index("dp"), device)
    parts = pieces.shape[0]
    per = rows * 2 * kept
    half = parts * per // 2
    modes = half // kept
    place = pl.ds(pl.multiple_of(block * BS, BS), BS)
    first = [first_all[p, place, :] for p in range(2)]
    second = [second_all[p, place, :] for p in range(2)]
    opened = [unfold(pieces[i]) for i in range(parts)]

    def spectrum(t):
        stacked = jnp.concatenate([piece[t * per : (t + 1) * per] for piece in opened], axis=0)
        return (dot(lat[...], stacked, 1, 0) * ortho_scale).astype(BF)

    def mask(k):
        start = 2 * per + k * 2 * modes
        return jnp.concatenate(
            [
                opened[j][start + p * modes : start + (p + 1) * modes]
                for p in range(2)
                for j in range(kept)
            ],
            axis=0,
        ).astype(F32)

    spec_act = spectrum(0)
    spec_cot = spectrum(1)
    passed = mask(0) > 0.0
    weight = mask(1)
    grad_out = jnp.where(weight > 0.0, weight * spec_cot.astype(F32), 0.0).astype(BF)

    bias_real = jnp.zeros((1, BS), F32)
    bias_imag = jnp.zeros((1, BS), F32)
    for b in range(BLOCKS):
        mine = block == b
        bias_real = jnp.where(mine, bias[0:1, b * BS : (b + 1) * BS], bias_real)
        bias_imag = jnp.where(mine, bias[1:2, b * BS : (b + 1) * BS], bias_imag)

    by_real = dot(spec_act, first[0], 1, 0)
    by_imag = dot(spec_act, first[1], 1, 0)
    pre = jnp.concatenate(
        [
            by_real[:half] - by_imag[half:] + bias_real,
            by_imag[:half] + by_real[half:] + bias_imag,
        ],
        axis=0,
    )
    hidden = jnp.where(passed, pre, 0.0).astype(BF)

    def adjoint(operand, matrix):
        real = dot(operand, matrix[0], 1, 1)
        imag = dot(operand, matrix[1], 1, 1)
        return jnp.concatenate([real[:half] + imag[half:], real[half:] - imag[:half]], axis=0)

    grad_pre = jnp.where(passed, adjoint(grad_out, second), 0.0).astype(BF)

    def turned(array):
        return jnp.concatenate([array[half:], -array[:half]], axis=0)

    at = 2 * BS * 3 // 4
    for a, (left, right) in enumerate(((spec_act, grad_pre), (hidden, grad_out))):
        slot = (a + device) % 2
        matrices = jnp.concatenate(
            [dot(left, right, 0, 0), dot(left, turned(right), 0, 0)], axis=0
        )
        terms[slot, 0:at, :] = fold(matrices).astype(BF)
        wide = right.astype(F32)
        sums = [jnp.sum(wide[p * half : (p + 1) * half], axis=0, keepdims=True) for p in range(2)]
        rest = terms.shape[1] - at
        sums = jnp.concatenate(sums + [jnp.zeros((rest - 2, BS), F32)], axis=0)
        terms[slot, at:, :] = jnp.concatenate(
            [sums, jnp.zeros((rest, THIRD), F32)], axis=1
        ).astype(BF)

    grad_spec = adjoint(grad_pre, first).astype(BF)
    lines = dot(lat_t[...], grad_spec, 1, 0)
    lines = jnp.concatenate([lines, jnp.zeros((2 * half, THIRD), F32)], axis=1).astype(BF)
    grad_lat[...] = lines.reshape(grad_lat.shape)


def inverse_lon_kernel(
    table,
    pieces,
    field_hbm,
    first_hbm,
    second_hbm,
    bias_first,
    bias_second,
    lines,
    field,
    matrices,
    sems,
    *,
    ortho_scale,
    grad_norm,
):
    rows = field_hbm.shape[1]
    per = table.shape[0]
    tiles = C // LANES
    group = lax.axis_index("dp")
    matrix_rows = 2 * BS * 3 // 4
    copies = []
    for b in range(BLOCKS):
        lines[:, b * BS : (b + 1) * BS] = pieces[owner_of(group, b), 0:per, 0:BS]
    for k in range(0, tiles, 2):
        wide = dot(table[...], lines[:, k * LANES : (k + 2) * LANES], 0, 0) * ortho_scale
        for i in range(2):
            field.at[k + i].reshape(LON * rows, LANES)[...] = wide[
                :, i * LANES : (i + 1) * LANES
            ].astype(BF)
            copy = pltpu.make_async_copy(
                field.at[k + i],
                field_hbm.at[:, :, (k + i) * LANES : (k + i + 1) * LANES],
                sems.at[k + i],
            )
            copy.start()
            copies.append(copy)
    for a, (target, vector) in enumerate(((first_hbm, bias_first), (second_hbm, bias_second))):
        for k in range(2):
            sources = [pieces[4 * y + 2 * k + a, per:, :].astype(F32) for y in range(2)]
            total = (sources[0] + sources[1]) * grad_norm
            opened = unfold(total[:matrix_rows])
            for p in range(2):
                matrices[a, p, k * BS : (k + 1) * BS, :] = opened[p * BS : (p + 1) * BS]
                vector[p : p + 1, k * BS : (k + 1) * BS] = total[
                    matrix_rows + p : matrix_rows + p + 1, :BS
                ]
        copy = pltpu.make_async_copy(matrices.at[a], target, sems.at[tiles + a])
        copy.start()
        copies.append(copy)
    for copy in copies:
        copy.wait()


def whole(memory=pltpu.VMEM):
    return pl.BlockSpec(memory_space=memory)


def by_blocks(
    activations, cotangent, w_first, w_second, b_first, lon_keep, relu_mask, shrink_mask
):
    groups = lax.axis_size("dp")
    parts = lax.axis_size("space")
    rows = activations.shape[1]
    lat_len = rows * parts
    kept = lon_keep.shape[0]
    ortho_scale = 1.0 / math.sqrt(lat_len * LON)
    grad_norm = 1.0 / math.sqrt(groups * lat_len * kept)
    params = pltpu.CompilerParams(vmem_limit_bytes=VMEM_LIMIT)
    tiles = C // LANES
    per = rows * 2 * kept
    height = (2 * per + 4 * lat_len) * 3 // 4
    term_rows = 2 * BS * 3 // 4 + 16

    sent, table = pl.pallas_call(
        forward_lon_kernel,
        out_shape=(
            jax.ShapeDtypeStruct((parts, height, LANES), BF),
            jax.ShapeDtypeStruct((per, LON * rows), BF),
        ),
        in_specs=[whole(pl.ANY)] * 5,
        out_specs=(whole(), whole()),
        scratch_shapes=[
            pltpu.VMEM((2, tiles, LON, rows, LANES), BF),
            pltpu.VMEM((2, 2, tiles, lat_len, 1, LANES), jnp.int32),
            pltpu.SMEM((kept,), jnp.int32),
            pltpu.SemaphoreType.DMA((1 + 6 * tiles,)),
        ],
        compiler_params=pltpu.CompilerParams(vmem_limit_bytes=WHOLE_VMEM),
        name="forward_lon",
    )(
        lon_keep,
        activations[0].transpose(1, 0, 2),
        cotangent[0].transpose(1, 0, 2),
        relu_mask[0],
        shrink_mask[0],
    )
    pieces = lax.all_to_all(sent, "space", 0, 0, tiled=True)

    lat = latitude_matrix(lat_len, kept)
    grad_lat, terms = pl.pallas_call(
        functools.partial(spectral_kernel, ortho_scale=ortho_scale, rows=rows, kept=kept),
        out_shape=(
            jax.ShapeDtypeStruct((parts, per, LANES), BF),
            jax.ShapeDtypeStruct((2, term_rows, LANES), BF),
        ),
        in_specs=[whole()] * 6,
        out_specs=(whole(), whole()),
        compiler_params=params,
        name="spectral",
    )(pieces, w_first, w_second, b_first, jnp.asarray(lat, BF), jnp.asarray(lat.T, BF))

    arrived = lax.ppermute(
        terms,
        ("dp", "space"),
        [
            (g * parts + c, (block_of(g, c) // 2) * parts + c)
            for g in range(groups)
            for c in range(parts)
        ],
    )
    other = lax.ppermute(arrived[1], "space", [(c, c ^ 1) for c in range(parts)])
    share = (arrived[0].astype(F32) + other.astype(F32)).astype(BF)
    returned = lax.all_to_all(
        jnp.concatenate(
            [grad_lat, jnp.broadcast_to(share[None], (parts,) + share.shape)], axis=1
        ),
        "space",
        0,
        0,
        tiled=True,
    )

    keep_rows = C // groups
    field, first, second, bias_first, bias_second = pl.pallas_call(
        functools.partial(inverse_lon_kernel, ortho_scale=ortho_scale, grad_norm=grad_norm),
        out_shape=(
            jax.ShapeDtypeStruct((LON, rows, C), BF),
            jax.ShapeDtypeStruct((2, keep_rows, BS), F32),
            jax.ShapeDtypeStruct((2, keep_rows, BS), F32),
            jax.ShapeDtypeStruct((2, keep_rows), F32),
            jax.ShapeDtypeStruct((2, keep_rows), F32),
        ),
        in_specs=[whole(), whole()],
        out_specs=(whole(pl.ANY),) * 3 + (whole(),) * 2,
        scratch_shapes=[
            pltpu.VMEM((per, C), BF),
            pltpu.VMEM((tiles, LON, rows, LANES), BF),
            pltpu.VMEM((2, 2, keep_rows, BS), F32),
            pltpu.SemaphoreType.DMA((tiles + 2,)),
        ],
        compiler_params=params,
        name="inverse_lon",
    )(table, returned)
    return field.transpose(1, 0, 2)[None], first, second, bias_first, bias_second


def build_tables(lon_keep, lat_len, lon_len):
    columns = jnp.arange(lon_len, dtype=jnp.int32)
    lon_phase = columns[:, None] * lon_keep[None, :] % lon_len
    lon_angle = lon_phase.astype(jnp.float32) * (2.0 * math.pi / lon_len)
    lon_table = jnp.stack([jnp.cos(lon_angle), -jnp.sin(lon_angle)], axis=1).astype(jnp.bfloat16)
    latitudes = jnp.arange(lat_len, dtype=jnp.int32)
    lat_phase = latitudes[:, None] * latitudes[None, :] % lat_len
    lat_angle = lat_phase.astype(jnp.float32) * (2.0 * math.pi / lat_len)
    cosine = jnp.cos(lat_angle)
    sine_part = jnp.sin(lat_angle)
    lat_table = jnp.stack(
        [jnp.stack([cosine, sine_part], axis=-1), jnp.stack([-sine_part, cosine], axis=-1)], axis=1
    ).astype(jnp.bfloat16)
    return (lon_table, lat_table)


def apply_blocks(operand, matrix):
    return jnp.einsum("smjbc,bcd->smjbd", operand, matrix, preferred_element_type=jnp.float32)


def adjoint(operand, matrix):
    return jnp.einsum("smjbd,bcd->smjbc", operand, matrix, preferred_element_type=jnp.float32)


def outer_sum(operand, other):
    return jnp.einsum("smjbc,smjbd->bcd", operand, other, preferred_element_type=jnp.float32)


def by_frequencies(
    activations, cotangent, w_first, w_second, b_first, lon_keep, relu_mask, shrink_mask
):
    parts = lax.axis_size("space")
    samples_dev = activations.shape[0]
    lat_len = activations.shape[1] * parts
    kept = lon_keep.shape[0]
    owned = kept // parts
    lon_table, lat_table = build_tables(lon_keep, lat_len, LON)
    ortho_scale = 1.0 / math.sqrt(lat_len * LON)
    act_lon = jnp.einsum(
        "shwc,wpk->shpkc", activations, lon_table, preferred_element_type=jnp.float32
    ).astype(jnp.bfloat16)
    cot_lon = jnp.einsum(
        "shwc,wpk->shpkc", cotangent, lon_table, preferred_element_type=jnp.float32
    ).astype(jnp.bfloat16)
    act_modes, cot_modes = (
        lax.all_to_all(act_lon, "space", split_axis=3, concat_axis=1, tiled=True),
        lax.all_to_all(cot_lon, "space", split_axis=3, concat_axis=1, tiled=True),
    )

    def latitude(modes):
        summed = jnp.einsum(
            "mphq,shqjc->smpjc", lat_table, modes, preferred_element_type=jnp.float32
        )
        return (summed * ortho_scale).astype(jnp.bfloat16)

    block_shape = (samples_dev, lat_len, 2, owned, BLOCKS, BS)
    spec_act = latitude(act_modes).reshape(block_shape)
    spec_cot = latitude(cot_modes)
    own_keep = lax.dynamic_slice_in_dim(lon_keep, lax.axis_index("space") * owned, owned)
    doubled = jnp.where((own_keep == 0) | (2 * own_keep == LON), 1.0, 2.0).astype(jnp.float32)
    grad_out = (
        jnp.where(
            shrink_mask > 0, doubled[None, None, None, :, None] * spec_cot.astype(jnp.float32), 0.0
        )
        .astype(jnp.bfloat16)
        .reshape(block_shape)
    )
    relu_gate = relu_mask.reshape(block_shape) > 0
    first_blocks = w_first.reshape(2, BLOCKS, BS, BS)
    second_blocks = w_second.reshape(2, BLOCKS, BS, BS)
    bias_blocks = b_first.reshape(2, BLOCKS, BS)
    act_real = spec_act[:, :, 0]
    act_imag = spec_act[:, :, 1]
    pre_real = (
        apply_blocks(act_real, first_blocks[0])
        - apply_blocks(act_imag, first_blocks[1])
        + bias_blocks[0]
    )
    pre_imag = (
        apply_blocks(act_real, first_blocks[1])
        + apply_blocks(act_imag, first_blocks[0])
        + bias_blocks[1]
    )
    hidden = jnp.where(relu_gate, jnp.stack([pre_real, pre_imag], axis=2), 0.0).astype(jnp.bfloat16)
    out_real = grad_out[:, :, 0]
    out_imag = grad_out[:, :, 1]
    hidden_real = adjoint(out_real, second_blocks[0]) + adjoint(out_imag, second_blocks[1])
    hidden_imag = -adjoint(out_real, second_blocks[1]) + adjoint(out_imag, second_blocks[0])
    grad_pre = jnp.where(relu_gate, jnp.stack([hidden_real, hidden_imag], axis=2), 0.0).astype(
        jnp.bfloat16
    )
    pre_grad_real = grad_pre[:, :, 0]
    pre_grad_imag = grad_pre[:, :, 1]
    spec_real = adjoint(pre_grad_real, first_blocks[0]) + adjoint(pre_grad_imag, first_blocks[1])
    spec_imag = -adjoint(pre_grad_real, first_blocks[1]) + adjoint(pre_grad_imag, first_blocks[0])
    grad_spec = (
        jnp.stack([spec_real, spec_imag], axis=2)
        .astype(jnp.bfloat16)
        .reshape(samples_dev, lat_len, 2, owned, C)
    )
    first_grad = jnp.stack(
        [
            outer_sum(act_real, pre_grad_real) + outer_sum(act_imag, pre_grad_imag),
            outer_sum(act_real, pre_grad_imag) - outer_sum(act_imag, pre_grad_real),
        ]
    ).reshape(2, C, BS)
    hid_real = hidden[:, :, 0]
    hid_imag = hidden[:, :, 1]
    second_grad = jnp.stack(
        [
            outer_sum(hid_real, out_real) + outer_sum(hid_imag, out_imag),
            outer_sum(hid_real, out_imag) - outer_sum(hid_imag, out_real),
        ]
    ).reshape(2, C, BS)
    bias_first = jnp.sum(grad_pre, axis=(0, 1, 3), dtype=jnp.float32).reshape(2, C)
    bias_second = jnp.sum(grad_out, axis=(0, 1, 3), dtype=jnp.float32).reshape(2, C)
    local_terms = (first_grad, second_grad, bias_first, bias_second)
    summed = lax.psum(
        (local_terms[0], local_terms[1], local_terms[2], local_terms[3]), ("dp", "space")
    )
    share_rows = C // lax.axis_size("dp")
    row_start = lax.axis_index("dp") * share_rows

    def take_share(array):
        return lax.dynamic_slice_in_dim(array, row_start, share_rows, 1)

    totals = jax.tree.map(take_share, summed)
    grad_norm = 1.0 / math.sqrt(samples_dev * lax.axis_size("dp") * lat_len * kept)
    grad_lat = jnp.einsum(
        "mqhp,smqjc->shpjc", lat_table, grad_spec, preferred_element_type=jnp.float32
    ).astype(jnp.bfloat16)
    returned = lax.all_to_all(grad_lat, "space", split_axis=1, concat_axis=3, tiled=True)
    grad_field = (
        jnp.einsum("wpk,shpkc->shwc", lon_table, returned, preferred_element_type=jnp.float32)
        * ortho_scale
    ).astype(jnp.bfloat16)
    return (
        grad_field,
        totals[0] * grad_norm,
        totals[1] * grad_norm,
        totals[2] * grad_norm,
        totals[3] * grad_norm,
    )


def solution(mesh):
    groups, parts = mesh.shape["dp"], mesh.shape["space"]

    def per_device(*arrays):
        activations, lon_keep = arrays[0], arrays[5]
        fits = (
            parts == BLOCKS
            and 2 * groups == BLOCKS
            and activations.shape[:2] == (1, 2)
            and lon_keep.shape[0] == parts
        )
        return by_blocks(*arrays) if fits else by_frequencies(*arrays)

    return jax.shard_map(
        per_device,
        mesh=mesh,
        in_specs=(
            P("dp", "space", None, None),
            P("dp", "space", None, None),
            P(),
            P(),
            P(),
            P(),
            P("dp", None, None, "space", None),
            P("dp", None, None, "space", None),
        ),
        out_specs=(
            P("dp", "space", None, None),
            P(None, "dp", None),
            P(None, "dp", None),
            P(None, "dp"),
            P(None, "dp"),
        ),
        check_vma=False,
    )
```

```python
import functools
import math

import jax
import jax.numpy as jnp
import numpy as np
from jax import lax
from jax.experimental import pallas as pl
from jax.experimental.pallas import tpu as pltpu
from jax.sharding import PartitionSpec as P

C = 768
BLOCKS = 8
LON = 180
BS = 96

BF = jnp.bfloat16
F32 = jnp.float32
LANES = 128
THIRD = LANES - BS
VMEM_LIMIT = 32 * 1024 * 1024
WHOLE_VMEM = 64 * 1024 * 1024 - 320 * 1024


def shift_of(group):
    return 2 * (group % 2) + group // 2


def block_of(group, device):
    lane = 2 * (device // 4) + device % 2
    return 2 * ((lane + shift_of(group)) % 4) + (device // 2) % 2


def owner_of(group, block):
    lane = (block // 2 + 4 - shift_of(group)) % 4
    return 4 * (lane // 2) + 2 * (block % 2) + lane % 2


def latitude_matrix(lat_len, kept):
    index = np.arange(lat_len)
    angle = ((index[:, None] * index[None, :]) % lat_len).astype(np.float32) * np.float32(
        2.0 * math.pi / lat_len
    )
    cosine, sine = np.cos(angle), np.sin(angle)
    table = np.stack([np.stack([cosine, sine], -1), np.stack([-sine, cosine], -1)], 1)
    full = np.einsum("mphq,jk->pjmhqk", table, np.eye(kept, dtype=np.float32))
    return full.reshape(2 * kept * lat_len, 2 * kept * lat_len)


def dot(lhs, rhs, lhs_axis, rhs_axis):
    return lax.dot_general(
        lhs, rhs, (((lhs_axis,), (rhs_axis,)), ((), ())), preferred_element_type=F32
    )


def fold(array):
    rows = array.shape[0] // 4
    beside = [array[3 * rows :, g * THIRD : (g + 1) * THIRD] for g in range(3)]
    return jnp.concatenate([array[: 3 * rows], jnp.concatenate(beside, axis=0)], axis=1)


def unfold(array):
    rows = array.shape[0] // 3
    beside = [array[g * rows : (g + 1) * rows, BS:] for g in range(3)]
    return jnp.concatenate([array[:, :BS], jnp.concatenate(beside, axis=1)], axis=0)


def forward_lon_kernel(
    keep_hbm, act_hbm, cot_hbm, relu_hbm, shrink_hbm, out, table_out, field, masks, keep, sems
):
    kept = keep.shape[0]
    rows = act_hbm.shape[1]
    modes = relu_hbm.shape[0]
    tiles = C // LANES
    columns = [slice(k * LANES, (k + 1) * LANES) for k in range(tiles)]
    keep_copy = pltpu.make_async_copy(keep_hbm, keep, sems.at[0])
    keep_copy.start()
    mask_copies, field_copies = [], []
    for t, source in enumerate((relu_hbm, shrink_hbm)):
        for p in range(2):
            for k in range(tiles):
                copy = pltpu.make_async_copy(
                    source.at[:, p, :, columns[k]],
                    masks.at[t, p, k],
                    sems.at[1 + (2 * t + p) * tiles + k],
                )
                copy.start()
                mask_copies.append(copy)
    for t, source in enumerate((act_hbm, cot_hbm)):
        for k in range(tiles):
            copy = pltpu.make_async_copy(
                source.at[:, :, columns[k]], field.at[t, k], sems.at[1 + (4 + t) * tiles + k]
            )
            copy.start()
            field_copies.append(copy)

    keep_copy.wait()
    shape = (rows * 2 * kept, LON * rows)
    line = lax.broadcasted_iota(jnp.int32, shape, 0)
    column = lax.broadcasted_iota(jnp.int32, shape, 1)
    frequency = jnp.zeros(shape, jnp.int32)
    for j in range(kept):
        frequency = jnp.where(line % kept == j, keep[j], frequency)
    turn = jnp.where((line // kept) % 2 == 1, LON // 4, 0)
    phase = ((column // rows) * frequency + turn) % LON
    table = jnp.cos(phase.astype(F32) * (2.0 * math.pi / LON))
    table = jnp.where(line // (2 * kept) == column % rows, table, 0.0).astype(BF)
    table_out[...] = table

    group = lax.axis_index("dp")
    own = keep[lax.axis_index("space")]
    scale = jnp.where((own == 0) | (2 * own == LON), 1.0, 2.0)
    for copy in mask_copies:
        copy.wait()

    def gate(t, value):
        return jnp.concatenate(
            [
                jnp.concatenate(
                    [
                        jnp.where(masks.at[t, p, k].reshape(modes, LANES)[...] > 0, value, 0.0)
                        for k in range(tiles)
                    ],
                    axis=1,
                )
                for p in range(2)
            ],
            axis=0,
        ).astype(BF)

    passed = gate(0, 1.0)
    scaled = gate(1, scale)
    per = table.shape[0]
    owners = [owner_of(group, b) for b in range(BLOCKS)]
    for b in range(BLOCKS):
        out[owners[b], 2 * per :, 0:BS] = passed[:, b * BS : (b + 1) * BS]
        beside = [scaled[:, b * BS + g * THIRD : b * BS + (g + 1) * THIRD] for g in range(3)]
        out[owners[b], :, BS:] = jnp.concatenate(beside, axis=0)

    for t in range(2):
        for copy in field_copies[t * tiles : (t + 1) * tiles]:
            copy.wait()
        wide = jnp.concatenate(
            [field.at[t, k].reshape(LON * rows, LANES)[...] for k in range(tiles)], axis=1
        )
        lines = dot(table, wide, 1, 0).astype(BF)
        for b in range(BLOCKS):
            out[owners[b], t * per : (t + 1) * per, 0:BS] = lines[:, b * BS : (b + 1) * BS]


def spectral_kernel(
    pieces, first_all, second_all, bias, lat, lat_t, grad_lat, terms, *, ortho_scale, rows, kept
):
    device = lax.axis_index("space")
    block = block_of(lax.axis_index("dp"), device)
    parts = pieces.shape[0]
    per = rows * 2 * kept
    half = parts * per // 2
    modes = half // kept
    place = pl.ds(pl.multiple_of(block * BS, BS), BS)
    first = [first_all[p, place, :] for p in range(2)]
    second = [second_all[p, place, :] for p in range(2)]
    opened = [unfold(pieces[i]) for i in range(parts)]

    def spectrum(t):
        stacked = jnp.concatenate([piece[t * per : (t + 1) * per] for piece in opened], axis=0)
        return (dot(lat[...], stacked, 1, 0) * ortho_scale).astype(BF)

    def mask(k):
        start = 2 * per + k * 2 * modes
        return jnp.concatenate(
            [
                opened[j][start + p * modes : start + (p + 1) * modes]
                for p in range(2)
                for j in range(kept)
            ],
            axis=0,
        ).astype(F32)

    spec_act = spectrum(0)
    spec_cot = spectrum(1)
    passed = mask(0) > 0.0
    weight = mask(1)
    grad_out = jnp.where(weight > 0.0, weight * spec_cot.astype(F32), 0.0).astype(BF)

    bias_real = jnp.zeros((1, BS), F32)
    bias_imag = jnp.zeros((1, BS), F32)
    for b in range(BLOCKS):
        mine = block == b
        bias_real = jnp.where(mine, bias[0:1, b * BS : (b + 1) * BS], bias_real)
        bias_imag = jnp.where(mine, bias[1:2, b * BS : (b + 1) * BS], bias_imag)

    by_real = dot(spec_act, first[0], 1, 0)
    by_imag = dot(spec_act, first[1], 1, 0)
    pre = jnp.concatenate(
        [
            by_real[:half] - by_imag[half:] + bias_real,
            by_imag[:half] + by_real[half:] + bias_imag,
        ],
        axis=0,
    )
    hidden = jnp.where(passed, pre, 0.0).astype(BF)

    def adjoint(operand, matrix):
        real = dot(operand, matrix[0], 1, 1)
        imag = dot(operand, matrix[1], 1, 1)
        return jnp.concatenate([real[:half] + imag[half:], real[half:] - imag[:half]], axis=0)

    grad_pre = jnp.where(passed, adjoint(grad_out, second), 0.0).astype(BF)

    def turned(array):
        return jnp.concatenate([array[half:], -array[:half]], axis=0)

    at = 3 * BS // 4
    blank = jnp.zeros((terms.shape[2] - at - 1, LANES), F32)
    for a, (left, right) in enumerate(((spec_act, grad_pre), (hidden, grad_out))):
        slot = (a + device) % 2
        wide = right.astype(F32)
        for p, other in enumerate((right, turned(right))):
            summed = jnp.sum(wide[p * half : (p + 1) * half], axis=0, keepdims=True)
            summed = jnp.concatenate([summed, jnp.zeros((1, THIRD), F32)], axis=1)
            terms[slot, p] = jnp.concatenate(
                [fold(dot(left, other, 0, 0)), summed, blank], axis=0
            ).astype(BF)

    grad_spec = adjoint(grad_pre, first).astype(BF)
    lines = dot(lat_t[...], grad_spec, 1, 0)
    lines = jnp.concatenate([lines, jnp.zeros((2 * half, THIRD), F32)], axis=1).astype(BF)
    grad_lat[...] = lines.reshape(grad_lat.shape)


def inverse_lon_kernel(table, pieces, field_hbm, lines, field, sems, *, ortho_scale):
    rows = field_hbm.shape[1]
    per = table.shape[0]
    tiles = C // LANES
    group = lax.axis_index("dp")
    copies = []
    for b in range(BLOCKS):
        lines[:, b * BS : (b + 1) * BS] = pieces[owner_of(group, b), 0:per, 0:BS]
    for k in range(0, tiles, 2):
        wide = dot(table[...], lines[:, k * LANES : (k + 2) * LANES], 0, 0) * ortho_scale
        for i in range(2):
            field.at[k + i].reshape(LON * rows, LANES)[...] = wide[
                :, i * LANES : (i + 1) * LANES
            ].astype(BF)
            copy = pltpu.make_async_copy(
                field.at[k + i],
                field_hbm.at[:, :, (k + i) * LANES : (k + i + 1) * LANES],
                sems.at[k + i],
            )
            copy.start()
            copies.append(copy)
    for copy in copies:
        copy.wait()


def gathered_kernel(pieces, others, first, second, bias_first, bias_second, *, grad_norm):
    core = lax.axis_index("space") % 2
    per = pieces.shape[1] - others.shape[1]
    at = 3 * BS // 4
    for a, (target, vector) in enumerate(((first, bias_first), (second, bias_second))):
        for k in range(2):
            near, far = 2 * k + a, 4 + 2 * k + a
            own = pieces[near, per:, :].astype(F32) + pieces[far, per:, :].astype(F32)
            other = others[near].astype(F32) + others[far].astype(F32)
            for p in range(2):
                total = jnp.where(core == p, own, other) * grad_norm
                target[p, k * BS : (k + 1) * BS, :] = unfold(total[:at])
                vector[p : p + 1, k * BS : (k + 1) * BS] = total[at : at + 1, :BS]


def whole(memory=pltpu.VMEM):
    return pl.BlockSpec(memory_space=memory)


def by_blocks(
    activations, cotangent, w_first, w_second, b_first, lon_keep, relu_mask, shrink_mask
):
    groups = lax.axis_size("dp")
    parts = lax.axis_size("space")
    rows = activations.shape[1]
    lat_len = rows * parts
    kept = lon_keep.shape[0]
    ortho_scale = 1.0 / math.sqrt(lat_len * LON)
    grad_norm = 1.0 / math.sqrt(groups * lat_len * kept)
    params = pltpu.CompilerParams(vmem_limit_bytes=VMEM_LIMIT)
    tiles = C // LANES
    per = rows * 2 * kept
    height = (2 * per + 4 * lat_len) * 3 // 4
    term_rows = 3 * BS // 4 + 8

    sent, table = pl.pallas_call(
        forward_lon_kernel,
        out_shape=(
            jax.ShapeDtypeStruct((parts, height, LANES), BF),
            jax.ShapeDtypeStruct((per, LON * rows), BF),
        ),
        in_specs=[whole(pl.ANY)] * 5,
        out_specs=(whole(), whole()),
        scratch_shapes=[
            pltpu.VMEM((2, tiles, LON, rows, LANES), BF),
            pltpu.VMEM((2, 2, tiles, lat_len, 1, LANES), jnp.int32),
            pltpu.SMEM((kept,), jnp.int32),
            pltpu.SemaphoreType.DMA((1 + 6 * tiles,)),
        ],
        compiler_params=pltpu.CompilerParams(vmem_limit_bytes=WHOLE_VMEM),
        name="forward_lon",
    )(
        lon_keep,
        activations[0].transpose(1, 0, 2),
        cotangent[0].transpose(1, 0, 2),
        relu_mask[0],
        shrink_mask[0],
    )
    pieces = lax.all_to_all(sent, "space", 0, 0, tiled=True)

    lat = latitude_matrix(lat_len, kept)
    grad_lat, terms = pl.pallas_call(
        functools.partial(spectral_kernel, ortho_scale=ortho_scale, rows=rows, kept=kept),
        out_shape=(
            jax.ShapeDtypeStruct((parts, per, LANES), BF),
            jax.ShapeDtypeStruct((2, 2, term_rows, LANES), BF),
        ),
        in_specs=[whole()] * 6,
        out_specs=(whole(), whole()),
        compiler_params=params,
        name="spectral",
    )(pieces, w_first, w_second, b_first, jnp.asarray(lat, BF), jnp.asarray(lat.T, BF))

    arrived = lax.ppermute(
        terms,
        ("dp", "space"),
        [
            (g * parts + c, (block_of(g, c) // 2) * parts + c)
            for g in range(groups)
            for c in range(parts)
        ],
    )
    other = lax.ppermute(arrived[1], "space", [(c, c ^ 1) for c in range(parts)])
    share = (arrived[0].astype(F32) + other.astype(F32)).astype(BF)
    share = jnp.broadcast_to(share[None], (parts // 2,) + share.shape)
    returned = lax.all_to_all(
        jnp.concatenate([grad_lat, share.reshape(parts, term_rows, LANES)], axis=1),
        "space",
        0,
        0,
        tiled=True,
    )
    others = lax.ppermute(returned[:, per:, :], "space", [(c, c ^ 1) for c in range(parts)])

    keep_rows = C // groups
    field = pl.pallas_call(
        functools.partial(inverse_lon_kernel, ortho_scale=ortho_scale),
        out_shape=jax.ShapeDtypeStruct((LON, rows, C), BF),
        in_specs=[whole(), whole()],
        out_specs=whole(pl.ANY),
        scratch_shapes=[
            pltpu.VMEM((per, C), BF),
            pltpu.VMEM((tiles, LON, rows, LANES), BF),
            pltpu.SemaphoreType.DMA((tiles,)),
        ],
        compiler_params=params,
        cost_estimate=pl.CostEstimate(
            flops=2 * per * LON * rows * C, bytes_accessed=8 * LON * rows * C, transcendentals=0
        ),
        name="inverse_lon",
    )(table, returned)
    first, second, bias_first, bias_second = pl.pallas_call(
        functools.partial(gathered_kernel, grad_norm=grad_norm),
        out_shape=(
            jax.ShapeDtypeStruct((2, keep_rows, BS), F32),
            jax.ShapeDtypeStruct((2, keep_rows, BS), F32),
            jax.ShapeDtypeStruct((2, keep_rows), F32),
            jax.ShapeDtypeStruct((2, keep_rows), F32),
        ),
        in_specs=[whole(), whole()],
        out_specs=(whole(),) * 4,
        compiler_params=params,
        name="gathered",
    )(returned, others)
    return field.transpose(1, 0, 2)[None], first, second, bias_first, bias_second


def build_tables(lon_keep, lat_len, lon_len):
    columns = jnp.arange(lon_len, dtype=jnp.int32)
    lon_phase = columns[:, None] * lon_keep[None, :] % lon_len
    lon_angle = lon_phase.astype(jnp.float32) * (2.0 * math.pi / lon_len)
    lon_table = jnp.stack([jnp.cos(lon_angle), -jnp.sin(lon_angle)], axis=1).astype(jnp.bfloat16)
    latitudes = jnp.arange(lat_len, dtype=jnp.int32)
    lat_phase = latitudes[:, None] * latitudes[None, :] % lat_len
    lat_angle = lat_phase.astype(jnp.float32) * (2.0 * math.pi / lat_len)
    cosine = jnp.cos(lat_angle)
    sine_part = jnp.sin(lat_angle)
    lat_table = jnp.stack(
        [jnp.stack([cosine, sine_part], axis=-1), jnp.stack([-sine_part, cosine], axis=-1)], axis=1
    ).astype(jnp.bfloat16)
    return (lon_table, lat_table)


def apply_blocks(operand, matrix):
    return jnp.einsum("smjbc,bcd->smjbd", operand, matrix, preferred_element_type=jnp.float32)


def adjoint(operand, matrix):
    return jnp.einsum("smjbd,bcd->smjbc", operand, matrix, preferred_element_type=jnp.float32)


def outer_sum(operand, other):
    return jnp.einsum("smjbc,smjbd->bcd", operand, other, preferred_element_type=jnp.float32)


def by_frequencies(
    activations, cotangent, w_first, w_second, b_first, lon_keep, relu_mask, shrink_mask
):
    parts = lax.axis_size("space")
    samples_dev = activations.shape[0]
    lat_len = activations.shape[1] * parts
    kept = lon_keep.shape[0]
    owned = kept // parts
    lon_table, lat_table = build_tables(lon_keep, lat_len, LON)
    ortho_scale = 1.0 / math.sqrt(lat_len * LON)
    act_lon = jnp.einsum(
        "shwc,wpk->shpkc", activations, lon_table, preferred_element_type=jnp.float32
    ).astype(jnp.bfloat16)
    cot_lon = jnp.einsum(
        "shwc,wpk->shpkc", cotangent, lon_table, preferred_element_type=jnp.float32
    ).astype(jnp.bfloat16)
    act_modes, cot_modes = (
        lax.all_to_all(act_lon, "space", split_axis=3, concat_axis=1, tiled=True),
        lax.all_to_all(cot_lon, "space", split_axis=3, concat_axis=1, tiled=True),
    )

    def latitude(modes):
        summed = jnp.einsum(
            "mphq,shqjc->smpjc", lat_table, modes, preferred_element_type=jnp.float32
        )
        return (summed * ortho_scale).astype(jnp.bfloat16)

    block_shape = (samples_dev, lat_len, 2, owned, BLOCKS, BS)
    spec_act = latitude(act_modes).reshape(block_shape)
    spec_cot = latitude(cot_modes)
    own_keep = lax.dynamic_slice_in_dim(lon_keep, lax.axis_index("space") * owned, owned)
    doubled = jnp.where((own_keep == 0) | (2 * own_keep == LON), 1.0, 2.0).astype(jnp.float32)
    grad_out = (
        jnp.where(
            shrink_mask > 0, doubled[None, None, None, :, None] * spec_cot.astype(jnp.float32), 0.0
        )
        .astype(jnp.bfloat16)
        .reshape(block_shape)
    )
    relu_gate = relu_mask.reshape(block_shape) > 0
    first_blocks = w_first.reshape(2, BLOCKS, BS, BS)
    second_blocks = w_second.reshape(2, BLOCKS, BS, BS)
    bias_blocks = b_first.reshape(2, BLOCKS, BS)
    act_real = spec_act[:, :, 0]
    act_imag = spec_act[:, :, 1]
    pre_real = (
        apply_blocks(act_real, first_blocks[0])
        - apply_blocks(act_imag, first_blocks[1])
        + bias_blocks[0]
    )
    pre_imag = (
        apply_blocks(act_real, first_blocks[1])
        + apply_blocks(act_imag, first_blocks[0])
        + bias_blocks[1]
    )
    hidden = jnp.where(relu_gate, jnp.stack([pre_real, pre_imag], axis=2), 0.0).astype(jnp.bfloat16)
    out_real = grad_out[:, :, 0]
    out_imag = grad_out[:, :, 1]
    hidden_real = adjoint(out_real, second_blocks[0]) + adjoint(out_imag, second_blocks[1])
    hidden_imag = -adjoint(out_real, second_blocks[1]) + adjoint(out_imag, second_blocks[0])
    grad_pre = jnp.where(relu_gate, jnp.stack([hidden_real, hidden_imag], axis=2), 0.0).astype(
        jnp.bfloat16
    )
    pre_grad_real = grad_pre[:, :, 0]
    pre_grad_imag = grad_pre[:, :, 1]
    spec_real = adjoint(pre_grad_real, first_blocks[0]) + adjoint(pre_grad_imag, first_blocks[1])
    spec_imag = -adjoint(pre_grad_real, first_blocks[1]) + adjoint(pre_grad_imag, first_blocks[0])
    grad_spec = (
        jnp.stack([spec_real, spec_imag], axis=2)
        .astype(jnp.bfloat16)
        .reshape(samples_dev, lat_len, 2, owned, C)
    )
    first_grad = jnp.stack(
        [
            outer_sum(act_real, pre_grad_real) + outer_sum(act_imag, pre_grad_imag),
            outer_sum(act_real, pre_grad_imag) - outer_sum(act_imag, pre_grad_real),
        ]
    ).reshape(2, C, BS)
    hid_real = hidden[:, :, 0]
    hid_imag = hidden[:, :, 1]
    second_grad = jnp.stack(
        [
            outer_sum(hid_real, out_real) + outer_sum(hid_imag, out_imag),
            outer_sum(hid_real, out_imag) - outer_sum(hid_imag, out_real),
        ]
    ).reshape(2, C, BS)
    bias_first = jnp.sum(grad_pre, axis=(0, 1, 3), dtype=jnp.float32).reshape(2, C)
    bias_second = jnp.sum(grad_out, axis=(0, 1, 3), dtype=jnp.float32).reshape(2, C)
    local_terms = (first_grad, second_grad, bias_first, bias_second)
    summed = lax.psum(
        (local_terms[0], local_terms[1], local_terms[2], local_terms[3]), ("dp", "space")
    )
    share_rows = C // lax.axis_size("dp")
    row_start = lax.axis_index("dp") * share_rows

    def take_share(array):
        return lax.dynamic_slice_in_dim(array, row_start, share_rows, 1)

    totals = jax.tree.map(take_share, summed)
    grad_norm = 1.0 / math.sqrt(samples_dev * lax.axis_size("dp") * lat_len * kept)
    grad_lat = jnp.einsum(
        "mqhp,smqjc->shpjc", lat_table, grad_spec, preferred_element_type=jnp.float32
    ).astype(jnp.bfloat16)
    returned = lax.all_to_all(grad_lat, "space", split_axis=1, concat_axis=3, tiled=True)
    grad_field = (
        jnp.einsum("wpk,shpkc->shwc", lon_table, returned, preferred_element_type=jnp.float32)
        * ortho_scale
    ).astype(jnp.bfloat16)
    return (
        grad_field,
        totals[0] * grad_norm,
        totals[1] * grad_norm,
        totals[2] * grad_norm,
        totals[3] * grad_norm,
    )


def solution(mesh):
    groups, parts = mesh.shape["dp"], mesh.shape["space"]

    def per_device(*arrays):
        activations, lon_keep = arrays[0], arrays[5]
        fits = (
            parts == BLOCKS
            and 2 * groups == BLOCKS
            and activations.shape[:2] == (1, 2)
            and lon_keep.shape[0] == parts
        )
        return by_blocks(*arrays) if fits else by_frequencies(*arrays)

    return jax.shard_map(
        per_device,
        mesh=mesh,
        in_specs=(
            P("dp", "space", None, None),
            P("dp", "space", None, None),
            P(),
            P(),
            P(),
            P(),
            P("dp", None, None, "space", None),
            P("dp", None, None, "space", None),
        ),
        out_specs=(
            P("dp", "space", None, None),
            P(None, "dp", None),
            P(None, "dp", None),
            P(None, "dp"),
            P(None, "dp"),
        ),
        check_vma=False,
    )
```

```python
import functools
import math

import jax
import jax.numpy as jnp
import numpy as np
from jax import lax
from jax.experimental import pallas as pl
from jax.experimental.pallas import tpu as pltpu
from jax.sharding import PartitionSpec as P

C = 768
BLOCKS = 8
LON = 180
BS = 96

BF = jnp.bfloat16
F32 = jnp.float32
LANES = 128
THIRD = LANES - BS
VMEM_LIMIT = 32 * 1024 * 1024


def shift_of(group):
    return 2 * (group % 2) + group // 2


def block_of(group, device):
    lane = 2 * (device // 4) + device % 2
    return 2 * ((lane + shift_of(group)) % 4) + (device // 2) % 2


def owner_of(group, block):
    lane = (block // 2 + 4 - shift_of(group)) % 4
    return 4 * (lane // 2) + 2 * (block % 2) + lane % 2


def latitude_matrix(lat_len, kept):
    index = np.arange(lat_len)
    angle = ((index[:, None] * index[None, :]) % lat_len).astype(np.float32) * np.float32(
        2.0 * math.pi / lat_len
    )
    cosine, sine = np.cos(angle), np.sin(angle)
    table = np.stack([np.stack([cosine, sine], -1), np.stack([-sine, cosine], -1)], 1)
    full = np.einsum("mphq,jk->pjmhqk", table, np.eye(kept, dtype=np.float32))
    return full.reshape(2 * kept * lat_len, 2 * kept * lat_len)


def dot(lhs, rhs, lhs_axis, rhs_axis):
    return lax.dot_general(
        lhs, rhs, (((lhs_axis,), (rhs_axis,)), ((), ())), preferred_element_type=F32
    )


def fold(array):
    rows = array.shape[0] // 4
    beside = [array[3 * rows :, g * THIRD : (g + 1) * THIRD] for g in range(3)]
    return jnp.concatenate([array[: 3 * rows], jnp.concatenate(beside, axis=0)], axis=1)


def unfold(array):
    rows = array.shape[0] // 3
    beside = [array[g * rows : (g + 1) * rows, BS:] for g in range(3)]
    return jnp.concatenate([array[:, :BS], jnp.concatenate(beside, axis=1)], axis=0)


def window_of(block):
    tile = jnp.minimum(block * BS // LANES, C // LANES - 2)
    return pl.multiple_of(tile * LANES, LANES), block * BS - tile * LANES


def forward_lon_kernel(
    keep_hbm,
    act_hbm,
    cot_hbm,
    relu_hbm,
    shrink_hbm,
    *refs,
):
    weights_hbm, matrices_hbm, refs = refs[:3], refs[3:5], refs[5:]
    out, table_out, *fetched, field, masks, keep, sems = refs
    group, device = lax.axis_index("dp"), lax.axis_index("space")
    start, _ = window_of(block_of(group, device))
    kept = keep.shape[0]
    rows = act_hbm.shape[1]
    modes = relu_hbm.shape[0]
    tiles = C // LANES
    columns = [slice(k * LANES, (k + 1) * LANES) for k in range(tiles)]
    keep_copy = pltpu.make_async_copy(keep_hbm, keep, sems.at[0])
    keep_copy.start()
    mask_copies, field_copies = [], []
    for t, source in enumerate((relu_hbm, shrink_hbm)):
        for p in range(2):
            for k in range(tiles):
                copy = pltpu.make_async_copy(
                    source.at[:, p, :, columns[k]],
                    masks.at[t, p, k],
                    sems.at[1 + (2 * t + p) * tiles + k],
                )
                copy.start()
                mask_copies.append(copy)
    for t, source in enumerate((act_hbm, cot_hbm)):
        for k in range(tiles):
            copy = pltpu.make_async_copy(
                source.at[:, :, columns[k]], field.at[t, k], sems.at[1 + (4 + t) * tiles + k]
            )
            copy.start()
            field_copies.append(copy)
    sources = [
        source.at[(slice(None),) * (len(source.shape) - 1) + (pl.ds(start, 2 * LANES),)]
        for source in weights_hbm
    ] + list(matrices_hbm)
    other_copies = []
    for i, (source, target) in enumerate(zip(sources, fetched)):
        copy = pltpu.make_async_copy(source, target, sems.at[1 + 6 * tiles + i])
        copy.start()
        other_copies.append(copy)

    keep_copy.wait()
    shape = (rows * 2 * kept, LON * rows)
    line = lax.broadcasted_iota(jnp.int32, shape, 0)
    column = lax.broadcasted_iota(jnp.int32, shape, 1)
    frequency = jnp.zeros(shape, jnp.int32)
    for j in range(kept):
        frequency = jnp.where(line % kept == j, keep[j], frequency)
    turn = jnp.where((line // kept) % 2 == 1, LON // 4, 0)
    phase = ((column // rows) * frequency + turn) % LON
    table = jnp.cos(phase.astype(F32) * (2.0 * math.pi / LON))
    table = jnp.where(line // (2 * kept) == column % rows, table, 0.0).astype(BF)
    table_out[...] = table

    own = keep[device]
    scale = jnp.where((own == 0) | (2 * own == LON), 1.0, 2.0)
    for copy in mask_copies:
        copy.wait()

    def gate(t, value):
        return jnp.concatenate(
            [
                jnp.concatenate(
                    [
                        jnp.where(masks.at[t, p, k].reshape(modes, LANES)[...] > 0, value, 0.0)
                        for k in range(tiles)
                    ],
                    axis=1,
                )
                for p in range(2)
            ],
            axis=0,
        ).astype(BF)

    passed = gate(0, 1.0)
    scaled = gate(1, scale)
    per = table.shape[0]
    owners = [owner_of(group, b) for b in range(BLOCKS)]
    for b in range(BLOCKS):
        out[owners[b], 2 * per :, 0:BS] = passed[:, b * BS : (b + 1) * BS]
        beside = [scaled[:, b * BS + g * THIRD : b * BS + (g + 1) * THIRD] for g in range(3)]
        out[owners[b], :, BS:] = jnp.concatenate(beside, axis=0)

    for t in range(2):
        for copy in field_copies[t * tiles : (t + 1) * tiles]:
            copy.wait()
        wide = jnp.concatenate(
            [field.at[t, k].reshape(LON * rows, LANES)[...] for k in range(tiles)], axis=1
        )
        lines = dot(table, wide, 1, 0).astype(BF)
        for b in range(BLOCKS):
            out[owners[b], t * per : (t + 1) * per, 0:BS] = lines[:, b * BS : (b + 1) * BS]
    for copy in other_copies:
        copy.wait()


def spectral_kernel(
    pieces, first_wide, second_wide, bias_wide, lat, lat_t, grad_lat, terms, *, ortho_scale, rows, kept
):
    device = lax.axis_index("space")
    _, offset = window_of(block_of(lax.axis_index("dp"), device))
    parts = pieces.shape[0]
    per = rows * 2 * kept
    half = parts * per // 2
    modes = half // kept
    chosen = lax.broadcasted_iota(jnp.int32, (2 * LANES, BS), 0) == (
        lax.broadcasted_iota(jnp.int32, (2 * LANES, BS), 1) + offset
    )
    chosen = jnp.where(chosen, 1.0, 0.0).astype(BF)
    first = [dot(first_wide[p], chosen, 1, 0).astype(BF) for p in range(2)]
    second = [dot(second_wide[p], chosen, 1, 0).astype(BF) for p in range(2)]
    bias = pltpu.roll(bias_wide[...], (2 * LANES - offset) % (2 * LANES), 1)
    opened = [unfold(pieces[i]) for i in range(parts)]

    def spectrum(t):
        stacked = jnp.concatenate([piece[t * per : (t + 1) * per] for piece in opened], axis=0)
        return (dot(lat[...], stacked, 1, 0) * ortho_scale).astype(BF)

    def mask(k):
        start = 2 * per + k * 2 * modes
        return jnp.concatenate(
            [
                opened[j][start + p * modes : start + (p + 1) * modes]
                for p in range(2)
                for j in range(kept)
            ],
            axis=0,
        ).astype(F32)

    spec_act = spectrum(0)
    spec_cot = spectrum(1)
    passed = mask(0) > 0.0
    weight = mask(1)
    grad_out = jnp.where(weight > 0.0, weight * spec_cot.astype(F32), 0.0).astype(BF)

    by_real = dot(spec_act, first[0], 1, 1)
    by_imag = dot(spec_act, first[1], 1, 1)
    pre = jnp.concatenate(
        [
            by_real[:half] - by_imag[half:] + bias[0:1, :BS],
            by_imag[:half] + by_real[half:] + bias[1:2, :BS],
        ],
        axis=0,
    )
    hidden = jnp.where(passed, pre, 0.0).astype(BF)

    def adjoint(operand, matrix):
        real = dot(operand, matrix[0], 1, 0)
        imag = dot(operand, matrix[1], 1, 0)
        return jnp.concatenate([real[:half] + imag[half:], real[half:] - imag[:half]], axis=0)

    grad_pre = jnp.where(passed, adjoint(grad_out, second), 0.0).astype(BF)

    def turned(array):
        return jnp.concatenate([array[half:], -array[:half]], axis=0)

    at = 3 * BS // 4
    blank = jnp.zeros((terms.shape[2] - at - 1, LANES), F32)
    for a, (left, right) in enumerate(((spec_act, grad_pre), (hidden, grad_out))):
        slot = (a + device) % 2
        wide = right.astype(F32)
        for p, other in enumerate((right, turned(right))):
            summed = jnp.sum(wide[p * half : (p + 1) * half], axis=0, keepdims=True)
            summed = jnp.concatenate([summed, jnp.zeros((1, THIRD), F32)], axis=1)
            terms[slot, p] = jnp.concatenate(
                [fold(dot(left, other, 0, 0)), summed, blank], axis=0
            ).astype(BF)

    grad_spec = adjoint(grad_pre, first).astype(BF)
    lines = dot(lat_t[...], grad_spec, 1, 0)
    lines = jnp.concatenate([lines, jnp.zeros((2 * half, THIRD), F32)], axis=1).astype(BF)
    grad_lat[...] = lines.reshape(grad_lat.shape)


def inverse_lon_kernel(table, pieces, field_hbm, lines, field, sems, *, ortho_scale):
    rows = field_hbm.shape[1]
    per = table.shape[0]
    tiles = C // LANES
    group = lax.axis_index("dp")
    copies = []
    for b in range(BLOCKS):
        lines[:, b * BS : (b + 1) * BS] = pieces[owner_of(group, b), 0:per, 0:BS]
    for k in range(0, tiles, 2):
        wide = dot(table[...], lines[:, k * LANES : (k + 2) * LANES], 0, 0) * ortho_scale
        for i in range(2):
            field.at[k + i].reshape(LON * rows, LANES)[...] = wide[
                :, i * LANES : (i + 1) * LANES
            ].astype(BF)
            copy = pltpu.make_async_copy(
                field.at[k + i],
                field_hbm.at[:, :, (k + i) * LANES : (k + i + 1) * LANES],
                sems.at[k + i],
            )
            copy.start()
            copies.append(copy)
    for copy in copies:
        copy.wait()


def gathered_kernel(pieces, others, first, second, bias_first, bias_second, *, grad_norm):
    core = lax.axis_index("space") % 2
    per = pieces.shape[1] - others.shape[1]
    at = 3 * BS // 4
    for a, (target, vector) in enumerate(((first, bias_first), (second, bias_second))):
        for k in range(2):
            near, far = 2 * k + a, 4 + 2 * k + a
            own = pieces[near, per:, :].astype(F32) + pieces[far, per:, :].astype(F32)
            other = others[near].astype(F32) + others[far].astype(F32)
            for p in range(2):
                total = jnp.where(core == p, own, other) * grad_norm
                target[p, k * BS : (k + 1) * BS, :] = unfold(total[:at])
                vector[p : p + 1, k * BS : (k + 1) * BS] = total[at : at + 1, :BS]


def whole(memory=pltpu.VMEM):
    return pl.BlockSpec(memory_space=memory)


def by_blocks(
    activations, cotangent, w_first, w_second, b_first, lon_keep, relu_mask, shrink_mask
):
    groups = lax.axis_size("dp")
    parts = lax.axis_size("space")
    rows = activations.shape[1]
    lat_len = rows * parts
    kept = lon_keep.shape[0]
    ortho_scale = 1.0 / math.sqrt(lat_len * LON)
    grad_norm = 1.0 / math.sqrt(groups * lat_len * kept)
    params = pltpu.CompilerParams(vmem_limit_bytes=VMEM_LIMIT)
    tiles = C // LANES
    per = rows * 2 * kept
    height = (2 * per + 4 * lat_len) * 3 // 4
    term_rows = 3 * BS // 4 + 8

    lat = latitude_matrix(lat_len, kept)
    sent, table, *fetched = pl.pallas_call(
        forward_lon_kernel,
        out_shape=(
            pltpu.VMEM((parts, height, LANES), BF),
            pltpu.VMEM((per, LON * rows), BF),
            pltpu.VMEM((2, BS, 2 * LANES), BF),
            pltpu.VMEM((2, BS, 2 * LANES), BF),
            pltpu.VMEM((2, 2 * LANES), F32),
            pltpu.VMEM(lat.shape, BF),
            pltpu.VMEM(lat.shape, BF),
        ),
        in_specs=[whole(pl.ANY)] * 10,
        out_specs=(whole(),) * 7,
        scratch_shapes=[
            pltpu.VMEM((2, tiles, LON, rows, LANES), BF),
            pltpu.VMEM((2, 2, tiles, lat_len, 1, LANES), jnp.int32),
            pltpu.SMEM((kept,), jnp.int32),
            pltpu.SemaphoreType.DMA((6 + 6 * tiles,)),
        ],
        compiler_params=params,
        name="forward_lon",
    )(
        *(
            pltpu.with_memory_space_constraint(array, pltpu.HBM)
            for array in (
                lon_keep,
                activations[0].transpose(1, 0, 2),
                cotangent[0].transpose(1, 0, 2),
                relu_mask[0],
                shrink_mask[0],
                w_first.transpose(0, 2, 1),
                w_second.transpose(0, 2, 1),
                b_first,
                jnp.asarray(lat, BF),
                jnp.asarray(lat.T, BF),
            )
        )
    )
    pieces = lax.all_to_all(sent, "space", 0, 0, tiled=True)

    grad_lat, terms = pl.pallas_call(
        functools.partial(spectral_kernel, ortho_scale=ortho_scale, rows=rows, kept=kept),
        out_shape=(
            jax.ShapeDtypeStruct((parts, per, LANES), BF),
            jax.ShapeDtypeStruct((2, 2, term_rows, LANES), BF),
        ),
        in_specs=[whole()] * 6,
        out_specs=(whole(), whole()),
        compiler_params=params,
        name="spectral",
    )(pieces, *fetched)

    arrived = lax.ppermute(
        terms,
        ("dp", "space"),
        [
            (g * parts + c, (block_of(g, c) // 2) * parts + c)
            for g in range(groups)
            for c in range(parts)
        ],
    )
    other = lax.ppermute(arrived[1], "space", [(c, c ^ 1) for c in range(parts)])
    share = (arrived[0].astype(F32) + other.astype(F32)).astype(BF)
    share = jnp.broadcast_to(share[None], (parts // 2,) + share.shape)
    returned = lax.all_to_all(
        jnp.concatenate([grad_lat, share.reshape(parts, term_rows, LANES)], axis=1),
        "space",
        0,
        0,
        tiled=True,
    )
    others = lax.ppermute(returned[:, per:, :], "space", [(c, c ^ 1) for c in range(parts)])

    keep_rows = C // groups
    field = pl.pallas_call(
        functools.partial(inverse_lon_kernel, ortho_scale=ortho_scale),
        out_shape=jax.ShapeDtypeStruct((LON, rows, C), BF),
        in_specs=[whole(), whole()],
        out_specs=whole(pl.ANY),
        scratch_shapes=[
            pltpu.VMEM((per, C), BF),
            pltpu.VMEM((tiles, LON, rows, LANES), BF),
            pltpu.SemaphoreType.DMA((tiles,)),
        ],
        compiler_params=params,
        cost_estimate=pl.CostEstimate(
            flops=2 * per * LON * rows * C, bytes_accessed=8 * LON * rows * C, transcendentals=0
        ),
        name="inverse_lon",
    )(table, returned)
    first, second, bias_first, bias_second = pl.pallas_call(
        functools.partial(gathered_kernel, grad_norm=grad_norm),
        out_shape=(
            jax.ShapeDtypeStruct((2, keep_rows, BS), F32),
            jax.ShapeDtypeStruct((2, keep_rows, BS), F32),
            jax.ShapeDtypeStruct((2, keep_rows), F32),
            jax.ShapeDtypeStruct((2, keep_rows), F32),
        ),
        in_specs=[whole(), whole()],
        out_specs=(whole(),) * 4,
        compiler_params=params,
        name="gathered",
    )(returned, others)
    return field.transpose(1, 0, 2)[None], first, second, bias_first, bias_second


def build_tables(lon_keep, lat_len, lon_len):
    columns = jnp.arange(lon_len, dtype=jnp.int32)
    lon_phase = columns[:, None] * lon_keep[None, :] % lon_len
    lon_angle = lon_phase.astype(jnp.float32) * (2.0 * math.pi / lon_len)
    lon_table = jnp.stack([jnp.cos(lon_angle), -jnp.sin(lon_angle)], axis=1).astype(jnp.bfloat16)
    latitudes = jnp.arange(lat_len, dtype=jnp.int32)
    lat_phase = latitudes[:, None] * latitudes[None, :] % lat_len
    lat_angle = lat_phase.astype(jnp.float32) * (2.0 * math.pi / lat_len)
    cosine = jnp.cos(lat_angle)
    sine_part = jnp.sin(lat_angle)
    lat_table = jnp.stack(
        [jnp.stack([cosine, sine_part], axis=-1), jnp.stack([-sine_part, cosine], axis=-1)], axis=1
    ).astype(jnp.bfloat16)
    return (lon_table, lat_table)


def apply_blocks(operand, matrix):
    return jnp.einsum("smjbc,bcd->smjbd", operand, matrix, preferred_element_type=jnp.float32)


def adjoint(operand, matrix):
    return jnp.einsum("smjbd,bcd->smjbc", operand, matrix, preferred_element_type=jnp.float32)


def outer_sum(operand, other):
    return jnp.einsum("smjbc,smjbd->bcd", operand, other, preferred_element_type=jnp.float32)


def by_frequencies(
    activations, cotangent, w_first, w_second, b_first, lon_keep, relu_mask, shrink_mask
):
    parts = lax.axis_size("space")
    samples_dev = activations.shape[0]
    lat_len = activations.shape[1] * parts
    kept = lon_keep.shape[0]
    owned = kept // parts
    lon_table, lat_table = build_tables(lon_keep, lat_len, LON)
    ortho_scale = 1.0 / math.sqrt(lat_len * LON)
    act_lon = jnp.einsum(
        "shwc,wpk->shpkc", activations, lon_table, preferred_element_type=jnp.float32
    ).astype(jnp.bfloat16)
    cot_lon = jnp.einsum(
        "shwc,wpk->shpkc", cotangent, lon_table, preferred_element_type=jnp.float32
    ).astype(jnp.bfloat16)
    act_modes, cot_modes = (
        lax.all_to_all(act_lon, "space", split_axis=3, concat_axis=1, tiled=True),
        lax.all_to_all(cot_lon, "space", split_axis=3, concat_axis=1, tiled=True),
    )

    def latitude(modes):
        summed = jnp.einsum(
            "mphq,shqjc->smpjc", lat_table, modes, preferred_element_type=jnp.float32
        )
        return (summed * ortho_scale).astype(jnp.bfloat16)

    block_shape = (samples_dev, lat_len, 2, owned, BLOCKS, BS)
    spec_act = latitude(act_modes).reshape(block_shape)
    spec_cot = latitude(cot_modes)
    own_keep = lax.dynamic_slice_in_dim(lon_keep, lax.axis_index("space") * owned, owned)
    doubled = jnp.where((own_keep == 0) | (2 * own_keep == LON), 1.0, 2.0).astype(jnp.float32)
    grad_out = (
        jnp.where(
            shrink_mask > 0, doubled[None, None, None, :, None] * spec_cot.astype(jnp.float32), 0.0
        )
        .astype(jnp.bfloat16)
        .reshape(block_shape)
    )
    relu_gate = relu_mask.reshape(block_shape) > 0
    first_blocks = w_first.reshape(2, BLOCKS, BS, BS)
    second_blocks = w_second.reshape(2, BLOCKS, BS, BS)
    bias_blocks = b_first.reshape(2, BLOCKS, BS)
    act_real = spec_act[:, :, 0]
    act_imag = spec_act[:, :, 1]
    pre_real = (
        apply_blocks(act_real, first_blocks[0])
        - apply_blocks(act_imag, first_blocks[1])
        + bias_blocks[0]
    )
    pre_imag = (
        apply_blocks(act_real, first_blocks[1])
        + apply_blocks(act_imag, first_blocks[0])
        + bias_blocks[1]
    )
    hidden = jnp.where(relu_gate, jnp.stack([pre_real, pre_imag], axis=2), 0.0).astype(jnp.bfloat16)
    out_real = grad_out[:, :, 0]
    out_imag = grad_out[:, :, 1]
    hidden_real = adjoint(out_real, second_blocks[0]) + adjoint(out_imag, second_blocks[1])
    hidden_imag = -adjoint(out_real, second_blocks[1]) + adjoint(out_imag, second_blocks[0])
    grad_pre = jnp.where(relu_gate, jnp.stack([hidden_real, hidden_imag], axis=2), 0.0).astype(
        jnp.bfloat16
    )
    pre_grad_real = grad_pre[:, :, 0]
    pre_grad_imag = grad_pre[:, :, 1]
    spec_real = adjoint(pre_grad_real, first_blocks[0]) + adjoint(pre_grad_imag, first_blocks[1])
    spec_imag = -adjoint(pre_grad_real, first_blocks[1]) + adjoint(pre_grad_imag, first_blocks[0])
    grad_spec = (
        jnp.stack([spec_real, spec_imag], axis=2)
        .astype(jnp.bfloat16)
        .reshape(samples_dev, lat_len, 2, owned, C)
    )
    first_grad = jnp.stack(
        [
            outer_sum(act_real, pre_grad_real) + outer_sum(act_imag, pre_grad_imag),
            outer_sum(act_real, pre_grad_imag) - outer_sum(act_imag, pre_grad_real),
        ]
    ).reshape(2, C, BS)
    hid_real = hidden[:, :, 0]
    hid_imag = hidden[:, :, 1]
    second_grad = jnp.stack(
        [
            outer_sum(hid_real, out_real) + outer_sum(hid_imag, out_imag),
            outer_sum(hid_real, out_imag) - outer_sum(hid_imag, out_real),
        ]
    ).reshape(2, C, BS)
    bias_first = jnp.sum(grad_pre, axis=(0, 1, 3), dtype=jnp.float32).reshape(2, C)
    bias_second = jnp.sum(grad_out, axis=(0, 1, 3), dtype=jnp.float32).reshape(2, C)
    local_terms = (first_grad, second_grad, bias_first, bias_second)
    summed = lax.psum(
        (local_terms[0], local_terms[1], local_terms[2], local_terms[3]), ("dp", "space")
    )
    share_rows = C // lax.axis_size("dp")
    row_start = lax.axis_index("dp") * share_rows

    def take_share(array):
        return lax.dynamic_slice_in_dim(array, row_start, share_rows, 1)

    totals = jax.tree.map(take_share, summed)
    grad_norm = 1.0 / math.sqrt(samples_dev * lax.axis_size("dp") * lat_len * kept)
    grad_lat = jnp.einsum(
        "mqhp,smqjc->shpjc", lat_table, grad_spec, preferred_element_type=jnp.float32
    ).astype(jnp.bfloat16)
    returned = lax.all_to_all(grad_lat, "space", split_axis=1, concat_axis=3, tiled=True)
    grad_field = (
        jnp.einsum("wpk,shpkc->shwc", lon_table, returned, preferred_element_type=jnp.float32)
        * ortho_scale
    ).astype(jnp.bfloat16)
    return (
        grad_field,
        totals[0] * grad_norm,
        totals[1] * grad_norm,
        totals[2] * grad_norm,
        totals[3] * grad_norm,
    )


def solution(mesh):
    groups, parts = mesh.shape["dp"], mesh.shape["space"]

    def per_device(*arrays):
        activations, lon_keep = arrays[0], arrays[5]
        fits = (
            parts == BLOCKS
            and 2 * groups == BLOCKS
            and activations.shape[:2] == (1, 2)
            and lon_keep.shape[0] == parts
        )
        return by_blocks(*arrays) if fits else by_frequencies(*arrays)

    return jax.shard_map(
        per_device,
        mesh=mesh,
        in_specs=(
            P("dp", "space", None, None),
            P("dp", "space", None, None),
            P(),
            P(),
            P(),
            P(),
            P("dp", None, None, "space", None),
            P("dp", None, None, "space", None),
        ),
        out_specs=(
            P("dp", "space", None, None),
            P(None, "dp", None),
            P(None, "dp", None),
            P(None, "dp"),
            P(None, "dp"),
        ),
        check_vma=False,
    )
```

```python
import functools
import math

import jax
import jax.numpy as jnp
import numpy as np
from jax import lax
from jax.experimental import pallas as pl
from jax.experimental.pallas import tpu as pltpu
from jax.sharding import PartitionSpec as P

C = 768
BLOCKS = 8
LON = 180
BS = 96

BF = jnp.bfloat16
F32 = jnp.float32
LANES = 128
THIRD = LANES - BS
VMEM_LIMIT = 32 * 1024 * 1024


def shift_of(group):
    return 2 * (group % 2) + group // 2


def block_of(group, device):
    lane = 2 * (device // 4) + device % 2
    return 2 * ((lane + shift_of(group)) % 4) + (device // 2) % 2


def owner_of(group, block):
    lane = (block // 2 + 4 - shift_of(group)) % 4
    return 4 * (lane // 2) + 2 * (block % 2) + lane % 2


def latitude_matrix(lat_len, kept):
    index = np.arange(lat_len)
    angle = ((index[:, None] * index[None, :]) % lat_len).astype(np.float32) * np.float32(
        2.0 * math.pi / lat_len
    )
    cosine, sine = np.cos(angle), np.sin(angle)
    table = np.stack([np.stack([cosine, sine], -1), np.stack([-sine, cosine], -1)], 1)
    full = np.einsum("mphq,jk->pjmhqk", table, np.eye(kept, dtype=np.float32))
    return full.reshape(2 * kept * lat_len, 2 * kept * lat_len)


def dot(lhs, rhs, lhs_axis, rhs_axis):
    return lax.dot_general(
        lhs, rhs, (((lhs_axis,), (rhs_axis,)), ((), ())), preferred_element_type=F32
    )


def fold(array):
    rows = array.shape[0] // 4
    beside = [array[3 * rows :, g * THIRD : (g + 1) * THIRD] for g in range(3)]
    return jnp.concatenate([array[: 3 * rows], jnp.concatenate(beside, axis=0)], axis=1)


def unfold(array):
    rows = array.shape[0] // 3
    beside = [array[g * rows : (g + 1) * rows, BS:] for g in range(3)]
    return jnp.concatenate([array[:, :BS], jnp.concatenate(beside, axis=1)], axis=0)


def window_of(block):
    tile = jnp.minimum(block * BS // LANES, C // LANES - 2)
    return pl.multiple_of(tile * LANES, LANES), block * BS - tile * LANES


def forward_lon_kernel(
    keep_hbm,
    act_hbm,
    cot_hbm,
    relu_hbm,
    shrink_hbm,
    *refs,
):
    weights_hbm, matrices_hbm, refs = refs[:3], refs[3:5], refs[5:]
    out, table_out, *fetched, field, masks, keep, sems = refs
    group, device = lax.axis_index("dp"), lax.axis_index("space")
    start, _ = window_of(block_of(group, device))
    kept = keep.shape[0]
    rows = act_hbm.shape[1]
    modes = relu_hbm.shape[0]
    tiles = C // LANES
    columns = [slice(k * LANES, (k + 1) * LANES) for k in range(tiles)]
    keep_copy = pltpu.make_async_copy(keep_hbm, keep, sems.at[0])
    keep_copy.start()
    mask_copies, field_copies = [], []
    for t, source in enumerate((relu_hbm, shrink_hbm)):
        for p in range(2):
            for k in range(tiles):
                copy = pltpu.make_async_copy(
                    source.at[:, p, :, columns[k]],
                    masks.at[t, p, k],
                    sems.at[1 + (2 * t + p) * tiles + k],
                )
                copy.start()
                mask_copies.append(copy)
    for t, source in enumerate((act_hbm, cot_hbm)):
        for k in range(tiles):
            copy = pltpu.make_async_copy(
                source.at[:, :, columns[k]], field.at[t, k], sems.at[1 + (4 + t) * tiles + k]
            )
            copy.start()
            field_copies.append(copy)
    sources = [
        source.at[(slice(None),) * (len(source.shape) - 1) + (pl.ds(start, 2 * LANES),)]
        for source in weights_hbm
    ] + list(matrices_hbm)
    other_copies = []
    for i, (source, target) in enumerate(zip(sources, fetched)):
        copy = pltpu.make_async_copy(source, target, sems.at[1 + 6 * tiles + i])
        copy.start()
        other_copies.append(copy)

    keep_copy.wait()
    shape = (rows * 2 * kept, LON * rows)
    line = lax.broadcasted_iota(jnp.int32, shape, 0)
    column = lax.broadcasted_iota(jnp.int32, shape, 1)
    frequency = jnp.zeros(shape, jnp.int32)
    for j in range(kept):
        frequency = jnp.where(line % kept == j, keep[j], frequency)
    turn = jnp.where((line // kept) % 2 == 1, LON // 4, 0)
    phase = ((column // rows) * frequency + turn) % LON
    table = jnp.cos(phase.astype(F32) * (2.0 * math.pi / LON))
    wide_table = jnp.where(line // (2 * kept) == column % rows, table, 0.0)
    table = wide_table.astype(BF)
    table_out[...] = wide_table.T.astype(BF)

    own = keep[device]
    scale = jnp.where((own == 0) | (2 * own == LON), 1.0, 2.0)
    for copy in mask_copies:
        copy.wait()

    def gate(t, value):
        return jnp.concatenate(
            [
                jnp.concatenate(
                    [
                        jnp.where(masks.at[t, p, k].reshape(modes, LANES)[...] > 0, value, 0.0)
                        for k in range(tiles)
                    ],
                    axis=1,
                )
                for p in range(2)
            ],
            axis=0,
        ).astype(BF)

    passed = gate(0, 1.0)
    scaled = gate(1, scale)
    per = table.shape[0]
    owners = [owner_of(group, b) for b in range(BLOCKS)]
    for b in range(BLOCKS):
        out[owners[b], 2 * per :, 0:BS] = passed[:, b * BS : (b + 1) * BS]
        beside = [scaled[:, b * BS + g * THIRD : b * BS + (g + 1) * THIRD] for g in range(3)]
        out[owners[b], :, BS:] = jnp.concatenate(beside, axis=0)

    for t in range(2):
        for copy in field_copies[t * tiles : (t + 1) * tiles]:
            copy.wait()
        wide = jnp.concatenate(
            [field.at[t, k].reshape(LON * rows, LANES)[...] for k in range(tiles)], axis=1
        )
        lines = dot(table, wide, 1, 0).astype(BF)
        for b in range(BLOCKS):
            out[owners[b], t * per : (t + 1) * per, 0:BS] = lines[:, b * BS : (b + 1) * BS]
    for copy in other_copies:
        copy.wait()


def block_adjoint(operand, matrix):
    half = operand.shape[0] // 2
    real = dot(operand, matrix[0], 1, 0)
    imag = dot(operand, matrix[1], 1, 0)
    return jnp.concatenate([real[:half] + imag[half:], real[half:] - imag[:half]], axis=0)


def spectral_kernel(
    pieces, first_wide, second_wide, bias_wide, lat, terms, grad_pre_out, first_out, *, ortho_scale, rows, kept
):
    device = lax.axis_index("space")
    _, offset = window_of(block_of(lax.axis_index("dp"), device))
    parts = pieces.shape[0]
    per = rows * 2 * kept
    half = parts * per // 2
    modes = half // kept
    chosen = lax.broadcasted_iota(jnp.int32, (2 * LANES, BS), 0) == (
        lax.broadcasted_iota(jnp.int32, (2 * LANES, BS), 1) + offset
    )
    chosen = jnp.where(chosen, 1.0, 0.0).astype(BF)
    first = [dot(first_wide[p], chosen, 1, 0).astype(BF) for p in range(2)]
    second = [dot(second_wide[p], chosen, 1, 0).astype(BF) for p in range(2)]
    bias = pltpu.roll(bias_wide[...], (2 * LANES - offset) % (2 * LANES), 1)
    opened = [unfold(pieces[i]) for i in range(parts)]

    def spectrum(t):
        stacked = jnp.concatenate([piece[t * per : (t + 1) * per] for piece in opened], axis=0)
        return (dot(lat[...], stacked, 1, 0) * ortho_scale).astype(BF)

    def mask(k):
        start = 2 * per + k * 2 * modes
        return jnp.concatenate(
            [
                opened[j][start + p * modes : start + (p + 1) * modes]
                for p in range(2)
                for j in range(kept)
            ],
            axis=0,
        ).astype(F32)

    spec_act = spectrum(0)
    spec_cot = spectrum(1)
    passed = mask(0) > 0.0
    weight = mask(1)
    grad_out = jnp.where(weight > 0.0, weight * spec_cot.astype(F32), 0.0).astype(BF)

    by_real = dot(spec_act, first[0], 1, 1)
    by_imag = dot(spec_act, first[1], 1, 1)
    pre = jnp.concatenate(
        [
            by_real[:half] - by_imag[half:] + bias[0:1, :BS],
            by_imag[:half] + by_real[half:] + bias[1:2, :BS],
        ],
        axis=0,
    )
    hidden = jnp.where(passed, pre, 0.0).astype(BF)

    grad_pre = jnp.where(passed, block_adjoint(grad_out, second), 0.0).astype(BF)
    grad_pre_out[...] = grad_pre
    for p in range(2):
        first_out[p] = first[p]

    def turned(array):
        return jnp.concatenate([array[half:], -array[:half]], axis=0)

    at = 3 * BS // 4
    blank = jnp.zeros((terms.shape[2] - at - 1, LANES), F32)
    for a, (left, right) in enumerate(((spec_act, grad_pre), (hidden, grad_out))):
        slot = (a + device) % 2
        wide = right.astype(F32)
        for p, other in enumerate((right, turned(right))):
            summed = jnp.sum(wide[p * half : (p + 1) * half], axis=0, keepdims=True)
            summed = jnp.concatenate([summed, jnp.zeros((1, THIRD), F32)], axis=1)
            terms[slot, p] = jnp.concatenate(
                [fold(dot(left, other, 0, 0)), summed, blank], axis=0
            ).astype(BF)


def grad_lat_kernel(grad_pre, first, lat_t, grad_lat):
    grad_spec = block_adjoint(grad_pre[...], first).astype(BF)
    lines = dot(lat_t[...], grad_spec, 1, 0)
    lines = jnp.concatenate([lines, jnp.zeros((lines.shape[0], THIRD), F32)], axis=1).astype(BF)
    grad_lat[...] = lines.reshape(grad_lat.shape)


def inverse_lon_kernel(table, pieces, field_hbm, field, sems, *, ortho_scale):
    rows = field_hbm.shape[1]
    per = table.shape[1]
    tiles = C // LANES
    group = lax.axis_index("dp")
    copies = []
    lines = jnp.concatenate(
        [pieces[owner_of(group, b), 0:per, 0:BS] for b in range(BLOCKS)], axis=1
    )
    for k in range(0, tiles, 2):
        wide = dot(table[...], lines[:, k * LANES : (k + 2) * LANES], 1, 0) * ortho_scale
        for i in range(2):
            field.at[k + i].reshape(LON * rows, LANES)[...] = wide[
                :, i * LANES : (i + 1) * LANES
            ].astype(BF)
            copy = pltpu.make_async_copy(
                field.at[k + i],
                field_hbm.at[:, :, (k + i) * LANES : (k + i + 1) * LANES],
                sems.at[k + i],
            )
            copy.start()
            copies.append(copy)
    for copy in copies:
        copy.wait()


def gathered_kernel(pieces, others, first, second, bias_first, bias_second, *, grad_norm):
    core = lax.axis_index("space") % 2
    per = pieces.shape[1] - others.shape[1]
    at = 3 * BS // 4
    for a, (target, vector) in enumerate(((first, bias_first), (second, bias_second))):
        for k in range(2):
            near, far = 2 * k + a, 4 + 2 * k + a
            own = pieces[near, per:, :].astype(F32) + pieces[far, per:, :].astype(F32)
            other = others[near].astype(F32) + others[far].astype(F32)
            for p in range(2):
                total = jnp.where(core == p, own, other) * grad_norm
                target[p, k * BS : (k + 1) * BS, :] = unfold(total[:at])
                vector[p : p + 1, k * BS : (k + 1) * BS] = total[at : at + 1, :BS]


def whole(memory=pltpu.VMEM):
    return pl.BlockSpec(memory_space=memory)


def by_blocks(
    activations, cotangent, w_first, w_second, b_first, lon_keep, relu_mask, shrink_mask
):
    groups = lax.axis_size("dp")
    parts = lax.axis_size("space")
    rows = activations.shape[1]
    lat_len = rows * parts
    kept = lon_keep.shape[0]
    ortho_scale = 1.0 / math.sqrt(lat_len * LON)
    grad_norm = 1.0 / math.sqrt(groups * lat_len * kept)
    params = pltpu.CompilerParams(vmem_limit_bytes=VMEM_LIMIT)
    tiles = C // LANES
    per = rows * 2 * kept
    height = (2 * per + 4 * lat_len) * 3 // 4
    term_rows = 3 * BS // 4 + 8

    lat = latitude_matrix(lat_len, kept)
    sent, table, *fetched = pl.pallas_call(
        forward_lon_kernel,
        out_shape=(
            pltpu.VMEM((parts, height, LANES), BF),
            pltpu.VMEM((LON * rows, per), BF),
            pltpu.VMEM((2, BS, 2 * LANES), BF),
            pltpu.VMEM((2, BS, 2 * LANES), BF),
            pltpu.VMEM((2, 2 * LANES), F32),
            pltpu.VMEM(lat.shape, BF),
            pltpu.VMEM(lat.shape, BF),
        ),
        in_specs=[whole(pl.ANY)] * 10,
        out_specs=(whole(),) * 7,
        scratch_shapes=[
            pltpu.VMEM((2, tiles, LON, rows, LANES), BF),
            pltpu.VMEM((2, 2, tiles, lat_len, 1, LANES), jnp.int32),
            pltpu.SMEM((kept,), jnp.int32),
            pltpu.SemaphoreType.DMA((6 + 6 * tiles,)),
        ],
        compiler_params=params,
        name="forward_lon",
    )(
        *(
            pltpu.with_memory_space_constraint(array, pltpu.HBM)
            for array in (
                lon_keep,
                activations[0].transpose(1, 0, 2),
                cotangent[0].transpose(1, 0, 2),
                relu_mask[0],
                shrink_mask[0],
                w_first.transpose(0, 2, 1),
                w_second.transpose(0, 2, 1),
                b_first,
                jnp.asarray(lat, BF),
                jnp.asarray(lat.T, BF),
            )
        )
    )
    pieces = lax.all_to_all(sent, "space", 0, 0, tiled=True)

    *fetched, lat_t = fetched
    terms, grad_pre, first_block = pl.pallas_call(
        functools.partial(spectral_kernel, ortho_scale=ortho_scale, rows=rows, kept=kept),
        out_shape=(
            jax.ShapeDtypeStruct((2, 2, term_rows, LANES), BF),
            pltpu.VMEM((lat.shape[0], BS), BF),
            pltpu.VMEM((2, BS, BS), BF),
        ),
        in_specs=[whole()] * 5,
        out_specs=(whole(),) * 3,
        compiler_params=params,
        name="spectral",
    )(pieces, *fetched)
    grad_lat = pl.pallas_call(
        grad_lat_kernel,
        out_shape=jax.ShapeDtypeStruct((parts, per, LANES), BF),
        in_specs=[whole()] * 3,
        out_specs=whole(),
        compiler_params=params,
        cost_estimate=pl.CostEstimate(
            flops=2 * lat.size * BS * 3, bytes_accessed=4 * lat.size, transcendentals=0
        ),
        name="grad_lat",
    )(grad_pre, first_block, lat_t)

    arrived = lax.ppermute(
        terms,
        ("dp", "space"),
        [
            (g * parts + c, (block_of(g, c) // 2) * parts + c)
            for g in range(groups)
            for c in range(parts)
        ],
    )
    other = lax.ppermute(arrived[1], "space", [(c, c ^ 1) for c in range(parts)])
    share = (arrived[0].astype(F32) + other.astype(F32)).astype(BF)
    share = jnp.broadcast_to(share[None], (parts // 2,) + share.shape)
    returned = lax.all_to_all(
        jnp.concatenate([grad_lat, share.reshape(parts, term_rows, LANES)], axis=1),
        "space",
        0,
        0,
        tiled=True,
    )
    others = lax.ppermute(returned[:, per:, :], "space", [(c, c ^ 1) for c in range(parts)])

    keep_rows = C // groups
    field = pl.pallas_call(
        functools.partial(inverse_lon_kernel, ortho_scale=ortho_scale),
        out_shape=jax.ShapeDtypeStruct((LON, rows, C), BF),
        in_specs=[whole(), whole()],
        out_specs=whole(pl.ANY),
        scratch_shapes=[
            pltpu.VMEM((tiles, LON, rows, LANES), BF),
            pltpu.SemaphoreType.DMA((tiles,)),
        ],
        compiler_params=params,
        cost_estimate=pl.CostEstimate(
            flops=2 * per * LON * rows * C, bytes_accessed=8 * LON * rows * C, transcendentals=0
        ),
        name="inverse_lon",
    )(table, returned)
    first, second, bias_first, bias_second = pl.pallas_call(
        functools.partial(gathered_kernel, grad_norm=grad_norm),
        out_shape=(
            jax.ShapeDtypeStruct((2, keep_rows, BS), F32),
            jax.ShapeDtypeStruct((2, keep_rows, BS), F32),
            jax.ShapeDtypeStruct((2, keep_rows), F32),
            jax.ShapeDtypeStruct((2, keep_rows), F32),
        ),
        in_specs=[whole(), whole()],
        out_specs=(whole(),) * 4,
        compiler_params=params,
        name="gathered",
    )(returned, others)
    return field.transpose(1, 0, 2)[None], first, second, bias_first, bias_second


def build_tables(lon_keep, lat_len, lon_len):
    columns = jnp.arange(lon_len, dtype=jnp.int32)
    lon_phase = columns[:, None] * lon_keep[None, :] % lon_len
    lon_angle = lon_phase.astype(jnp.float32) * (2.0 * math.pi / lon_len)
    lon_table = jnp.stack([jnp.cos(lon_angle), -jnp.sin(lon_angle)], axis=1).astype(jnp.bfloat16)
    latitudes = jnp.arange(lat_len, dtype=jnp.int32)
    lat_phase = latitudes[:, None] * latitudes[None, :] % lat_len
    lat_angle = lat_phase.astype(jnp.float32) * (2.0 * math.pi / lat_len)
    cosine = jnp.cos(lat_angle)
    sine_part = jnp.sin(lat_angle)
    lat_table = jnp.stack(
        [jnp.stack([cosine, sine_part], axis=-1), jnp.stack([-sine_part, cosine], axis=-1)], axis=1
    ).astype(jnp.bfloat16)
    return (lon_table, lat_table)


def apply_blocks(operand, matrix):
    return jnp.einsum("smjbc,bcd->smjbd", operand, matrix, preferred_element_type=jnp.float32)


def adjoint(operand, matrix):
    return jnp.einsum("smjbd,bcd->smjbc", operand, matrix, preferred_element_type=jnp.float32)


def outer_sum(operand, other):
    return jnp.einsum("smjbc,smjbd->bcd", operand, other, preferred_element_type=jnp.float32)


def by_frequencies(
    activations, cotangent, w_first, w_second, b_first, lon_keep, relu_mask, shrink_mask
):
    parts = lax.axis_size("space")
    samples_dev = activations.shape[0]
    lat_len = activations.shape[1] * parts
    kept = lon_keep.shape[0]
    owned = kept // parts
    lon_table, lat_table = build_tables(lon_keep, lat_len, LON)
    ortho_scale = 1.0 / math.sqrt(lat_len * LON)
    act_lon = jnp.einsum(
        "shwc,wpk->shpkc", activations, lon_table, preferred_element_type=jnp.float32
    ).astype(jnp.bfloat16)
    cot_lon = jnp.einsum(
        "shwc,wpk->shpkc", cotangent, lon_table, preferred_element_type=jnp.float32
    ).astype(jnp.bfloat16)
    act_modes, cot_modes = (
        lax.all_to_all(act_lon, "space", split_axis=3, concat_axis=1, tiled=True),
        lax.all_to_all(cot_lon, "space", split_axis=3, concat_axis=1, tiled=True),
    )

    def latitude(modes):
        summed = jnp.einsum(
            "mphq,shqjc->smpjc", lat_table, modes, preferred_element_type=jnp.float32
        )
        return (summed * ortho_scale).astype(jnp.bfloat16)

    block_shape = (samples_dev, lat_len, 2, owned, BLOCKS, BS)
    spec_act = latitude(act_modes).reshape(block_shape)
    spec_cot = latitude(cot_modes)
    own_keep = lax.dynamic_slice_in_dim(lon_keep, lax.axis_index("space") * owned, owned)
    doubled = jnp.where((own_keep == 0) | (2 * own_keep == LON), 1.0, 2.0).astype(jnp.float32)
    grad_out = (
        jnp.where(
            shrink_mask > 0, doubled[None, None, None, :, None] * spec_cot.astype(jnp.float32), 0.0
        )
        .astype(jnp.bfloat16)
        .reshape(block_shape)
    )
    relu_gate = relu_mask.reshape(block_shape) > 0
    first_blocks = w_first.reshape(2, BLOCKS, BS, BS)
    second_blocks = w_second.reshape(2, BLOCKS, BS, BS)
    bias_blocks = b_first.reshape(2, BLOCKS, BS)
    act_real = spec_act[:, :, 0]
    act_imag = spec_act[:, :, 1]
    pre_real = (
        apply_blocks(act_real, first_blocks[0])
        - apply_blocks(act_imag, first_blocks[1])
        + bias_blocks[0]
    )
    pre_imag = (
        apply_blocks(act_real, first_blocks[1])
        + apply_blocks(act_imag, first_blocks[0])
        + bias_blocks[1]
    )
    hidden = jnp.where(relu_gate, jnp.stack([pre_real, pre_imag], axis=2), 0.0).astype(jnp.bfloat16)
    out_real = grad_out[:, :, 0]
    out_imag = grad_out[:, :, 1]
    hidden_real = adjoint(out_real, second_blocks[0]) + adjoint(out_imag, second_blocks[1])
    hidden_imag = -adjoint(out_real, second_blocks[1]) + adjoint(out_imag, second_blocks[0])
    grad_pre = jnp.where(relu_gate, jnp.stack([hidden_real, hidden_imag], axis=2), 0.0).astype(
        jnp.bfloat16
    )
    pre_grad_real = grad_pre[:, :, 0]
    pre_grad_imag = grad_pre[:, :, 1]
    spec_real = adjoint(pre_grad_real, first_blocks[0]) + adjoint(pre_grad_imag, first_blocks[1])
    spec_imag = -adjoint(pre_grad_real, first_blocks[1]) + adjoint(pre_grad_imag, first_blocks[0])
    grad_spec = (
        jnp.stack([spec_real, spec_imag], axis=2)
        .astype(jnp.bfloat16)
        .reshape(samples_dev, lat_len, 2, owned, C)
    )
    first_grad = jnp.stack(
        [
            outer_sum(act_real, pre_grad_real) + outer_sum(act_imag, pre_grad_imag),
            outer_sum(act_real, pre_grad_imag) - outer_sum(act_imag, pre_grad_real),
        ]
    ).reshape(2, C, BS)
    hid_real = hidden[:, :, 0]
    hid_imag = hidden[:, :, 1]
    second_grad = jnp.stack(
        [
            outer_sum(hid_real, out_real) + outer_sum(hid_imag, out_imag),
            outer_sum(hid_real, out_imag) - outer_sum(hid_imag, out_real),
        ]
    ).reshape(2, C, BS)
    bias_first = jnp.sum(grad_pre, axis=(0, 1, 3), dtype=jnp.float32).reshape(2, C)
    bias_second = jnp.sum(grad_out, axis=(0, 1, 3), dtype=jnp.float32).reshape(2, C)
    local_terms = (first_grad, second_grad, bias_first, bias_second)
    summed = lax.psum(
        (local_terms[0], local_terms[1], local_terms[2], local_terms[3]), ("dp", "space")
    )
    share_rows = C // lax.axis_size("dp")
    row_start = lax.axis_index("dp") * share_rows

    def take_share(array):
        return lax.dynamic_slice_in_dim(array, row_start, share_rows, 1)

    totals = jax.tree.map(take_share, summed)
    grad_norm = 1.0 / math.sqrt(samples_dev * lax.axis_size("dp") * lat_len * kept)
    grad_lat = jnp.einsum(
        "mqhp,smqjc->shpjc", lat_table, grad_spec, preferred_element_type=jnp.float32
    ).astype(jnp.bfloat16)
    returned = lax.all_to_all(grad_lat, "space", split_axis=1, concat_axis=3, tiled=True)
    grad_field = (
        jnp.einsum("wpk,shpkc->shwc", lon_table, returned, preferred_element_type=jnp.float32)
        * ortho_scale
    ).astype(jnp.bfloat16)
    return (
        grad_field,
        totals[0] * grad_norm,
        totals[1] * grad_norm,
        totals[2] * grad_norm,
        totals[3] * grad_norm,
    )


def solution(mesh):
    groups, parts = mesh.shape["dp"], mesh.shape["space"]

    def per_device(*arrays):
        activations, lon_keep = arrays[0], arrays[5]
        fits = (
            parts == BLOCKS
            and 2 * groups == BLOCKS
            and activations.shape[:2] == (1, 2)
            and lon_keep.shape[0] == parts
        )
        return by_blocks(*arrays) if fits else by_frequencies(*arrays)

    return jax.shard_map(
        per_device,
        mesh=mesh,
        in_specs=(
            P("dp", "space", None, None),
            P("dp", "space", None, None),
            P(),
            P(),
            P(),
            P(),
            P("dp", None, None, "space", None),
            P("dp", None, None, "space", None),
        ),
        out_specs=(
            P("dp", "space", None, None),
            P(None, "dp", None),
            P(None, "dp", None),
            P(None, "dp"),
            P(None, "dp"),
        ),
        check_vma=False,
    )
```

```python
import functools
import math

import jax
import jax.numpy as jnp
import numpy as np
from jax import lax
from jax.experimental import pallas as pl
from jax.experimental.pallas import tpu as pltpu
from jax.sharding import PartitionSpec as P

C = 768
BLOCKS = 8
LON = 180
BS = 96

BF = jnp.bfloat16
F32 = jnp.float32
LANES = 128
THIRD = LANES - BS
LON_ROOM = 192
VMEM_LIMIT = 32 * 1024 * 1024


def shift_of(group):
    return 2 * (group % 2) + group // 2


def block_of(group, device):
    lane = 2 * (device // 4) + device % 2
    return 2 * ((lane + shift_of(group)) % 4) + (device // 2) % 2


def owner_of(group, block):
    lane = (block // 2 + 4 - shift_of(group)) % 4
    return 4 * (lane // 2) + 2 * (block % 2) + lane % 2


def latitude_matrix(lat_len, kept):
    index = np.arange(lat_len)
    angle = ((index[:, None] * index[None, :]) % lat_len).astype(np.float32) * np.float32(
        2.0 * math.pi / lat_len
    )
    cosine, sine = np.cos(angle), np.sin(angle)
    table = np.stack([np.stack([cosine, sine], -1), np.stack([-sine, cosine], -1)], 1)
    full = np.einsum("mphq,jk->pjmhqk", table, np.eye(kept, dtype=np.float32))
    return full.reshape(2 * kept * lat_len, 2 * kept * lat_len)


def dot(lhs, rhs, lhs_axis, rhs_axis):
    return lax.dot_general(
        lhs, rhs, (((lhs_axis,), (rhs_axis,)), ((), ())), preferred_element_type=F32
    )


def fold(array):
    rows = array.shape[0] // 4
    beside = [array[3 * rows :, g * THIRD : (g + 1) * THIRD] for g in range(3)]
    return jnp.concatenate([array[: 3 * rows], jnp.concatenate(beside, axis=0)], axis=1)


def unfold(array):
    rows = array.shape[0] // 3
    beside = [array[g * rows : (g + 1) * rows, BS:] for g in range(3)]
    return jnp.concatenate([array[:, :BS], jnp.concatenate(beside, axis=1)], axis=0)


def window_of(block):
    tile = jnp.minimum(block * BS // LANES, C // LANES - 2)
    return pl.multiple_of(tile * LANES, LANES), block * BS - tile * LANES


def forward_lon_kernel(
    keep_hbm,
    act_hbm,
    cot_hbm,
    relu_hbm,
    shrink_hbm,
    *refs,
):
    weights_hbm, matrices_hbm, refs = refs[:3], refs[3:5], refs[5:]
    out, table_out, *fetched, field, masks, keep, sems = refs
    group, device = lax.axis_index("dp"), lax.axis_index("space")
    start, _ = window_of(block_of(group, device))
    kept = keep.shape[0]
    rows = act_hbm.shape[1]
    modes = relu_hbm.shape[0]
    tiles = C // LANES
    columns = [slice(k * LANES, (k + 1) * LANES) for k in range(tiles)]
    keep_copy = pltpu.make_async_copy(keep_hbm, keep, sems.at[0])
    keep_copy.start()
    mask_copies, field_copies = [], []
    for t, source in enumerate((relu_hbm, shrink_hbm)):
        for p in range(2):
            for k in range(tiles):
                copy = pltpu.make_async_copy(
                    source.at[:, p, :, columns[k]],
                    masks.at[t, p, k],
                    sems.at[1 + (2 * t + p) * tiles + k],
                )
                copy.start()
                mask_copies.append(copy)
    for t, source in enumerate((act_hbm, cot_hbm)):
        for k in range(tiles):
            copy = pltpu.make_async_copy(
                source.at[:, :, columns[k]], field.at[t, k, 0:LON], sems.at[1 + (4 + t) * tiles + k]
            )
            copy.start()
            field_copies.append(copy)
    sources = [
        source.at[(slice(None),) * (len(source.shape) - 1) + (pl.ds(start, 2 * LANES),)]
        for source in weights_hbm
    ] + list(matrices_hbm)
    other_copies = []
    for i, (source, target) in enumerate(zip(sources, fetched)):
        copy = pltpu.make_async_copy(source, target, sems.at[1 + 6 * tiles + i])
        copy.start()
        other_copies.append(copy)

    keep_copy.wait()
    shape = (rows * 2 * kept, LON * rows)
    line = lax.broadcasted_iota(jnp.int32, shape, 0)
    column = lax.broadcasted_iota(jnp.int32, shape, 1)
    frequency = jnp.zeros(shape, jnp.int32)
    for j in range(kept):
        frequency = jnp.where(line % kept == j, keep[j], frequency)
    turn = jnp.where((line // kept) % 2 == 1, LON // 4, 0)
    phase = ((column // rows) * frequency + turn) % LON
    table = jnp.cos(phase.astype(F32) * (2.0 * math.pi / LON))
    wide_table = jnp.where(line // (2 * kept) == column % rows, table, 0.0)
    table = wide_table.astype(BF)
    table_out[...] = wide_table.T.astype(BF)

    own = keep[device]
    scale = jnp.where((own == 0) | (2 * own == LON), 1.0, 2.0)
    for copy in mask_copies:
        copy.wait()

    def gate(t, value):
        return jnp.concatenate(
            [
                jnp.concatenate(
                    [
                        jnp.where(masks.at[t, p, k].reshape(modes, LANES)[...] > 0, value, 0.0)
                        for k in range(tiles)
                    ],
                    axis=1,
                )
                for p in range(2)
            ],
            axis=0,
        ).astype(BF)

    passed = gate(0, 1.0)
    scaled = gate(1, scale)
    per = table.shape[0]
    owners = [owner_of(group, b) for b in range(BLOCKS)]
    for b in range(BLOCKS):
        out[owners[b], 2 * per :, 0:BS] = passed[:, b * BS : (b + 1) * BS]
        beside = [scaled[:, b * BS + g * THIRD : b * BS + (g + 1) * THIRD] for g in range(3)]
        out[owners[b], :, BS:] = jnp.concatenate(beside, axis=0)

    for t in range(2):
        for copy in field_copies[t * tiles : (t + 1) * tiles]:
            copy.wait()
        wide = jnp.concatenate(
            [
                field.at[t, k].reshape(LON_ROOM * rows, LANES)[0 : LON * rows]
                for k in range(tiles)
            ],
            axis=1,
        )
        lines = dot(table, wide, 1, 0).astype(BF)
        for b in range(BLOCKS):
            out[owners[b], t * per : (t + 1) * per, 0:BS] = lines[:, b * BS : (b + 1) * BS]
    for copy in other_copies:
        copy.wait()


def block_adjoint(operand, matrix):
    half = operand.shape[0] // 2
    real = dot(operand, matrix[0], 1, 0)
    imag = dot(operand, matrix[1], 1, 0)
    return jnp.concatenate([real[:half] + imag[half:], real[half:] - imag[:half]], axis=0)


def spectral_kernel(
    pieces, first_wide, second_wide, bias_wide, lat, terms, grad_pre_out, first_out, *, ortho_scale, rows, kept
):
    device = lax.axis_index("space")
    _, offset = window_of(block_of(lax.axis_index("dp"), device))
    parts = pieces.shape[0]
    per = rows * 2 * kept
    half = parts * per // 2
    modes = half // kept
    chosen = lax.broadcasted_iota(jnp.int32, (2 * LANES, BS), 0) == (
        lax.broadcasted_iota(jnp.int32, (2 * LANES, BS), 1) + offset
    )
    chosen = jnp.where(chosen, 1.0, 0.0).astype(BF)
    first = [dot(first_wide[p], chosen, 1, 0).astype(BF) for p in range(2)]
    second = [dot(second_wide[p], chosen, 1, 0).astype(BF) for p in range(2)]
    bias = pltpu.roll(bias_wide[...], (2 * LANES - offset) % (2 * LANES), 1)
    opened = [unfold(pieces[i]) for i in range(parts)]

    def spectrum(t):
        stacked = jnp.concatenate([piece[t * per : (t + 1) * per] for piece in opened], axis=0)
        return (dot(lat[...], stacked, 1, 0) * ortho_scale).astype(BF)

    def mask(k):
        start = 2 * per + k * 2 * modes
        return jnp.concatenate(
            [
                opened[j][start + p * modes : start + (p + 1) * modes]
                for p in range(2)
                for j in range(kept)
            ],
            axis=0,
        ).astype(F32)

    spec_act = spectrum(0)
    spec_cot = spectrum(1)
    passed = mask(0) > 0.0
    weight = mask(1)
    grad_out = jnp.where(weight > 0.0, weight * spec_cot.astype(F32), 0.0).astype(BF)

    by_real = dot(spec_act, first[0], 1, 1)
    by_imag = dot(spec_act, first[1], 1, 1)
    pre = jnp.concatenate(
        [
            by_real[:half] - by_imag[half:] + bias[0:1, :BS],
            by_imag[:half] + by_real[half:] + bias[1:2, :BS],
        ],
        axis=0,
    )
    hidden = jnp.where(passed, pre, 0.0).astype(BF)

    grad_pre = jnp.where(passed, block_adjoint(grad_out, second), 0.0).astype(BF)
    grad_pre_out[...] = grad_pre
    for p in range(2):
        first_out[p] = first[p]

    def turned(array):
        return jnp.concatenate([array[half:], -array[:half]], axis=0)

    at = 3 * BS // 4
    blank = jnp.zeros((terms.shape[2] - at - 1, LANES), F32)
    for a, (left, right) in enumerate(((spec_act, grad_pre), (hidden, grad_out))):
        slot = (a + device) % 2
        wide = right.astype(F32)
        for p, other in enumerate((right, turned(right))):
            summed = jnp.sum(wide[p * half : (p + 1) * half], axis=0, keepdims=True)
            summed = jnp.concatenate([summed, jnp.zeros((1, THIRD), F32)], axis=1)
            terms[slot, p] = jnp.concatenate(
                [fold(dot(left, other, 0, 0)), summed, blank], axis=0
            ).astype(BF)


def grad_lat_kernel(grad_pre, first, lat_t, grad_lat):
    grad_spec = block_adjoint(grad_pre[...], first).astype(BF)
    lines = dot(lat_t[...], grad_spec, 1, 0)
    lines = jnp.concatenate([lines, jnp.zeros((lines.shape[0], THIRD), F32)], axis=1).astype(BF)
    grad_lat[...] = lines.reshape(grad_lat.shape)


def inverse_lon_kernel(table, pieces, field_hbm, field, sems, *, ortho_scale):
    rows = field_hbm.shape[1]
    per = table.shape[1]
    tiles = C // LANES
    group = lax.axis_index("dp")
    copies = []
    lines = jnp.concatenate(
        [pieces[owner_of(group, b), 0:per, 0:BS] for b in range(BLOCKS)], axis=1
    )
    for k in range(0, tiles, 2):
        wide = dot(table[...], lines[:, k * LANES : (k + 2) * LANES], 1, 0) * ortho_scale
        for i in range(2):
            field.at[k + i].reshape(LON_ROOM * rows, LANES)[0 : LON * rows] = wide[
                :, i * LANES : (i + 1) * LANES
            ].astype(BF)
            copy = pltpu.make_async_copy(
                field.at[k + i, 0:LON],
                field_hbm.at[:, :, (k + i) * LANES : (k + i + 1) * LANES],
                sems.at[k + i],
            )
            copy.start()
            copies.append(copy)
    for copy in copies:
        copy.wait()


def gathered_kernel(pieces, others, first, second, bias_first, bias_second, *, grad_norm):
    core = lax.axis_index("space") % 2
    per = pieces.shape[1] - others.shape[1]
    at = 3 * BS // 4
    for a, (target, vector) in enumerate(((first, bias_first), (second, bias_second))):
        for k in range(2):
            near, far = 2 * k + a, 4 + 2 * k + a
            own = pieces[near, per:, :].astype(F32) + pieces[far, per:, :].astype(F32)
            other = others[near].astype(F32) + others[far].astype(F32)
            for p in range(2):
                total = jnp.where(core == p, own, other) * grad_norm
                target[p, k * BS : (k + 1) * BS, :] = unfold(total[:at])
                vector[p : p + 1, k * BS : (k + 1) * BS] = total[at : at + 1, :BS]


def whole(memory=pltpu.VMEM):
    return pl.BlockSpec(memory_space=memory)


def by_blocks(
    activations, cotangent, w_first, w_second, b_first, lon_keep, relu_mask, shrink_mask
):
    groups = lax.axis_size("dp")
    parts = lax.axis_size("space")
    rows = activations.shape[1]
    lat_len = rows * parts
    kept = lon_keep.shape[0]
    ortho_scale = 1.0 / math.sqrt(lat_len * LON)
    grad_norm = 1.0 / math.sqrt(groups * lat_len * kept)
    params = pltpu.CompilerParams(vmem_limit_bytes=VMEM_LIMIT)
    tiles = C // LANES
    per = rows * 2 * kept
    height = (2 * per + 4 * lat_len) * 3 // 4
    term_rows = 3 * BS // 4 + 8

    lat = latitude_matrix(lat_len, kept)
    sent, table, *fetched = pl.pallas_call(
        forward_lon_kernel,
        out_shape=(
            pltpu.VMEM((parts, height, LANES), BF),
            pltpu.VMEM((LON * rows, per), BF),
            pltpu.VMEM((2, BS, 2 * LANES), BF),
            pltpu.VMEM((2, BS, 2 * LANES), BF),
            pltpu.VMEM((2, 2 * LANES), F32),
            pltpu.VMEM(lat.shape, BF),
            pltpu.VMEM(lat.shape, BF),
        ),
        in_specs=[whole(pl.ANY)] * 10,
        out_specs=(whole(),) * 7,
        scratch_shapes=[
            pltpu.VMEM((2, tiles, LON_ROOM, rows, LANES), BF),
            pltpu.VMEM((2, 2, tiles, lat_len, 1, LANES), jnp.int32),
            pltpu.SMEM((kept,), jnp.int32),
            pltpu.SemaphoreType.DMA((6 + 6 * tiles,)),
        ],
        compiler_params=params,
        name="forward_lon",
    )(
        *(
            pltpu.with_memory_space_constraint(array, pltpu.HBM)
            for array in (
                lon_keep,
                activations[0].transpose(1, 0, 2),
                cotangent[0].transpose(1, 0, 2),
                relu_mask[0],
                shrink_mask[0],
                w_first.transpose(0, 2, 1),
                w_second.transpose(0, 2, 1),
                b_first,
                jnp.asarray(lat, BF),
                jnp.asarray(lat.T, BF),
            )
        )
    )
    pieces = lax.all_to_all(sent, "space", 0, 0, tiled=True)

    *fetched, lat_t = fetched
    terms, grad_pre, first_block = pl.pallas_call(
        functools.partial(spectral_kernel, ortho_scale=ortho_scale, rows=rows, kept=kept),
        out_shape=(
            jax.ShapeDtypeStruct((2, 2, term_rows, LANES), BF),
            pltpu.VMEM((lat.shape[0], BS), BF),
            pltpu.VMEM((2, BS, BS), BF),
        ),
        in_specs=[whole()] * 5,
        out_specs=(whole(),) * 3,
        compiler_params=params,
        name="spectral",
    )(pieces, *fetched)
    grad_lat = pl.pallas_call(
        grad_lat_kernel,
        out_shape=jax.ShapeDtypeStruct((parts, per, LANES), BF),
        in_specs=[whole()] * 3,
        out_specs=whole(),
        compiler_params=params,
        cost_estimate=pl.CostEstimate(
            flops=2 * lat.size * BS * 3, bytes_accessed=4 * lat.size, transcendentals=0
        ),
        name="grad_lat",
    )(grad_pre, first_block, lat_t)

    arrived = lax.ppermute(
        terms,
        ("dp", "space"),
        [
            (g * parts + c, (block_of(g, c) // 2) * parts + c)
            for g in range(groups)
            for c in range(parts)
        ],
    )
    other = lax.ppermute(arrived[1], "space", [(c, c ^ 1) for c in range(parts)])
    share = (arrived[0].astype(F32) + other.astype(F32)).astype(BF)
    share = jnp.broadcast_to(share[None], (parts // 2,) + share.shape)
    returned = lax.all_to_all(
        jnp.concatenate([grad_lat, share.reshape(parts, term_rows, LANES)], axis=1),
        "space",
        0,
        0,
        tiled=True,
    )
    others = lax.ppermute(returned[:, per:, :], "space", [(c, c ^ 1) for c in range(parts)])

    keep_rows = C // groups
    field = pl.pallas_call(
        functools.partial(inverse_lon_kernel, ortho_scale=ortho_scale),
        out_shape=jax.ShapeDtypeStruct((LON, rows, C), BF),
        in_specs=[whole(), whole()],
        out_specs=whole(pl.ANY),
        scratch_shapes=[
            pltpu.VMEM((tiles, LON_ROOM, rows, LANES), BF),
            pltpu.SemaphoreType.DMA((tiles,)),
        ],
        compiler_params=params,
        cost_estimate=pl.CostEstimate(
            flops=2 * per * LON * rows * C, bytes_accessed=8 * LON * rows * C, transcendentals=0
        ),
        name="inverse_lon",
    )(table, returned)
    first, second, bias_first, bias_second = pl.pallas_call(
        functools.partial(gathered_kernel, grad_norm=grad_norm),
        out_shape=(
            jax.ShapeDtypeStruct((2, keep_rows, BS), F32),
            jax.ShapeDtypeStruct((2, keep_rows, BS), F32),
            jax.ShapeDtypeStruct((2, keep_rows), F32),
            jax.ShapeDtypeStruct((2, keep_rows), F32),
        ),
        in_specs=[whole(), whole()],
        out_specs=(whole(),) * 4,
        compiler_params=params,
        name="gathered",
    )(returned, others)
    return field.transpose(1, 0, 2)[None], first, second, bias_first, bias_second


def build_tables(lon_keep, lat_len, lon_len):
    columns = jnp.arange(lon_len, dtype=jnp.int32)
    lon_phase = columns[:, None] * lon_keep[None, :] % lon_len
    lon_angle = lon_phase.astype(jnp.float32) * (2.0 * math.pi / lon_len)
    lon_table = jnp.stack([jnp.cos(lon_angle), -jnp.sin(lon_angle)], axis=1).astype(jnp.bfloat16)
    latitudes = jnp.arange(lat_len, dtype=jnp.int32)
    lat_phase = latitudes[:, None] * latitudes[None, :] % lat_len
    lat_angle = lat_phase.astype(jnp.float32) * (2.0 * math.pi / lat_len)
    cosine = jnp.cos(lat_angle)
    sine_part = jnp.sin(lat_angle)
    lat_table = jnp.stack(
        [jnp.stack([cosine, sine_part], axis=-1), jnp.stack([-sine_part, cosine], axis=-1)], axis=1
    ).astype(jnp.bfloat16)
    return (lon_table, lat_table)


def apply_blocks(operand, matrix):
    return jnp.einsum("smjbc,bcd->smjbd", operand, matrix, preferred_element_type=jnp.float32)


def adjoint(operand, matrix):
    return jnp.einsum("smjbd,bcd->smjbc", operand, matrix, preferred_element_type=jnp.float32)


def outer_sum(operand, other):
    return jnp.einsum("smjbc,smjbd->bcd", operand, other, preferred_element_type=jnp.float32)


def by_frequencies(
    activations, cotangent, w_first, w_second, b_first, lon_keep, relu_mask, shrink_mask
):
    parts = lax.axis_size("space")
    samples_dev = activations.shape[0]
    lat_len = activations.shape[1] * parts
    kept = lon_keep.shape[0]
    owned = kept // parts
    lon_table, lat_table = build_tables(lon_keep, lat_len, LON)
    ortho_scale = 1.0 / math.sqrt(lat_len * LON)
    act_lon = jnp.einsum(
        "shwc,wpk->shpkc", activations, lon_table, preferred_element_type=jnp.float32
    ).astype(jnp.bfloat16)
    cot_lon = jnp.einsum(
        "shwc,wpk->shpkc", cotangent, lon_table, preferred_element_type=jnp.float32
    ).astype(jnp.bfloat16)
    act_modes, cot_modes = (
        lax.all_to_all(act_lon, "space", split_axis=3, concat_axis=1, tiled=True),
        lax.all_to_all(cot_lon, "space", split_axis=3, concat_axis=1, tiled=True),
    )

    def latitude(modes):
        summed = jnp.einsum(
            "mphq,shqjc->smpjc", lat_table, modes, preferred_element_type=jnp.float32
        )
        return (summed * ortho_scale).astype(jnp.bfloat16)

    block_shape = (samples_dev, lat_len, 2, owned, BLOCKS, BS)
    spec_act = latitude(act_modes).reshape(block_shape)
    spec_cot = latitude(cot_modes)
    own_keep = lax.dynamic_slice_in_dim(lon_keep, lax.axis_index("space") * owned, owned)
    doubled = jnp.where((own_keep == 0) | (2 * own_keep == LON), 1.0, 2.0).astype(jnp.float32)
    grad_out = (
        jnp.where(
            shrink_mask > 0, doubled[None, None, None, :, None] * spec_cot.astype(jnp.float32), 0.0
        )
        .astype(jnp.bfloat16)
        .reshape(block_shape)
    )
    relu_gate = relu_mask.reshape(block_shape) > 0
    first_blocks = w_first.reshape(2, BLOCKS, BS, BS)
    second_blocks = w_second.reshape(2, BLOCKS, BS, BS)
    bias_blocks = b_first.reshape(2, BLOCKS, BS)
    act_real = spec_act[:, :, 0]
    act_imag = spec_act[:, :, 1]
    pre_real = (
        apply_blocks(act_real, first_blocks[0])
        - apply_blocks(act_imag, first_blocks[1])
        + bias_blocks[0]
    )
    pre_imag = (
        apply_blocks(act_real, first_blocks[1])
        + apply_blocks(act_imag, first_blocks[0])
        + bias_blocks[1]
    )
    hidden = jnp.where(relu_gate, jnp.stack([pre_real, pre_imag], axis=2), 0.0).astype(jnp.bfloat16)
    out_real = grad_out[:, :, 0]
    out_imag = grad_out[:, :, 1]
    hidden_real = adjoint(out_real, second_blocks[0]) + adjoint(out_imag, second_blocks[1])
    hidden_imag = -adjoint(out_real, second_blocks[1]) + adjoint(out_imag, second_blocks[0])
    grad_pre = jnp.where(relu_gate, jnp.stack([hidden_real, hidden_imag], axis=2), 0.0).astype(
        jnp.bfloat16
    )
    pre_grad_real = grad_pre[:, :, 0]
    pre_grad_imag = grad_pre[:, :, 1]
    spec_real = adjoint(pre_grad_real, first_blocks[0]) + adjoint(pre_grad_imag, first_blocks[1])
    spec_imag = -adjoint(pre_grad_real, first_blocks[1]) + adjoint(pre_grad_imag, first_blocks[0])
    grad_spec = (
        jnp.stack([spec_real, spec_imag], axis=2)
        .astype(jnp.bfloat16)
        .reshape(samples_dev, lat_len, 2, owned, C)
    )
    first_grad = jnp.stack(
        [
            outer_sum(act_real, pre_grad_real) + outer_sum(act_imag, pre_grad_imag),
            outer_sum(act_real, pre_grad_imag) - outer_sum(act_imag, pre_grad_real),
        ]
    ).reshape(2, C, BS)
    hid_real = hidden[:, :, 0]
    hid_imag = hidden[:, :, 1]
    second_grad = jnp.stack(
        [
            outer_sum(hid_real, out_real) + outer_sum(hid_imag, out_imag),
            outer_sum(hid_real, out_imag) - outer_sum(hid_imag, out_real),
        ]
    ).reshape(2, C, BS)
    bias_first = jnp.sum(grad_pre, axis=(0, 1, 3), dtype=jnp.float32).reshape(2, C)
    bias_second = jnp.sum(grad_out, axis=(0, 1, 3), dtype=jnp.float32).reshape(2, C)
    local_terms = (first_grad, second_grad, bias_first, bias_second)
    summed = lax.psum(
        (local_terms[0], local_terms[1], local_terms[2], local_terms[3]), ("dp", "space")
    )
    share_rows = C // lax.axis_size("dp")
    row_start = lax.axis_index("dp") * share_rows

    def take_share(array):
        return lax.dynamic_slice_in_dim(array, row_start, share_rows, 1)

    totals = jax.tree.map(take_share, summed)
    grad_norm = 1.0 / math.sqrt(samples_dev * lax.axis_size("dp") * lat_len * kept)
    grad_lat = jnp.einsum(
        "mqhp,smqjc->shpjc", lat_table, grad_spec, preferred_element_type=jnp.float32
    ).astype(jnp.bfloat16)
    returned = lax.all_to_all(grad_lat, "space", split_axis=1, concat_axis=3, tiled=True)
    grad_field = (
        jnp.einsum("wpk,shpkc->shwc", lon_table, returned, preferred_element_type=jnp.float32)
        * ortho_scale
    ).astype(jnp.bfloat16)
    return (
        grad_field,
        totals[0] * grad_norm,
        totals[1] * grad_norm,
        totals[2] * grad_norm,
        totals[3] * grad_norm,
    )


def solution(mesh):
    groups, parts = mesh.shape["dp"], mesh.shape["space"]

    def per_device(*arrays):
        activations, lon_keep = arrays[0], arrays[5]
        fits = (
            parts == BLOCKS
            and 2 * groups == BLOCKS
            and activations.shape[:2] == (1, 2)
            and lon_keep.shape[0] == parts
        )
        return by_blocks(*arrays) if fits else by_frequencies(*arrays)

    return jax.shard_map(
        per_device,
        mesh=mesh,
        in_specs=(
            P("dp", "space", None, None),
            P("dp", "space", None, None),
            P(),
            P(),
            P(),
            P(),
            P("dp", None, None, "space", None),
            P("dp", None, None, "space", None),
        ),
        out_specs=(
            P("dp", "space", None, None),
            P(None, "dp", None),
            P(None, "dp", None),
            P(None, "dp"),
            P(None, "dp"),
        ),
        check_vma=False,
    )
```

```python
import functools
import math

import jax
import jax.numpy as jnp
import numpy as np
from jax import lax
from jax.experimental import pallas as pl
from jax.experimental.pallas import tpu as pltpu
from jax.sharding import PartitionSpec as P

C = 768
BLOCKS = 8
LON = 180
BS = 96

BF = jnp.bfloat16
F32 = jnp.float32
LANES = 128
THIRD = LANES - BS
VMEM_LIMIT = 32 * 1024 * 1024


def shift_of(group):
    return 2 * (group % 2) + group // 2


def block_of(group, device):
    lane = 2 * (device // 4) + device % 2
    return 2 * ((lane + shift_of(group)) % 4) + (device // 2) % 2


def owner_of(group, block):
    lane = (block // 2 + 4 - shift_of(group)) % 4
    return 4 * (lane // 2) + 2 * (block % 2) + lane % 2


def latitude_matrix(lat_len, kept):
    index = np.arange(lat_len)
    angle = ((index[:, None] * index[None, :]) % lat_len).astype(np.float32) * np.float32(
        2.0 * math.pi / lat_len
    )
    cosine, sine = np.cos(angle), np.sin(angle)
    table = np.stack([np.stack([cosine, sine], -1), np.stack([-sine, cosine], -1)], 1)
    full = np.einsum("mphq,jk->pjmhqk", table, np.eye(kept, dtype=np.float32))
    return full.reshape(2 * kept * lat_len, 2 * kept * lat_len)


def dot(lhs, rhs, lhs_axis, rhs_axis):
    return lax.dot_general(
        lhs, rhs, (((lhs_axis,), (rhs_axis,)), ((), ())), preferred_element_type=F32
    )


def fold(array):
    rows = array.shape[0] // 4
    beside = [array[3 * rows :, g * THIRD : (g + 1) * THIRD] for g in range(3)]
    return jnp.concatenate([array[: 3 * rows], jnp.concatenate(beside, axis=0)], axis=1)


def unfold(array):
    rows = array.shape[0] // 3
    beside = [array[g * rows : (g + 1) * rows, BS:] for g in range(3)]
    return jnp.concatenate([array[:, :BS], jnp.concatenate(beside, axis=1)], axis=0)


def window_of(block):
    tile = jnp.minimum(block * BS // LANES, C // LANES - 2)
    return pl.multiple_of(tile * LANES, LANES), block * BS - tile * LANES


def forward_lon_kernel(
    keep_hbm,
    act_hbm,
    cot_hbm,
    relu_hbm,
    shrink_hbm,
    *refs,
):
    weights_hbm, matrices_hbm, refs = refs[:3], refs[3:5], refs[5:]
    out, table_out, *fetched, field, masks, keep, sems = refs
    group, device = lax.axis_index("dp"), lax.axis_index("space")
    start, _ = window_of(block_of(group, device))
    kept = keep.shape[0]
    rows = act_hbm.shape[1]
    modes = relu_hbm.shape[0]
    tiles = C // LANES
    columns = [slice(k * LANES, (k + 1) * LANES) for k in range(tiles)]
    keep_copy = pltpu.make_async_copy(keep_hbm, keep, sems.at[0])
    keep_copy.start()
    mask_copies, field_copies = [], []
    for t, source in enumerate((relu_hbm, shrink_hbm)):
        for p in range(2):
            for k in range(tiles):
                copy = pltpu.make_async_copy(
                    source.at[:, p, :, columns[k]],
                    masks.at[t, p, k],
                    sems.at[1 + (2 * t + p) * tiles + k],
                )
                copy.start()
                mask_copies.append(copy)
    for t, source in enumerate((act_hbm, cot_hbm)):
        for k in range(tiles):
            copy = pltpu.make_async_copy(
                source.at[:, :, columns[k]], field.at[t, k], sems.at[1 + (4 + t) * tiles + k]
            )
            copy.start()
            field_copies.append(copy)
    sources = [
        source.at[(slice(None),) * (len(source.shape) - 1) + (pl.ds(start, 2 * LANES),)]
        for source in weights_hbm
    ] + list(matrices_hbm)
    other_copies = []
    for i, (source, target) in enumerate(zip(sources, fetched)):
        copy = pltpu.make_async_copy(source, target, sems.at[1 + 6 * tiles + i])
        copy.start()
        other_copies.append(copy)

    keep_copy.wait()
    shape = (rows * 2 * kept, LON * rows)
    line = lax.broadcasted_iota(jnp.int32, shape, 0)
    column = lax.broadcasted_iota(jnp.int32, shape, 1)
    frequency = jnp.zeros(shape, jnp.int32)
    for j in range(kept):
        frequency = jnp.where(line % kept == j, keep[j], frequency)
    turn = jnp.where((line // kept) % 2 == 1, LON // 4, 0)
    phase = ((column // rows) * frequency + turn) % LON
    table = jnp.cos(phase.astype(F32) * (2.0 * math.pi / LON))
    wide_table = jnp.where(line // (2 * kept) == column % rows, table, 0.0)
    table = wide_table.astype(BF)
    table_out[...] = wide_table.T.astype(BF)

    own = keep[device]
    scale = jnp.where((own == 0) | (2 * own == LON), 1.0, 2.0)
    for copy in mask_copies:
        copy.wait()

    def gate(t, value):
        return jnp.concatenate(
            [
                jnp.concatenate(
                    [
                        jnp.where(masks.at[t, p, k].reshape(modes, LANES)[...] > 0, value, 0.0)
                        for k in range(tiles)
                    ],
                    axis=1,
                )
                for p in range(2)
            ],
            axis=0,
        ).astype(BF)

    passed = gate(0, 1.0)
    scaled = gate(1, scale)
    per = table.shape[0]
    owners = [owner_of(group, b) for b in range(BLOCKS)]
    for b in range(BLOCKS):
        out[owners[b], 2 * per :, 0:BS] = passed[:, b * BS : (b + 1) * BS]
        beside = [scaled[:, b * BS + g * THIRD : b * BS + (g + 1) * THIRD] for g in range(3)]
        out[owners[b], :, BS:] = jnp.concatenate(beside, axis=0)

    for t in range(2):
        for copy in field_copies[t * tiles : (t + 1) * tiles]:
            copy.wait()
        wide = jnp.concatenate(
            [
                field[t, k].reshape(LON * rows, LANES) for k in range(tiles)
            ],
            axis=1,
        )
        lines = dot(table, wide, 1, 0).astype(BF)
        for b in range(BLOCKS):
            out[owners[b], t * per : (t + 1) * per, 0:BS] = lines[:, b * BS : (b + 1) * BS]
    for copy in other_copies:
        copy.wait()


def block_adjoint(operand, matrix):
    half = operand.shape[0] // 2
    real = dot(operand, matrix[0], 1, 0)
    imag = dot(operand, matrix[1], 1, 0)
    return jnp.concatenate([real[:half] + imag[half:], real[half:] - imag[:half]], axis=0)


def spectral_kernel(
    pieces, first_wide, second_wide, bias_wide, lat, terms, grad_pre_out, first_out, *, ortho_scale, rows, kept
):
    device = lax.axis_index("space")
    _, offset = window_of(block_of(lax.axis_index("dp"), device))
    parts = pieces.shape[0]
    per = rows * 2 * kept
    half = parts * per // 2
    modes = half // kept
    chosen = lax.broadcasted_iota(jnp.int32, (2 * LANES, BS), 0) == (
        lax.broadcasted_iota(jnp.int32, (2 * LANES, BS), 1) + offset
    )
    chosen = jnp.where(chosen, 1.0, 0.0).astype(BF)
    first = [dot(first_wide[p], chosen, 1, 0).astype(BF) for p in range(2)]
    second = [dot(second_wide[p], chosen, 1, 0).astype(BF) for p in range(2)]
    bias = pltpu.roll(bias_wide[...], (2 * LANES - offset) % (2 * LANES), 1)
    opened = [unfold(pieces[i]) for i in range(parts)]

    def spectrum(t):
        stacked = jnp.concatenate([piece[t * per : (t + 1) * per] for piece in opened], axis=0)
        return (dot(lat[...], stacked, 1, 0) * ortho_scale).astype(BF)

    def mask(k):
        start = 2 * per + k * 2 * modes
        return jnp.concatenate(
            [
                opened[j][start + p * modes : start + (p + 1) * modes]
                for p in range(2)
                for j in range(kept)
            ],
            axis=0,
        ).astype(F32)

    spec_act = spectrum(0)
    spec_cot = spectrum(1)
    passed = mask(0) > 0.0
    weight = mask(1)
    grad_out = jnp.where(weight > 0.0, weight * spec_cot.astype(F32), 0.0).astype(BF)

    by_real = dot(spec_act, first[0], 1, 1)
    by_imag = dot(spec_act, first[1], 1, 1)
    pre = jnp.concatenate(
        [
            by_real[:half] - by_imag[half:] + bias[0:1, :BS],
            by_imag[:half] + by_real[half:] + bias[1:2, :BS],
        ],
        axis=0,
    )
    hidden = jnp.where(passed, pre, 0.0).astype(BF)

    grad_pre = jnp.where(passed, block_adjoint(grad_out, second), 0.0).astype(BF)
    grad_pre_out[...] = grad_pre
    for p in range(2):
        first_out[p] = first[p]

    def turned(array):
        return jnp.concatenate([array[half:], -array[:half]], axis=0)

    at = 3 * BS // 4
    blank = jnp.zeros((terms.shape[2] - at - 1, LANES), F32)
    for a, (left, right) in enumerate(((spec_act, grad_pre), (hidden, grad_out))):
        slot = (a + device) % 2
        wide = right.astype(F32)
        for p, other in enumerate((right, turned(right))):
            summed = jnp.sum(wide[p * half : (p + 1) * half], axis=0, keepdims=True)
            summed = jnp.concatenate([summed, jnp.zeros((1, THIRD), F32)], axis=1)
            terms[slot, p] = jnp.concatenate(
                [fold(dot(left, other, 0, 0)), summed, blank], axis=0
            ).astype(BF)


def grad_lat_kernel(grad_pre, first, lat_t, grad_lat):
    grad_spec = block_adjoint(grad_pre[...], first).astype(BF)
    lines = dot(lat_t[...], grad_spec, 1, 0)
    lines = jnp.concatenate([lines, jnp.zeros((lines.shape[0], THIRD), F32)], axis=1).astype(BF)
    grad_lat[...] = lines.reshape(grad_lat.shape)


def inverse_lon_kernel(table, pieces, field, *, ortho_scale):
    rows = field.shape[1]
    per = table.shape[1]
    group = lax.axis_index("dp")
    lines = jnp.concatenate(
        [pieces[owner_of(group, b), 0:per, 0:BS] for b in range(BLOCKS)], axis=1
    )
    wide = (dot(table[...], lines, 1, 0) * ortho_scale).astype(BF)
    for k in range(C // LANES):
        lanes = slice(k * LANES, (k + 1) * LANES)
        field[:, :, lanes] = wide[:, lanes].reshape(LON, rows, LANES)


def gathered_kernel(pieces, others, first, second, bias_first, bias_second, *, grad_norm):
    core = lax.axis_index("space") % 2
    per = pieces.shape[1] - others.shape[1]
    at = 3 * BS // 4
    for a, (target, vector) in enumerate(((first, bias_first), (second, bias_second))):
        for k in range(2):
            near, far = 2 * k + a, 4 + 2 * k + a
            own = pieces[near, per:, :].astype(F32) + pieces[far, per:, :].astype(F32)
            other = others[near].astype(F32) + others[far].astype(F32)
            for p in range(2):
                total = jnp.where(core == p, own, other) * grad_norm
                target[p, k * BS : (k + 1) * BS, :] = unfold(total[:at])
                vector[p : p + 1, k * BS : (k + 1) * BS] = total[at : at + 1, :BS]


def whole(memory=pltpu.VMEM):
    return pl.BlockSpec(memory_space=memory)


def by_blocks(
    activations, cotangent, w_first, w_second, b_first, lon_keep, relu_mask, shrink_mask
):
    groups = lax.axis_size("dp")
    parts = lax.axis_size("space")
    rows = activations.shape[1]
    lat_len = rows * parts
    kept = lon_keep.shape[0]
    ortho_scale = 1.0 / math.sqrt(lat_len * LON)
    grad_norm = 1.0 / math.sqrt(groups * lat_len * kept)
    params = pltpu.CompilerParams(vmem_limit_bytes=VMEM_LIMIT)
    tiles = C // LANES
    per = rows * 2 * kept
    height = (2 * per + 4 * lat_len) * 3 // 4
    term_rows = 3 * BS // 4 + 8

    lat = latitude_matrix(lat_len, kept)
    sent, table, *fetched = pl.pallas_call(
        forward_lon_kernel,
        out_shape=(
            pltpu.VMEM((parts, height, LANES), BF),
            pltpu.VMEM((LON * rows, per), BF),
            pltpu.VMEM((2, BS, 2 * LANES), BF),
            pltpu.VMEM((2, BS, 2 * LANES), BF),
            pltpu.VMEM((2, 2 * LANES), F32),
            pltpu.VMEM(lat.shape, BF),
            pltpu.VMEM(lat.shape, BF),
        ),
        in_specs=[whole(pl.ANY)] * 10,
        out_specs=(whole(),) * 7,
        scratch_shapes=[
            pltpu.VMEM((2, tiles, LON, rows, LANES), BF),
            pltpu.VMEM((2, 2, tiles, lat_len, 1, LANES), jnp.int32),
            pltpu.SMEM((kept,), jnp.int32),
            pltpu.SemaphoreType.DMA((6 + 6 * tiles,)),
        ],
        compiler_params=params,
        name="forward_lon",
    )(
        *(
            pltpu.with_memory_space_constraint(array, pltpu.HBM)
            for array in (
                lon_keep,
                activations[0].transpose(1, 0, 2),
                cotangent[0].transpose(1, 0, 2),
                relu_mask[0],
                shrink_mask[0],
                w_first.transpose(0, 2, 1),
                w_second.transpose(0, 2, 1),
                b_first,
                jnp.asarray(lat, BF),
                jnp.asarray(lat.T, BF),
            )
        )
    )
    pieces = lax.all_to_all(sent, "space", 0, 0, tiled=True)

    *fetched, lat_t = fetched
    terms, grad_pre, first_block = pl.pallas_call(
        functools.partial(spectral_kernel, ortho_scale=ortho_scale, rows=rows, kept=kept),
        out_shape=(
            jax.ShapeDtypeStruct((2, 2, term_rows, LANES), BF),
            pltpu.VMEM((lat.shape[0], BS), BF),
            pltpu.VMEM((2, BS, BS), BF),
        ),
        in_specs=[whole()] * 5,
        out_specs=(whole(),) * 3,
        compiler_params=params,
        name="spectral",
    )(pieces, *fetched)
    grad_lat = pl.pallas_call(
        grad_lat_kernel,
        out_shape=jax.ShapeDtypeStruct((parts, per, LANES), BF),
        in_specs=[whole()] * 3,
        out_specs=whole(),
        compiler_params=params,
        cost_estimate=pl.CostEstimate(
            flops=2 * lat.size * BS * 3, bytes_accessed=4 * lat.size, transcendentals=0
        ),
        name="grad_lat",
    )(grad_pre, first_block, lat_t)

    arrived = lax.ppermute(
        terms,
        ("dp", "space"),
        [
            (g * parts + c, (block_of(g, c) // 2) * parts + c)
            for g in range(groups)
            for c in range(parts)
        ],
    )
    other = lax.ppermute(arrived[1], "space", [(c, c ^ 1) for c in range(parts)])
    share = (arrived[0].astype(F32) + other.astype(F32)).astype(BF)
    share = jnp.broadcast_to(share[None], (parts // 2,) + share.shape)
    returned = lax.all_to_all(
        jnp.concatenate([grad_lat, share.reshape(parts, term_rows, LANES)], axis=1),
        "space",
        0,
        0,
        tiled=True,
    )
    others = lax.ppermute(returned[:, per:, :], "space", [(c, c ^ 1) for c in range(parts)])

    keep_rows = C // groups
    field = pl.pallas_call(
        functools.partial(inverse_lon_kernel, ortho_scale=ortho_scale),
        out_shape=jax.ShapeDtypeStruct((LON, rows, C), BF),
        in_specs=[whole(), whole()],
        out_specs=whole(),
        compiler_params=params,
        cost_estimate=pl.CostEstimate(
            flops=2 * per * LON * rows * C, bytes_accessed=8 * LON * rows * C, transcendentals=0
        ),
        name="inverse_lon",
    )(table, returned)
    first, second, bias_first, bias_second = pl.pallas_call(
        functools.partial(gathered_kernel, grad_norm=grad_norm),
        out_shape=(
            jax.ShapeDtypeStruct((2, keep_rows, BS), F32),
            jax.ShapeDtypeStruct((2, keep_rows, BS), F32),
            jax.ShapeDtypeStruct((2, keep_rows), F32),
            jax.ShapeDtypeStruct((2, keep_rows), F32),
        ),
        in_specs=[whole(), whole()],
        out_specs=(whole(),) * 4,
        compiler_params=params,
        name="gathered",
    )(returned, others)
    return field.transpose(1, 0, 2)[None], first, second, bias_first, bias_second


def build_tables(lon_keep, lat_len, lon_len):
    columns = jnp.arange(lon_len, dtype=jnp.int32)
    lon_phase = columns[:, None] * lon_keep[None, :] % lon_len
    lon_angle = lon_phase.astype(jnp.float32) * (2.0 * math.pi / lon_len)
    lon_table = jnp.stack([jnp.cos(lon_angle), -jnp.sin(lon_angle)], axis=1).astype(jnp.bfloat16)
    latitudes = jnp.arange(lat_len, dtype=jnp.int32)
    lat_phase = latitudes[:, None] * latitudes[None, :] % lat_len
    lat_angle = lat_phase.astype(jnp.float32) * (2.0 * math.pi / lat_len)
    cosine = jnp.cos(lat_angle)
    sine_part = jnp.sin(lat_angle)
    lat_table = jnp.stack(
        [jnp.stack([cosine, sine_part], axis=-1), jnp.stack([-sine_part, cosine], axis=-1)], axis=1
    ).astype(jnp.bfloat16)
    return (lon_table, lat_table)


def apply_blocks(operand, matrix):
    return jnp.einsum("smjbc,bcd->smjbd", operand, matrix, preferred_element_type=jnp.float32)


def adjoint(operand, matrix):
    return jnp.einsum("smjbd,bcd->smjbc", operand, matrix, preferred_element_type=jnp.float32)


def outer_sum(operand, other):
    return jnp.einsum("smjbc,smjbd->bcd", operand, other, preferred_element_type=jnp.float32)


def by_frequencies(
    activations, cotangent, w_first, w_second, b_first, lon_keep, relu_mask, shrink_mask
):
    parts = lax.axis_size("space")
    samples_dev = activations.shape[0]
    lat_len = activations.shape[1] * parts
    kept = lon_keep.shape[0]
    owned = kept // parts
    lon_table, lat_table = build_tables(lon_keep, lat_len, LON)
    ortho_scale = 1.0 / math.sqrt(lat_len * LON)
    act_lon = jnp.einsum(
        "shwc,wpk->shpkc", activations, lon_table, preferred_element_type=jnp.float32
    ).astype(jnp.bfloat16)
    cot_lon = jnp.einsum(
        "shwc,wpk->shpkc", cotangent, lon_table, preferred_element_type=jnp.float32
    ).astype(jnp.bfloat16)
    act_modes, cot_modes = (
        lax.all_to_all(act_lon, "space", split_axis=3, concat_axis=1, tiled=True),
        lax.all_to_all(cot_lon, "space", split_axis=3, concat_axis=1, tiled=True),
    )

    def latitude(modes):
        summed = jnp.einsum(
            "mphq,shqjc->smpjc", lat_table, modes, preferred_element_type=jnp.float32
        )
        return (summed * ortho_scale).astype(jnp.bfloat16)

    block_shape = (samples_dev, lat_len, 2, owned, BLOCKS, BS)
    spec_act = latitude(act_modes).reshape(block_shape)
    spec_cot = latitude(cot_modes)
    own_keep = lax.dynamic_slice_in_dim(lon_keep, lax.axis_index("space") * owned, owned)
    doubled = jnp.where((own_keep == 0) | (2 * own_keep == LON), 1.0, 2.0).astype(jnp.float32)
    grad_out = (
        jnp.where(
            shrink_mask > 0, doubled[None, None, None, :, None] * spec_cot.astype(jnp.float32), 0.0
        )
        .astype(jnp.bfloat16)
        .reshape(block_shape)
    )
    relu_gate = relu_mask.reshape(block_shape) > 0
    first_blocks = w_first.reshape(2, BLOCKS, BS, BS)
    second_blocks = w_second.reshape(2, BLOCKS, BS, BS)
    bias_blocks = b_first.reshape(2, BLOCKS, BS)
    act_real = spec_act[:, :, 0]
    act_imag = spec_act[:, :, 1]
    pre_real = (
        apply_blocks(act_real, first_blocks[0])
        - apply_blocks(act_imag, first_blocks[1])
        + bias_blocks[0]
    )
    pre_imag = (
        apply_blocks(act_real, first_blocks[1])
        + apply_blocks(act_imag, first_blocks[0])
        + bias_blocks[1]
    )
    hidden = jnp.where(relu_gate, jnp.stack([pre_real, pre_imag], axis=2), 0.0).astype(jnp.bfloat16)
    out_real = grad_out[:, :, 0]
    out_imag = grad_out[:, :, 1]
    hidden_real = adjoint(out_real, second_blocks[0]) + adjoint(out_imag, second_blocks[1])
    hidden_imag = -adjoint(out_real, second_blocks[1]) + adjoint(out_imag, second_blocks[0])
    grad_pre = jnp.where(relu_gate, jnp.stack([hidden_real, hidden_imag], axis=2), 0.0).astype(
        jnp.bfloat16
    )
    pre_grad_real = grad_pre[:, :, 0]
    pre_grad_imag = grad_pre[:, :, 1]
    spec_real = adjoint(pre_grad_real, first_blocks[0]) + adjoint(pre_grad_imag, first_blocks[1])
    spec_imag = -adjoint(pre_grad_real, first_blocks[1]) + adjoint(pre_grad_imag, first_blocks[0])
    grad_spec = (
        jnp.stack([spec_real, spec_imag], axis=2)
        .astype(jnp.bfloat16)
        .reshape(samples_dev, lat_len, 2, owned, C)
    )
    first_grad = jnp.stack(
        [
            outer_sum(act_real, pre_grad_real) + outer_sum(act_imag, pre_grad_imag),
            outer_sum(act_real, pre_grad_imag) - outer_sum(act_imag, pre_grad_real),
        ]
    ).reshape(2, C, BS)
    hid_real = hidden[:, :, 0]
    hid_imag = hidden[:, :, 1]
    second_grad = jnp.stack(
        [
            outer_sum(hid_real, out_real) + outer_sum(hid_imag, out_imag),
            outer_sum(hid_real, out_imag) - outer_sum(hid_imag, out_real),
        ]
    ).reshape(2, C, BS)
    bias_first = jnp.sum(grad_pre, axis=(0, 1, 3), dtype=jnp.float32).reshape(2, C)
    bias_second = jnp.sum(grad_out, axis=(0, 1, 3), dtype=jnp.float32).reshape(2, C)
    local_terms = (first_grad, second_grad, bias_first, bias_second)
    summed = lax.psum(
        (local_terms[0], local_terms[1], local_terms[2], local_terms[3]), ("dp", "space")
    )
    share_rows = C // lax.axis_size("dp")
    row_start = lax.axis_index("dp") * share_rows

    def take_share(array):
        return lax.dynamic_slice_in_dim(array, row_start, share_rows, 1)

    totals = jax.tree.map(take_share, summed)
    grad_norm = 1.0 / math.sqrt(samples_dev * lax.axis_size("dp") * lat_len * kept)
    grad_lat = jnp.einsum(
        "mqhp,smqjc->shpjc", lat_table, grad_spec, preferred_element_type=jnp.float32
    ).astype(jnp.bfloat16)
    returned = lax.all_to_all(grad_lat, "space", split_axis=1, concat_axis=3, tiled=True)
    grad_field = (
        jnp.einsum("wpk,shpkc->shwc", lon_table, returned, preferred_element_type=jnp.float32)
        * ortho_scale
    ).astype(jnp.bfloat16)
    return (
        grad_field,
        totals[0] * grad_norm,
        totals[1] * grad_norm,
        totals[2] * grad_norm,
        totals[3] * grad_norm,
    )


def solution(mesh):
    groups, parts = mesh.shape["dp"], mesh.shape["space"]

    def per_device(*arrays):
        activations, lon_keep = arrays[0], arrays[5]
        fits = (
            parts == BLOCKS
            and 2 * groups == BLOCKS
            and activations.shape[:2] == (1, 2)
            and lon_keep.shape[0] == parts
        )
        return by_blocks(*arrays) if fits else by_frequencies(*arrays)

    return jax.shard_map(
        per_device,
        mesh=mesh,
        in_specs=(
            P("dp", "space", None, None),
            P("dp", "space", None, None),
            P(),
            P(),
            P(),
            P(),
            P("dp", None, None, "space", None),
            P("dp", None, None, "space", None),
        ),
        out_specs=(
            P("dp", "space", None, None),
            P(None, "dp", None),
            P(None, "dp", None),
            P(None, "dp"),
            P(None, "dp"),
        ),
        check_vma=False,
    )
```

```python
import functools
import math

import jax
import jax.numpy as jnp
import numpy as np
from jax import lax
from jax.experimental import pallas as pl
from jax.experimental.pallas import tpu as pltpu
from jax.sharding import PartitionSpec as P

C = 768
BLOCKS = 8
LON = 180
BS = 96

BF = jnp.bfloat16
F32 = jnp.float32
LANES = 128
THIRD = LANES - BS
LON_CUT = 96
VMEM_LIMIT = 32 * 1024 * 1024


def shift_of(group):
    return 2 * (group % 2) + group // 2


def block_of(group, device):
    lane = 2 * (device // 4) + device % 2
    return 2 * ((lane + shift_of(group)) % 4) + (device // 2) % 2


def owner_of(group, block):
    lane = (block // 2 + 4 - shift_of(group)) % 4
    return 4 * (lane // 2) + 2 * (block % 2) + lane % 2


def latitude_matrix(lat_len, kept):
    index = np.arange(lat_len)
    angle = ((index[:, None] * index[None, :]) % lat_len).astype(np.float32) * np.float32(
        2.0 * math.pi / lat_len
    )
    cosine, sine = np.cos(angle), np.sin(angle)
    table = np.stack([np.stack([cosine, sine], -1), np.stack([-sine, cosine], -1)], 1)
    full = np.einsum("mphq,jk->pjmhqk", table, np.eye(kept, dtype=np.float32))
    return full.reshape(2 * kept * lat_len, 2 * kept * lat_len)


def dot(lhs, rhs, lhs_axis, rhs_axis):
    return lax.dot_general(
        lhs, rhs, (((lhs_axis,), (rhs_axis,)), ((), ())), preferred_element_type=F32
    )


def fold(array):
    rows = array.shape[0] // 4
    beside = [array[3 * rows :, g * THIRD : (g + 1) * THIRD] for g in range(3)]
    return jnp.concatenate([array[: 3 * rows], jnp.concatenate(beside, axis=0)], axis=1)


def unfold(array):
    rows = array.shape[0] // 3
    beside = [array[g * rows : (g + 1) * rows, BS:] for g in range(3)]
    return jnp.concatenate([array[:, :BS], jnp.concatenate(beside, axis=1)], axis=0)


def window_of(block):
    tile = jnp.minimum(block * BS // LANES, C // LANES - 2)
    return pl.multiple_of(tile * LANES, LANES), block * BS - tile * LANES


def forward_lon_kernel(
    keep_hbm,
    act_hbm,
    cot_hbm,
    relu_hbm,
    shrink_hbm,
    *refs,
):
    weights_hbm, matrices_hbm, refs = refs[:3], refs[3:5], refs[5:]
    out, table_out, *fetched, field, masks, keep, sems = refs
    group, device = lax.axis_index("dp"), lax.axis_index("space")
    start, _ = window_of(block_of(group, device))
    kept = keep.shape[0]
    rows = act_hbm.shape[1]
    modes = relu_hbm.shape[0]
    tiles = C // LANES
    columns = [slice(k * LANES, (k + 1) * LANES) for k in range(tiles)]
    keep_copy = pltpu.make_async_copy(keep_hbm, keep, sems.at[0])
    keep_copy.start()
    mask_copies, field_copies = [], []
    for t, source in enumerate((relu_hbm, shrink_hbm)):
        for p in range(2):
            for k in range(tiles):
                copy = pltpu.make_async_copy(
                    source.at[:, p, :, columns[k]],
                    masks.at[t, p, k],
                    sems.at[1 + (2 * t + p) * tiles + k],
                )
                copy.start()
                mask_copies.append(copy)
    for t, source in enumerate((act_hbm, cot_hbm)):
        for k in range(tiles):
            copy = pltpu.make_async_copy(
                source.at[:, :, columns[k]], field.at[t, k], sems.at[1 + (4 + t) * tiles + k]
            )
            copy.start()
            field_copies.append(copy)
    sources = [
        source.at[(slice(None),) * (len(source.shape) - 1) + (pl.ds(start, 2 * LANES),)]
        for source in weights_hbm
    ] + list(matrices_hbm)
    other_copies = []
    for i, (source, target) in enumerate(zip(sources, fetched)):
        copy = pltpu.make_async_copy(source, target, sems.at[1 + 6 * tiles + i])
        copy.start()
        other_copies.append(copy)

    keep_copy.wait()
    shape = (rows * 2 * kept, LON * rows)
    line = lax.broadcasted_iota(jnp.int32, shape, 0)
    column = lax.broadcasted_iota(jnp.int32, shape, 1)
    frequency = jnp.zeros(shape, jnp.int32)
    for j in range(kept):
        frequency = jnp.where(line % kept == j, keep[j], frequency)
    turn = jnp.where((line // kept) % 2 == 1, LON // 4, 0)
    phase = ((column // rows) * frequency + turn) % LON
    table = jnp.cos(phase.astype(F32) * (2.0 * math.pi / LON))
    wide_table = jnp.where(line // (2 * kept) == column % rows, table, 0.0)
    table = wide_table.astype(BF)
    table_out[...] = wide_table.T.astype(BF)

    own = keep[device]
    scale = jnp.where((own == 0) | (2 * own == LON), 1.0, 2.0)
    for copy in mask_copies:
        copy.wait()

    def gate(t, value):
        return jnp.concatenate(
            [
                jnp.concatenate(
                    [
                        jnp.where(masks.at[t, p, k].reshape(modes, LANES)[...] > 0, value, 0.0)
                        for k in range(tiles)
                    ],
                    axis=1,
                )
                for p in range(2)
            ],
            axis=0,
        ).astype(BF)

    passed = gate(0, 1.0)
    scaled = gate(1, scale)
    per = table.shape[0]
    owners = [owner_of(group, b) for b in range(BLOCKS)]
    for b in range(BLOCKS):
        out[owners[b], 2 * per :, 0:BS] = passed[:, b * BS : (b + 1) * BS]
        beside = [scaled[:, b * BS + g * THIRD : b * BS + (g + 1) * THIRD] for g in range(3)]
        out[owners[b], :, BS:] = jnp.concatenate(beside, axis=0)

    for t in range(2):
        for copy in field_copies[t * tiles : (t + 1) * tiles]:
            copy.wait()
        wide = jnp.concatenate(
            [
                field[t, k].reshape(LON * rows, LANES) for k in range(tiles)
            ],
            axis=1,
        )
        lines = dot(table, wide, 1, 0).astype(BF)
        for b in range(BLOCKS):
            out[owners[b], t * per : (t + 1) * per, 0:BS] = lines[:, b * BS : (b + 1) * BS]
    for copy in other_copies:
        copy.wait()


def block_adjoint(operand, matrix):
    half = operand.shape[0] // 2
    both = dot(operand, matrix, 1, 0)
    real, imag = both[:, :LANES], both[:, LANES:]
    return jnp.concatenate([real[:half] + imag[half:], real[half:] - imag[:half]], axis=0)


def spectral_kernel(
    pieces,
    first_wide,
    second_wide,
    bias_wide,
    lat,
    terms,
    grad_pre_out,
    first_out,
    *,
    ortho_scale,
    rows,
    kept,
):
    device = lax.axis_index("space")
    _, offset = window_of(block_of(lax.axis_index("dp"), device))
    parts = pieces.shape[0]
    per = rows * 2 * kept
    half = parts * per // 2
    modes = half // kept
    spare = jnp.zeros((LANES - BS, LANES), F32)
    place = lax.broadcasted_iota(jnp.int32, (2 * LANES, LANES), 1)
    chosen = (lax.broadcasted_iota(jnp.int32, (2 * LANES, LANES), 0) == place + offset) & (
        place < BS
    )
    chosen = jnp.where(chosen, 1.0, 0.0).astype(BF)

    def matrices(wide):
        found = dot(wide[...].reshape(2 * BS, 2 * LANES), chosen, 1, 0)
        return [jnp.concatenate([found[p * BS : (p + 1) * BS], spare], axis=0) for p in range(2)]

    first, second = matrices(first_wide), matrices(second_wide)
    across = jnp.concatenate(first, axis=0).astype(BF)
    first_out[...] = jnp.concatenate(first, axis=1).astype(BF)
    second = jnp.concatenate(second, axis=1).astype(BF)
    bias = pltpu.roll(bias_wide[...], (2 * LANES - offset) % (2 * LANES), 1)[:, :LANES]
    bias = jnp.where(lax.broadcasted_iota(jnp.int32, bias.shape, 1) < BS, bias, 0.0)

    def mode_rows(found):
        return jnp.concatenate(
            [found[j][p * modes : (p + 1) * modes] for p in range(2) for j in range(kept)], axis=0
        ).astype(F32)

    group = pieces.shape[1] // 3
    passed = mode_rows([pieces[j, 2 * per :, :] for j in range(kept)]) > 0.0
    weight = mode_rows(
        [
            jnp.concatenate(
                [pieces[j, g * group : (g + 1) * group, BS:] for g in range(3)]
                + [jnp.zeros((group, THIRD), BF)],
                axis=1,
            )
            for j in range(kept)
        ]
    )

    stacked = jnp.concatenate(
        [
            jnp.concatenate([pieces[i, t * per : (t + 1) * per, :] for i in range(parts)], axis=0)
            for t in range(2)
        ],
        axis=1,
    )
    spectra = (dot(lat[...], stacked, 1, 0) * ortho_scale).astype(BF)
    spec_act, spec_cot = spectra[:, :LANES], spectra[:, LANES:]
    grad_out = jnp.where(weight > 0.0, weight * spec_cot.astype(F32), 0.0).astype(BF)
    grad_pre = jnp.where(passed, block_adjoint(grad_out, second), 0.0).astype(BF)
    grad_pre_out[...] = grad_pre

    both = dot(spec_act, across, 1, 1)
    by_real, by_imag = both[:, :LANES], both[:, LANES:]
    pre = jnp.concatenate(
        [
            by_real[:half] - by_imag[half:] + bias[0:1],
            by_imag[:half] + by_real[half:] + bias[1:2],
        ],
        axis=0,
    )
    hidden = jnp.where(passed, pre, 0.0).astype(BF)

    at = 3 * BS // 4
    blank = jnp.zeros((terms.shape[2] - at - 1, LANES), F32)
    for a, (left, right) in enumerate(((spec_act, grad_pre), (hidden, grad_out))):
        slot = (a + device) % 2
        wide = right.astype(F32)
        turned = jnp.concatenate([right[half:], -right[:half]], axis=0)
        products = dot(left, jnp.concatenate([right, turned], axis=1), 0, 0)
        for p in range(2):
            summed = jnp.sum(wide[p * half : (p + 1) * half], axis=0, keepdims=True)
            terms[slot, p] = jnp.concatenate(
                [fold(products[:BS, p * LANES : p * LANES + BS]), summed, blank], axis=0
            ).astype(BF)


def grad_lat_kernel(grad_pre, first, lat_t, grad_lat):
    grad_spec = block_adjoint(grad_pre[...], first[...]).astype(BF)
    lines = dot(lat_t[...], grad_spec, 1, 0)
    per = lines.shape[0] // grad_lat.shape[0]
    for i in range(grad_lat.shape[0]):
        grad_lat[i] = fold(lines[i * per : (i + 1) * per, :BS]).astype(BF)


def inverse_lon_kernel(table, pieces, field_hbm, field, sems, *, ortho_scale):
    rows = field.shape[1]
    per = table.shape[1]
    group = lax.axis_index("dp")
    lines = jnp.concatenate(
        [unfold(pieces[owner_of(group, b), 0 : 3 * per // 4, :]) for b in range(BLOCKS)], axis=1
    )
    copies = []
    for i, (start, stop) in enumerate(((0, LON_CUT), (LON_CUT, LON))):
        wide = (dot(table[start * rows : stop * rows], lines, 1, 0) * ortho_scale).astype(BF)
        for k in range(C // LANES):
            lanes = slice(k * LANES, (k + 1) * LANES)
            field[start:stop, :, lanes] = wide[:, lanes].reshape(stop - start, rows, LANES)
        copy = pltpu.make_async_copy(
            field.at[start:stop], field_hbm.at[start:stop], sems.at[i]
        )
        copy.start()
        copies.append(copy)
    for copy in copies:
        copy.wait()


def gathered_kernel(pieces, others, first, second, bias_first, bias_second, *, grad_norm):
    core = lax.axis_index("space") % 2
    per = pieces.shape[1] - others.shape[1]
    at = 3 * BS // 4
    for a, (target, vector) in enumerate(((first, bias_first), (second, bias_second))):
        for k in range(2):
            near, far = 2 * k + a, 4 + 2 * k + a
            own = pieces[near, per:, :].astype(F32) + pieces[far, per:, :].astype(F32)
            other = others[near].astype(F32) + others[far].astype(F32)
            for p in range(2):
                total = jnp.where(core == p, own, other) * grad_norm
                target[p, k * BS : (k + 1) * BS, :] = unfold(total[:at])
                vector[p : p + 1, k * BS : (k + 1) * BS] = total[at : at + 1, :BS]


def whole(memory=pltpu.VMEM):
    return pl.BlockSpec(memory_space=memory)


def by_blocks(
    activations, cotangent, w_first, w_second, b_first, lon_keep, relu_mask, shrink_mask
):
    groups = lax.axis_size("dp")
    parts = lax.axis_size("space")
    rows = activations.shape[1]
    lat_len = rows * parts
    kept = lon_keep.shape[0]
    ortho_scale = 1.0 / math.sqrt(lat_len * LON)
    grad_norm = 1.0 / math.sqrt(groups * lat_len * kept)
    params = pltpu.CompilerParams(vmem_limit_bytes=VMEM_LIMIT)
    tiles = C // LANES
    per = rows * 2 * kept
    height = (2 * per + 4 * lat_len) * 3 // 4
    term_rows = 3 * BS // 4 + 8

    lat = latitude_matrix(lat_len, kept)
    sent, table, *fetched = pl.pallas_call(
        forward_lon_kernel,
        out_shape=(
            pltpu.VMEM((parts, height, LANES), BF),
            pltpu.VMEM((LON * rows, per), BF),
            pltpu.VMEM((2, BS, 2 * LANES), BF),
            pltpu.VMEM((2, BS, 2 * LANES), BF),
            pltpu.VMEM((2, 2 * LANES), F32),
            pltpu.VMEM(lat.shape, BF),
            pltpu.VMEM(lat.shape, BF),
        ),
        in_specs=[whole(pl.ANY)] * 10,
        out_specs=(whole(),) * 7,
        scratch_shapes=[
            pltpu.VMEM((2, tiles, LON, rows, LANES), BF),
            pltpu.VMEM((2, 2, tiles, lat_len, 1, LANES), jnp.int32),
            pltpu.SMEM((kept,), jnp.int32),
            pltpu.SemaphoreType.DMA((6 + 6 * tiles,)),
        ],
        compiler_params=params,
        name="forward_lon",
    )(
        *(
            pltpu.with_memory_space_constraint(array, pltpu.HBM)
            for array in (
                lon_keep,
                activations[0].transpose(1, 0, 2),
                cotangent[0].transpose(1, 0, 2),
                relu_mask[0],
                shrink_mask[0],
                w_first.transpose(0, 2, 1),
                w_second.transpose(0, 2, 1),
                b_first,
                jnp.asarray(lat, BF),
                jnp.asarray(lat.T, BF),
            )
        )
    )
    pieces = lax.all_to_all(sent, "space", 0, 0, tiled=True)

    *fetched, lat_t = fetched
    terms, grad_pre, first_block = pl.pallas_call(
        functools.partial(spectral_kernel, ortho_scale=ortho_scale, rows=rows, kept=kept),
        out_shape=(
            jax.ShapeDtypeStruct((2, 2, term_rows, LANES), BF),
            pltpu.VMEM((lat.shape[0], LANES), BF),
            pltpu.VMEM((LANES, 2 * LANES), BF),
        ),
        in_specs=[whole()] * 5,
        out_specs=(whole(),) * 3,
        compiler_params=params,
        name="spectral",
    )(pieces, *fetched)
    grad_lat = pl.pallas_call(
        grad_lat_kernel,
        out_shape=jax.ShapeDtypeStruct((parts, 3 * per // 4, LANES), BF),
        in_specs=[whole()] * 3,
        out_specs=whole(),
        compiler_params=params,
        cost_estimate=pl.CostEstimate(
            flops=2 * lat.size * BS * 3, bytes_accessed=4 * lat.size, transcendentals=0
        ),
        name="grad_lat",
    )(grad_pre, first_block, lat_t)

    arrived = lax.ppermute(
        terms,
        ("dp", "space"),
        [
            (g * parts + c, (block_of(g, c) // 2) * parts + c)
            for g in range(groups)
            for c in range(parts)
        ],
    )
    other = lax.ppermute(arrived[1], "space", [(c, c ^ 1) for c in range(parts)])
    share = (arrived[0].astype(F32) + other.astype(F32)).astype(BF)
    share = jnp.broadcast_to(share[None], (parts // 2,) + share.shape)
    returned = lax.all_to_all(
        jnp.concatenate([grad_lat, share.reshape(parts, term_rows, LANES)], axis=1),
        "space",
        0,
        0,
        tiled=True,
    )
    others = lax.ppermute(returned[:, 3 * per // 4 :, :], "space", [(c, c ^ 1) for c in range(parts)])

    keep_rows = C // groups
    field = pl.pallas_call(
        functools.partial(inverse_lon_kernel, ortho_scale=ortho_scale),
        out_shape=jax.ShapeDtypeStruct((LON, rows, C), BF),
        in_specs=[whole(), whole()],
        out_specs=whole(pl.ANY),
        scratch_shapes=[
            pltpu.VMEM((LON, rows, C), BF),
            pltpu.SemaphoreType.DMA((2,)),
        ],
        compiler_params=params,
        cost_estimate=pl.CostEstimate(
            flops=2 * per * LON * rows * C, bytes_accessed=8 * LON * rows * C, transcendentals=0
        ),
        name="inverse_lon",
    )(table, returned)
    first, second, bias_first, bias_second = pl.pallas_call(
        functools.partial(gathered_kernel, grad_norm=grad_norm),
        out_shape=(
            jax.ShapeDtypeStruct((2, keep_rows, BS), F32),
            jax.ShapeDtypeStruct((2, keep_rows, BS), F32),
            jax.ShapeDtypeStruct((2, keep_rows), F32),
            jax.ShapeDtypeStruct((2, keep_rows), F32),
        ),
        in_specs=[whole(), whole()],
        out_specs=(whole(),) * 4,
        compiler_params=params,
        name="gathered",
    )(returned, others)
    return field.transpose(1, 0, 2)[None], first, second, bias_first, bias_second


def build_tables(lon_keep, lat_len, lon_len):
    columns = jnp.arange(lon_len, dtype=jnp.int32)
    lon_phase = columns[:, None] * lon_keep[None, :] % lon_len
    lon_angle = lon_phase.astype(jnp.float32) * (2.0 * math.pi / lon_len)
    lon_table = jnp.stack([jnp.cos(lon_angle), -jnp.sin(lon_angle)], axis=1).astype(jnp.bfloat16)
    latitudes = jnp.arange(lat_len, dtype=jnp.int32)
    lat_phase = latitudes[:, None] * latitudes[None, :] % lat_len
    lat_angle = lat_phase.astype(jnp.float32) * (2.0 * math.pi / lat_len)
    cosine = jnp.cos(lat_angle)
    sine_part = jnp.sin(lat_angle)
    lat_table = jnp.stack(
        [jnp.stack([cosine, sine_part], axis=-1), jnp.stack([-sine_part, cosine], axis=-1)], axis=1
    ).astype(jnp.bfloat16)
    return (lon_table, lat_table)


def apply_blocks(operand, matrix):
    return jnp.einsum("smjbc,bcd->smjbd", operand, matrix, preferred_element_type=jnp.float32)


def adjoint(operand, matrix):
    return jnp.einsum("smjbd,bcd->smjbc", operand, matrix, preferred_element_type=jnp.float32)


def outer_sum(operand, other):
    return jnp.einsum("smjbc,smjbd->bcd", operand, other, preferred_element_type=jnp.float32)


def by_frequencies(
    activations, cotangent, w_first, w_second, b_first, lon_keep, relu_mask, shrink_mask
):
    parts = lax.axis_size("space")
    samples_dev = activations.shape[0]
    lat_len = activations.shape[1] * parts
    kept = lon_keep.shape[0]
    owned = kept // parts
    lon_table, lat_table = build_tables(lon_keep, lat_len, LON)
    ortho_scale = 1.0 / math.sqrt(lat_len * LON)
    act_lon = jnp.einsum(
        "shwc,wpk->shpkc", activations, lon_table, preferred_element_type=jnp.float32
    ).astype(jnp.bfloat16)
    cot_lon = jnp.einsum(
        "shwc,wpk->shpkc", cotangent, lon_table, preferred_element_type=jnp.float32
    ).astype(jnp.bfloat16)
    act_modes, cot_modes = (
        lax.all_to_all(act_lon, "space", split_axis=3, concat_axis=1, tiled=True),
        lax.all_to_all(cot_lon, "space", split_axis=3, concat_axis=1, tiled=True),
    )

    def latitude(modes):
        summed = jnp.einsum(
            "mphq,shqjc->smpjc", lat_table, modes, preferred_element_type=jnp.float32
        )
        return (summed * ortho_scale).astype(jnp.bfloat16)

    block_shape = (samples_dev, lat_len, 2, owned, BLOCKS, BS)
    spec_act = latitude(act_modes).reshape(block_shape)
    spec_cot = latitude(cot_modes)
    own_keep = lax.dynamic_slice_in_dim(lon_keep, lax.axis_index("space") * owned, owned)
    doubled = jnp.where((own_keep == 0) | (2 * own_keep == LON), 1.0, 2.0).astype(jnp.float32)
    grad_out = (
        jnp.where(
            shrink_mask > 0, doubled[None, None, None, :, None] * spec_cot.astype(jnp.float32), 0.0
        )
        .astype(jnp.bfloat16)
        .reshape(block_shape)
    )
    relu_gate = relu_mask.reshape(block_shape) > 0
    first_blocks = w_first.reshape(2, BLOCKS, BS, BS)
    second_blocks = w_second.reshape(2, BLOCKS, BS, BS)
    bias_blocks = b_first.reshape(2, BLOCKS, BS)
    act_real = spec_act[:, :, 0]
    act_imag = spec_act[:, :, 1]
    pre_real = (
        apply_blocks(act_real, first_blocks[0])
        - apply_blocks(act_imag, first_blocks[1])
        + bias_blocks[0]
    )
    pre_imag = (
        apply_blocks(act_real, first_blocks[1])
        + apply_blocks(act_imag, first_blocks[0])
        + bias_blocks[1]
    )
    hidden = jnp.where(relu_gate, jnp.stack([pre_real, pre_imag], axis=2), 0.0).astype(jnp.bfloat16)
    out_real = grad_out[:, :, 0]
    out_imag = grad_out[:, :, 1]
    hidden_real = adjoint(out_real, second_blocks[0]) + adjoint(out_imag, second_blocks[1])
    hidden_imag = -adjoint(out_real, second_blocks[1]) + adjoint(out_imag, second_blocks[0])
    grad_pre = jnp.where(relu_gate, jnp.stack([hidden_real, hidden_imag], axis=2), 0.0).astype(
        jnp.bfloat16
    )
    pre_grad_real = grad_pre[:, :, 0]
    pre_grad_imag = grad_pre[:, :, 1]
    spec_real = adjoint(pre_grad_real, first_blocks[0]) + adjoint(pre_grad_imag, first_blocks[1])
    spec_imag = -adjoint(pre_grad_real, first_blocks[1]) + adjoint(pre_grad_imag, first_blocks[0])
    grad_spec = (
        jnp.stack([spec_real, spec_imag], axis=2)
        .astype(jnp.bfloat16)
        .reshape(samples_dev, lat_len, 2, owned, C)
    )
    first_grad = jnp.stack(
        [
            outer_sum(act_real, pre_grad_real) + outer_sum(act_imag, pre_grad_imag),
            outer_sum(act_real, pre_grad_imag) - outer_sum(act_imag, pre_grad_real),
        ]
    ).reshape(2, C, BS)
    hid_real = hidden[:, :, 0]
    hid_imag = hidden[:, :, 1]
    second_grad = jnp.stack(
        [
            outer_sum(hid_real, out_real) + outer_sum(hid_imag, out_imag),
            outer_sum(hid_real, out_imag) - outer_sum(hid_imag, out_real),
        ]
    ).reshape(2, C, BS)
    bias_first = jnp.sum(grad_pre, axis=(0, 1, 3), dtype=jnp.float32).reshape(2, C)
    bias_second = jnp.sum(grad_out, axis=(0, 1, 3), dtype=jnp.float32).reshape(2, C)
    local_terms = (first_grad, second_grad, bias_first, bias_second)
    summed = lax.psum(
        (local_terms[0], local_terms[1], local_terms[2], local_terms[3]), ("dp", "space")
    )
    share_rows = C // lax.axis_size("dp")
    row_start = lax.axis_index("dp") * share_rows

    def take_share(array):
        return lax.dynamic_slice_in_dim(array, row_start, share_rows, 1)

    totals = jax.tree.map(take_share, summed)
    grad_norm = 1.0 / math.sqrt(samples_dev * lax.axis_size("dp") * lat_len * kept)
    grad_lat = jnp.einsum(
        "mqhp,smqjc->shpjc", lat_table, grad_spec, preferred_element_type=jnp.float32
    ).astype(jnp.bfloat16)
    returned = lax.all_to_all(grad_lat, "space", split_axis=1, concat_axis=3, tiled=True)
    grad_field = (
        jnp.einsum("wpk,shpkc->shwc", lon_table, returned, preferred_element_type=jnp.float32)
        * ortho_scale
    ).astype(jnp.bfloat16)
    return (
        grad_field,
        totals[0] * grad_norm,
        totals[1] * grad_norm,
        totals[2] * grad_norm,
        totals[3] * grad_norm,
    )


def solution(mesh):
    groups, parts = mesh.shape["dp"], mesh.shape["space"]

    def per_device(*arrays):
        activations, lon_keep = arrays[0], arrays[5]
        fits = (
            parts == BLOCKS
            and 2 * groups == BLOCKS
            and activations.shape[:2] == (1, 2)
            and lon_keep.shape[0] == parts
        )
        return by_blocks(*arrays) if fits else by_frequencies(*arrays)

    return jax.shard_map(
        per_device,
        mesh=mesh,
        in_specs=(
            P("dp", "space", None, None),
            P("dp", "space", None, None),
            P(),
            P(),
            P(),
            P(),
            P("dp", None, None, "space", None),
            P("dp", None, None, "space", None),
        ),
        out_specs=(
            P("dp", "space", None, None),
            P(None, "dp", None),
            P(None, "dp", None),
            P(None, "dp"),
            P(None, "dp"),
        ),
        check_vma=False,
    )
```

```python
import functools
import math

import jax
import jax.numpy as jnp
import numpy as np
from jax import lax
from jax.experimental import pallas as pl
from jax.experimental.pallas import tpu as pltpu
from jax.sharding import PartitionSpec as P

C = 768
BLOCKS = 8
LON = 180
BS = 96

BF = jnp.bfloat16
F32 = jnp.float32
LANES = 128
THIRD = LANES - BS
LON_CUT = 96
VMEM_LIMIT = 32 * 1024 * 1024


def shift_of(group):
    return 2 * (group % 2) + group // 2


def block_of(group, device):
    lane = 2 * (device // 4) + device % 2
    return 2 * ((lane + shift_of(group)) % 4) + (device // 2) % 2


def owner_of(group, block):
    lane = (block // 2 + 4 - shift_of(group)) % 4
    return 4 * (lane // 2) + 2 * (block % 2) + lane % 2


def latitude_matrix(lat_len, kept):
    index = np.arange(lat_len)
    angle = ((index[:, None] * index[None, :]) % lat_len).astype(np.float32) * np.float32(
        2.0 * math.pi / lat_len
    )
    cosine, sine = np.cos(angle), np.sin(angle)
    table = np.stack([np.stack([cosine, sine], -1), np.stack([-sine, cosine], -1)], 1)
    full = np.einsum("mphq,jk->pjmhqk", table, np.eye(kept, dtype=np.float32))
    return full.reshape(2 * kept * lat_len, 2 * kept * lat_len)


def dot(lhs, rhs, lhs_axis, rhs_axis):
    return lax.dot_general(
        lhs, rhs, (((lhs_axis,), (rhs_axis,)), ((), ())), preferred_element_type=F32
    )


def fold(array):
    rows = array.shape[0] // 4
    beside = [array[3 * rows :, g * THIRD : (g + 1) * THIRD] for g in range(3)]
    return jnp.concatenate([array[: 3 * rows], jnp.concatenate(beside, axis=0)], axis=1)


def unfold(array):
    rows = array.shape[0] // 3
    beside = [array[g * rows : (g + 1) * rows, BS:] for g in range(3)]
    return jnp.concatenate([array[:, :BS], jnp.concatenate(beside, axis=1)], axis=0)


def window_of(block):
    tile = jnp.minimum(block * BS // LANES, C // LANES - 2)
    return pl.multiple_of(tile * LANES, LANES), block * BS - tile * LANES


def forward_lon_kernel(
    keep_hbm,
    act_hbm,
    cot_hbm,
    relu_hbm,
    shrink_hbm,
    *refs,
):
    weights_hbm, matrices_hbm, refs = refs[:3], refs[3:5], refs[5:]
    out, table_out, *fetched, field, masks, keep, sems = refs
    group, device = lax.axis_index("dp"), lax.axis_index("space")
    start, _ = window_of(block_of(group, device))
    kept = keep.shape[0]
    rows = act_hbm.shape[1]
    modes = relu_hbm.shape[0]
    tiles = C // LANES
    columns = [slice(k * LANES, (k + 1) * LANES) for k in range(tiles)]
    keep_copy = pltpu.make_async_copy(keep_hbm, keep, sems.at[0])
    keep_copy.start()
    mask_copies, field_copies = [], []
    for t, source in enumerate((relu_hbm, shrink_hbm)):
        copy = pltpu.make_async_copy(source, masks.at[t], sems.at[1 + t])
        copy.start()
        mask_copies.append(copy)
    for t, source in enumerate((act_hbm, cot_hbm)):
        copy = pltpu.make_async_copy(source, field.at[t], sems.at[3 + t])
        copy.start()
        field_copies.append(copy)
    sources = [
        source.at[(slice(None),) * (len(source.shape) - 1) + (pl.ds(start, 2 * LANES),)]
        for source in weights_hbm
    ] + list(matrices_hbm)
    other_copies = []
    for i, (source, target) in enumerate(zip(sources, fetched)):
        copy = pltpu.make_async_copy(source, target, sems.at[5 + i])
        copy.start()
        other_copies.append(copy)

    keep_copy.wait()
    shape = (rows * 2 * kept, LON * rows)
    line = lax.broadcasted_iota(jnp.int32, shape, 0)
    column = lax.broadcasted_iota(jnp.int32, shape, 1)
    frequency = jnp.zeros(shape, jnp.int32)
    for j in range(kept):
        frequency = jnp.where(line % kept == j, keep[j], frequency)
    turn = jnp.where((line // kept) % 2 == 1, LON // 4, 0)
    phase = ((column // rows) * frequency + turn) % LON
    table = jnp.cos(phase.astype(F32) * (2.0 * math.pi / LON))
    wide_table = jnp.where(line // (2 * kept) == column % rows, table, 0.0)
    table = wide_table.astype(BF)
    table_out[...] = wide_table.T.astype(BF)

    own = keep[device]
    scale = jnp.where((own == 0) | (2 * own == LON), 1.0, 2.0)
    for copy in mask_copies:
        copy.wait()

    def gate(t, value):
        return jnp.concatenate(
            [jnp.where(masks[t, :, p, 0, :] > 0, value, 0.0) for p in range(2)], axis=0
        ).astype(BF)

    passed = gate(0, 1.0)
    scaled = gate(1, scale)
    per = table.shape[0]
    owners = [owner_of(group, b) for b in range(BLOCKS)]
    for b in range(BLOCKS):
        out[owners[b], 2 * per :, 0:BS] = passed[:, b * BS : (b + 1) * BS]
        beside = [scaled[:, b * BS + g * THIRD : b * BS + (g + 1) * THIRD] for g in range(3)]
        out[owners[b], :, BS:] = jnp.concatenate(beside, axis=0)

    for t in range(2):
        field_copies[t].wait()
        wide = jnp.concatenate(
            [
                field[t, :, :, columns[k]].reshape(LON * rows, LANES) for k in range(tiles)
            ],
            axis=1,
        )
        lines = dot(table, wide, 1, 0).astype(BF)
        for b in range(BLOCKS):
            out[owners[b], t * per : (t + 1) * per, 0:BS] = lines[:, b * BS : (b + 1) * BS]
    for copy in other_copies:
        copy.wait()


def block_adjoint(operand, matrix):
    half = operand.shape[0] // 2
    both = dot(operand, matrix, 1, 0)
    real, imag = both[:, :LANES], both[:, LANES:]
    return jnp.concatenate([real[:half] + imag[half:], real[half:] - imag[:half]], axis=0)


def spectral_kernel(
    pieces,
    first_wide,
    second_wide,
    bias_wide,
    lat,
    terms,
    grad_pre_out,
    first_out,
    *,
    ortho_scale,
    rows,
    kept,
):
    device = lax.axis_index("space")
    _, offset = window_of(block_of(lax.axis_index("dp"), device))
    parts = pieces.shape[0]
    per = rows * 2 * kept
    half = parts * per // 2
    modes = half // kept
    spare = jnp.zeros((LANES - BS, LANES), F32)
    place = lax.broadcasted_iota(jnp.int32, (2 * LANES, LANES), 1)
    chosen = (lax.broadcasted_iota(jnp.int32, (2 * LANES, LANES), 0) == place + offset) & (
        place < BS
    )
    chosen = jnp.where(chosen, 1.0, 0.0).astype(BF)

    def matrices(wide):
        found = dot(wide[...].reshape(2 * BS, 2 * LANES), chosen, 1, 0)
        return [jnp.concatenate([found[p * BS : (p + 1) * BS], spare], axis=0) for p in range(2)]

    first, second = matrices(first_wide), matrices(second_wide)
    across = jnp.concatenate(first, axis=0).astype(BF)
    first_out[...] = jnp.concatenate(first, axis=1).astype(BF)
    second = jnp.concatenate(second, axis=1).astype(BF)
    bias = pltpu.roll(bias_wide[...], (2 * LANES - offset) % (2 * LANES), 1)[:, :LANES]
    bias = jnp.where(lax.broadcasted_iota(jnp.int32, bias.shape, 1) < BS, bias, 0.0)

    def mode_rows(found):
        return jnp.concatenate(
            [found[j][p * modes : (p + 1) * modes] for p in range(2) for j in range(kept)], axis=0
        ).astype(F32)

    group = pieces.shape[1] // 3
    passed = mode_rows([pieces[j, 2 * per :, :] for j in range(kept)]) > 0.0
    weight = mode_rows(
        [
            jnp.concatenate(
                [pieces[j, g * group : (g + 1) * group, BS:] for g in range(3)]
                + [jnp.zeros((group, THIRD), BF)],
                axis=1,
            )
            for j in range(kept)
        ]
    )

    stacked = jnp.concatenate(
        [
            jnp.concatenate([pieces[i, t * per : (t + 1) * per, :] for i in range(parts)], axis=0)
            for t in range(2)
        ],
        axis=1,
    )
    spectra = (dot(lat[...], stacked, 1, 0) * ortho_scale).astype(BF)
    spec_act, spec_cot = spectra[:, :LANES], spectra[:, LANES:]
    grad_out = jnp.where(weight > 0.0, weight * spec_cot.astype(F32), 0.0).astype(BF)
    grad_pre = jnp.where(passed, block_adjoint(grad_out, second), 0.0).astype(BF)
    grad_pre_out[...] = grad_pre

    both = dot(spec_act, across, 1, 1)
    by_real, by_imag = both[:, :LANES], both[:, LANES:]
    pre = jnp.concatenate(
        [
            by_real[:half] - by_imag[half:] + bias[0:1],
            by_imag[:half] + by_real[half:] + bias[1:2],
        ],
        axis=0,
    )
    hidden = jnp.where(passed, pre, 0.0).astype(BF)

    at = 3 * BS // 4
    blank = jnp.zeros((terms.shape[2] - at - 1, LANES), F32)
    for a, (left, right) in enumerate(((spec_act, grad_pre), (hidden, grad_out))):
        slot = (a + device) % 2
        wide = right.astype(F32)
        turned = jnp.concatenate([right[half:], -right[:half]], axis=0)
        products = dot(left, jnp.concatenate([right, turned], axis=1), 0, 0)
        for p in range(2):
            summed = jnp.sum(wide[p * half : (p + 1) * half], axis=0, keepdims=True)
            terms[slot, p] = jnp.concatenate(
                [fold(products[:BS, p * LANES : p * LANES + BS]), summed, blank], axis=0
            ).astype(BF)


def grad_lat_kernel(grad_pre, first, lat_t, grad_lat):
    grad_spec = block_adjoint(grad_pre[...], first[...]).astype(BF)
    lines = dot(lat_t[...], grad_spec, 1, 0)
    per = lines.shape[0] // grad_lat.shape[0]
    for i in range(grad_lat.shape[0]):
        grad_lat[i] = fold(lines[i * per : (i + 1) * per, :BS]).astype(BF)


def inverse_lon_kernel(table, pieces, field_hbm, field, sems, *, ortho_scale):
    rows = field.shape[1]
    per = table.shape[1]
    group = lax.axis_index("dp")
    lines = jnp.concatenate(
        [unfold(pieces[owner_of(group, b), 0 : 3 * per // 4, :]) for b in range(BLOCKS)], axis=1
    )
    copies = []
    for i, (start, stop) in enumerate(((0, LON_CUT), (LON_CUT, LON))):
        wide = (dot(table[start * rows : stop * rows], lines, 1, 0) * ortho_scale).astype(BF)
        for k in range(C // LANES):
            lanes = slice(k * LANES, (k + 1) * LANES)
            field[start:stop, :, lanes] = wide[:, lanes].reshape(stop - start, rows, LANES)
        copy = pltpu.make_async_copy(
            field.at[start:stop], field_hbm.at[start:stop], sems.at[i]
        )
        copy.start()
        copies.append(copy)
    for copy in copies:
        copy.wait()


def gathered_kernel(pieces, others, first, second, bias_first, bias_second, *, grad_norm):
    core = lax.axis_index("space") % 2
    per = pieces.shape[1] - others.shape[1]
    at = 3 * BS // 4
    for a, (target, vector) in enumerate(((first, bias_first), (second, bias_second))):
        for k in range(2):
            near, far = 2 * k + a, 4 + 2 * k + a
            own = pieces[near, per:, :].astype(F32) + pieces[far, per:, :].astype(F32)
            other = others[near].astype(F32) + others[far].astype(F32)
            for p in range(2):
                total = jnp.where(core == p, own, other) * grad_norm
                target[p, k * BS : (k + 1) * BS, :] = unfold(total[:at])
                vector[p : p + 1, k * BS : (k + 1) * BS] = total[at : at + 1, :BS]


def whole(memory=pltpu.VMEM):
    return pl.BlockSpec(memory_space=memory)


def by_blocks(
    activations, cotangent, w_first, w_second, b_first, lon_keep, relu_mask, shrink_mask
):
    groups = lax.axis_size("dp")
    parts = lax.axis_size("space")
    rows = activations.shape[1]
    lat_len = rows * parts
    kept = lon_keep.shape[0]
    ortho_scale = 1.0 / math.sqrt(lat_len * LON)
    grad_norm = 1.0 / math.sqrt(groups * lat_len * kept)
    params = pltpu.CompilerParams(vmem_limit_bytes=VMEM_LIMIT)
    tiles = C // LANES
    per = rows * 2 * kept
    height = (2 * per + 4 * lat_len) * 3 // 4
    term_rows = 3 * BS // 4 + 8

    lat = latitude_matrix(lat_len, kept)
    sent, table, *fetched = pl.pallas_call(
        forward_lon_kernel,
        out_shape=(
            pltpu.VMEM((parts, height, LANES), BF),
            pltpu.VMEM((LON * rows, per), BF),
            pltpu.VMEM((2, BS, 2 * LANES), BF),
            pltpu.VMEM((2, BS, 2 * LANES), BF),
            pltpu.VMEM((2, 2 * LANES), F32),
            pltpu.VMEM(lat.shape, BF),
            pltpu.VMEM(lat.shape, BF),
        ),
        in_specs=[whole(pl.ANY)] * 10,
        out_specs=(whole(),) * 7,
        scratch_shapes=[
            pltpu.VMEM((2, LON, rows, C), BF),
            pltpu.VMEM((2, lat_len, 2, 1, C), jnp.int32),
            pltpu.SMEM((kept,), jnp.int32),
            pltpu.SemaphoreType.DMA((10,)),
        ],
        compiler_params=params,
        name="forward_lon",
    )(
        *(
            pltpu.with_memory_space_constraint(array, pltpu.HBM)
            for array in (
                lon_keep,
                activations[0].transpose(1, 0, 2),
                cotangent[0].transpose(1, 0, 2),
                relu_mask[0],
                shrink_mask[0],
                w_first.transpose(0, 2, 1),
                w_second.transpose(0, 2, 1),
                b_first,
                jnp.asarray(lat, BF),
                jnp.asarray(lat.T, BF),
            )
        )
    )
    pieces = lax.all_to_all(sent, "space", 0, 0, tiled=True)

    *fetched, lat_t = fetched
    terms, grad_pre, first_block = pl.pallas_call(
        functools.partial(spectral_kernel, ortho_scale=ortho_scale, rows=rows, kept=kept),
        out_shape=(
            jax.ShapeDtypeStruct((2, 2, term_rows, LANES), BF),
            pltpu.VMEM((lat.shape[0], LANES), BF),
            pltpu.VMEM((LANES, 2 * LANES), BF),
        ),
        in_specs=[whole()] * 5,
        out_specs=(whole(),) * 3,
        compiler_params=params,
        name="spectral",
    )(pieces, *fetched)
    grad_lat = pl.pallas_call(
        grad_lat_kernel,
        out_shape=jax.ShapeDtypeStruct((parts, 3 * per // 4, LANES), BF),
        in_specs=[whole()] * 3,
        out_specs=whole(),
        compiler_params=params,
        cost_estimate=pl.CostEstimate(
            flops=2 * lat.size * BS * 3, bytes_accessed=4 * lat.size, transcendentals=0
        ),
        name="grad_lat",
    )(grad_pre, first_block, lat_t)

    arrived = lax.ppermute(
        terms,
        ("dp", "space"),
        [
            (g * parts + c, (block_of(g, c) // 2) * parts + c)
            for g in range(groups)
            for c in range(parts)
        ],
    )
    other = lax.ppermute(arrived[1], "space", [(c, c ^ 1) for c in range(parts)])
    share = (arrived[0].astype(F32) + other.astype(F32)).astype(BF)
    share = jnp.broadcast_to(share[None], (parts // 2,) + share.shape)
    returned = lax.all_to_all(
        jnp.concatenate([grad_lat, share.reshape(parts, term_rows, LANES)], axis=1),
        "space",
        0,
        0,
        tiled=True,
    )
    others = lax.ppermute(returned[:, 3 * per // 4 :, :], "space", [(c, c ^ 1) for c in range(parts)])

    keep_rows = C // groups
    field = pl.pallas_call(
        functools.partial(inverse_lon_kernel, ortho_scale=ortho_scale),
        out_shape=jax.ShapeDtypeStruct((LON, rows, C), BF),
        in_specs=[whole(), whole()],
        out_specs=whole(pl.ANY),
        scratch_shapes=[
            pltpu.VMEM((LON, rows, C), BF),
            pltpu.SemaphoreType.DMA((2,)),
        ],
        compiler_params=params,
        cost_estimate=pl.CostEstimate(
            flops=2 * per * LON * rows * C, bytes_accessed=8 * LON * rows * C, transcendentals=0
        ),
        name="inverse_lon",
    )(table, returned)
    first, second, bias_first, bias_second = pl.pallas_call(
        functools.partial(gathered_kernel, grad_norm=grad_norm),
        out_shape=(
            jax.ShapeDtypeStruct((2, keep_rows, BS), F32),
            jax.ShapeDtypeStruct((2, keep_rows, BS), F32),
            jax.ShapeDtypeStruct((2, keep_rows), F32),
            jax.ShapeDtypeStruct((2, keep_rows), F32),
        ),
        in_specs=[whole(), whole()],
        out_specs=(whole(),) * 4,
        compiler_params=params,
        name="gathered",
    )(returned, others)
    return field.transpose(1, 0, 2)[None], first, second, bias_first, bias_second


def build_tables(lon_keep, lat_len, lon_len):
    columns = jnp.arange(lon_len, dtype=jnp.int32)
    lon_phase = columns[:, None] * lon_keep[None, :] % lon_len
    lon_angle = lon_phase.astype(jnp.float32) * (2.0 * math.pi / lon_len)
    lon_table = jnp.stack([jnp.cos(lon_angle), -jnp.sin(lon_angle)], axis=1).astype(jnp.bfloat16)
    latitudes = jnp.arange(lat_len, dtype=jnp.int32)
    lat_phase = latitudes[:, None] * latitudes[None, :] % lat_len
    lat_angle = lat_phase.astype(jnp.float32) * (2.0 * math.pi / lat_len)
    cosine = jnp.cos(lat_angle)
    sine_part = jnp.sin(lat_angle)
    lat_table = jnp.stack(
        [jnp.stack([cosine, sine_part], axis=-1), jnp.stack([-sine_part, cosine], axis=-1)], axis=1
    ).astype(jnp.bfloat16)
    return (lon_table, lat_table)


def apply_blocks(operand, matrix):
    return jnp.einsum("smjbc,bcd->smjbd", operand, matrix, preferred_element_type=jnp.float32)


def adjoint(operand, matrix):
    return jnp.einsum("smjbd,bcd->smjbc", operand, matrix, preferred_element_type=jnp.float32)


def outer_sum(operand, other):
    return jnp.einsum("smjbc,smjbd->bcd", operand, other, preferred_element_type=jnp.float32)


def by_frequencies(
    activations, cotangent, w_first, w_second, b_first, lon_keep, relu_mask, shrink_mask
):
    parts = lax.axis_size("space")
    samples_dev = activations.shape[0]
    lat_len = activations.shape[1] * parts
    kept = lon_keep.shape[0]
    owned = kept // parts
    lon_table, lat_table = build_tables(lon_keep, lat_len, LON)
    ortho_scale = 1.0 / math.sqrt(lat_len * LON)
    act_lon = jnp.einsum(
        "shwc,wpk->shpkc", activations, lon_table, preferred_element_type=jnp.float32
    ).astype(jnp.bfloat16)
    cot_lon = jnp.einsum(
        "shwc,wpk->shpkc", cotangent, lon_table, preferred_element_type=jnp.float32
    ).astype(jnp.bfloat16)
    act_modes, cot_modes = (
        lax.all_to_all(act_lon, "space", split_axis=3, concat_axis=1, tiled=True),
        lax.all_to_all(cot_lon, "space", split_axis=3, concat_axis=1, tiled=True),
    )

    def latitude(modes):
        summed = jnp.einsum(
            "mphq,shqjc->smpjc", lat_table, modes, preferred_element_type=jnp.float32
        )
        return (summed * ortho_scale).astype(jnp.bfloat16)

    block_shape = (samples_dev, lat_len, 2, owned, BLOCKS, BS)
    spec_act = latitude(act_modes).reshape(block_shape)
    spec_cot = latitude(cot_modes)
    own_keep = lax.dynamic_slice_in_dim(lon_keep, lax.axis_index("space") * owned, owned)
    doubled = jnp.where((own_keep == 0) | (2 * own_keep == LON), 1.0, 2.0).astype(jnp.float32)
    grad_out = (
        jnp.where(
            shrink_mask > 0, doubled[None, None, None, :, None] * spec_cot.astype(jnp.float32), 0.0
        )
        .astype(jnp.bfloat16)
        .reshape(block_shape)
    )
    relu_gate = relu_mask.reshape(block_shape) > 0
    first_blocks = w_first.reshape(2, BLOCKS, BS, BS)
    second_blocks = w_second.reshape(2, BLOCKS, BS, BS)
    bias_blocks = b_first.reshape(2, BLOCKS, BS)
    act_real = spec_act[:, :, 0]
    act_imag = spec_act[:, :, 1]
    pre_real = (
        apply_blocks(act_real, first_blocks[0])
        - apply_blocks(act_imag, first_blocks[1])
        + bias_blocks[0]
    )
    pre_imag = (
        apply_blocks(act_real, first_blocks[1])
        + apply_blocks(act_imag, first_blocks[0])
        + bias_blocks[1]
    )
    hidden = jnp.where(relu_gate, jnp.stack([pre_real, pre_imag], axis=2), 0.0).astype(jnp.bfloat16)
    out_real = grad_out[:, :, 0]
    out_imag = grad_out[:, :, 1]
    hidden_real = adjoint(out_real, second_blocks[0]) + adjoint(out_imag, second_blocks[1])
    hidden_imag = -adjoint(out_real, second_blocks[1]) + adjoint(out_imag, second_blocks[0])
    grad_pre = jnp.where(relu_gate, jnp.stack([hidden_real, hidden_imag], axis=2), 0.0).astype(
        jnp.bfloat16
    )
    pre_grad_real = grad_pre[:, :, 0]
    pre_grad_imag = grad_pre[:, :, 1]
    spec_real = adjoint(pre_grad_real, first_blocks[0]) + adjoint(pre_grad_imag, first_blocks[1])
    spec_imag = -adjoint(pre_grad_real, first_blocks[1]) + adjoint(pre_grad_imag, first_blocks[0])
    grad_spec = (
        jnp.stack([spec_real, spec_imag], axis=2)
        .astype(jnp.bfloat16)
        .reshape(samples_dev, lat_len, 2, owned, C)
    )
    first_grad = jnp.stack(
        [
            outer_sum(act_real, pre_grad_real) + outer_sum(act_imag, pre_grad_imag),
            outer_sum(act_real, pre_grad_imag) - outer_sum(act_imag, pre_grad_real),
        ]
    ).reshape(2, C, BS)
    hid_real = hidden[:, :, 0]
    hid_imag = hidden[:, :, 1]
    second_grad = jnp.stack(
        [
            outer_sum(hid_real, out_real) + outer_sum(hid_imag, out_imag),
            outer_sum(hid_real, out_imag) - outer_sum(hid_imag, out_real),
        ]
    ).reshape(2, C, BS)
    bias_first = jnp.sum(grad_pre, axis=(0, 1, 3), dtype=jnp.float32).reshape(2, C)
    bias_second = jnp.sum(grad_out, axis=(0, 1, 3), dtype=jnp.float32).reshape(2, C)
    local_terms = (first_grad, second_grad, bias_first, bias_second)
    summed = lax.psum(
        (local_terms[0], local_terms[1], local_terms[2], local_terms[3]), ("dp", "space")
    )
    share_rows = C // lax.axis_size("dp")
    row_start = lax.axis_index("dp") * share_rows

    def take_share(array):
        return lax.dynamic_slice_in_dim(array, row_start, share_rows, 1)

    totals = jax.tree.map(take_share, summed)
    grad_norm = 1.0 / math.sqrt(samples_dev * lax.axis_size("dp") * lat_len * kept)
    grad_lat = jnp.einsum(
        "mqhp,smqjc->shpjc", lat_table, grad_spec, preferred_element_type=jnp.float32
    ).astype(jnp.bfloat16)
    returned = lax.all_to_all(grad_lat, "space", split_axis=1, concat_axis=3, tiled=True)
    grad_field = (
        jnp.einsum("wpk,shpkc->shwc", lon_table, returned, preferred_element_type=jnp.float32)
        * ortho_scale
    ).astype(jnp.bfloat16)
    return (
        grad_field,
        totals[0] * grad_norm,
        totals[1] * grad_norm,
        totals[2] * grad_norm,
        totals[3] * grad_norm,
    )


def solution(mesh):
    groups, parts = mesh.shape["dp"], mesh.shape["space"]

    def per_device(*arrays):
        activations, lon_keep = arrays[0], arrays[5]
        fits = (
            parts == BLOCKS
            and 2 * groups == BLOCKS
            and activations.shape[:2] == (1, 2)
            and lon_keep.shape[0] == parts
        )
        return by_blocks(*arrays) if fits else by_frequencies(*arrays)

    return jax.shard_map(
        per_device,
        mesh=mesh,
        in_specs=(
            P("dp", "space", None, None),
            P("dp", "space", None, None),
            P(),
            P(),
            P(),
            P(),
            P("dp", None, None, "space", None),
            P("dp", None, None, "space", None),
        ),
        out_specs=(
            P("dp", "space", None, None),
            P(None, "dp", None),
            P(None, "dp", None),
            P(None, "dp"),
            P(None, "dp"),
        ),
        check_vma=False,
    )
```

```python
import functools
import math

import jax
import jax.numpy as jnp
import numpy as np
from jax import lax
from jax.experimental import pallas as pl
from jax.experimental.pallas import tpu as pltpu
from jax.sharding import PartitionSpec as P

C = 768
BLOCKS = 8
LON = 180
BS = 96

BF = jnp.bfloat16
F32 = jnp.float32
LANES = 128
THIRD = LANES - BS
LON_CUT = 96
VMEM_LIMIT = 32 * 1024 * 1024


def shift_of(group):
    return 2 * (group % 2) + group // 2


def block_of(group, device):
    lane = 2 * (device // 4) + device % 2
    return 2 * ((lane + shift_of(group)) % 4) + (device // 2) % 2


def owner_of(group, block):
    lane = (block // 2 + 4 - shift_of(group)) % 4
    return 4 * (lane // 2) + 2 * (block % 2) + lane % 2


def latitude_matrix(lat_len, kept):
    index = np.arange(lat_len)
    angle = ((index[:, None] * index[None, :]) % lat_len).astype(np.float32) * np.float32(
        2.0 * math.pi / lat_len
    )
    cosine, sine = np.cos(angle), np.sin(angle)
    table = np.stack([np.stack([cosine, sine], -1), np.stack([-sine, cosine], -1)], 1)
    full = np.einsum("mphq,jk->pjmhqk", table, np.eye(kept, dtype=np.float32))
    return full.reshape(2 * kept * lat_len, 2 * kept * lat_len)


def dot(lhs, rhs, lhs_axis, rhs_axis):
    return lax.dot_general(
        lhs, rhs, (((lhs_axis,), (rhs_axis,)), ((), ())), preferred_element_type=F32
    )


def fold(array):
    rows = array.shape[0] // 4
    beside = [array[3 * rows :, g * THIRD : (g + 1) * THIRD] for g in range(3)]
    return jnp.concatenate([array[: 3 * rows], jnp.concatenate(beside, axis=0)], axis=1)


def unfold(array):
    rows = array.shape[0] // 3
    beside = [array[g * rows : (g + 1) * rows, BS:] for g in range(3)]
    return jnp.concatenate([array[:, :BS], jnp.concatenate(beside, axis=1)], axis=0)


def window_of(block):
    tile = jnp.minimum(block * BS // LANES, C // LANES - 2)
    return pl.multiple_of(tile * LANES, LANES), block * BS - tile * LANES


def forward_lon_kernel(
    keep_hbm,
    act_hbm,
    cot_hbm,
    relu_hbm,
    shrink_hbm,
    *refs,
):
    weights_hbm, matrices_hbm, refs = refs[:3], refs[3:5], refs[5:]
    out, table_out, *fetched, field, masks, keep, sems = refs
    group, device = lax.axis_index("dp"), lax.axis_index("space")
    start, _ = window_of(block_of(group, device))
    kept = keep.shape[0]
    rows = act_hbm.shape[1]
    modes = relu_hbm.shape[0]
    tiles = C // LANES
    columns = [slice(k * LANES, (k + 1) * LANES) for k in range(tiles)]
    keep_copy = pltpu.make_async_copy(keep_hbm, keep, sems.at[0])
    keep_copy.start()
    mask_copies, field_copies = [], []
    for t, source in enumerate((act_hbm, cot_hbm)):
        copy = pltpu.make_async_copy(source, field.at[t], sems.at[3 + t])
        copy.start()
        field_copies.append(copy)
    for t, source in enumerate((relu_hbm, shrink_hbm)):
        copy = pltpu.make_async_copy(source, masks.at[t], sems.at[1 + t])
        copy.start()
        mask_copies.append(copy)
    sources = [
        source.at[(slice(None),) * (len(source.shape) - 1) + (pl.ds(start, 2 * LANES),)]
        for source in weights_hbm
    ] + list(matrices_hbm)
    other_copies = []
    for i, (source, target) in enumerate(zip(sources, fetched)):
        copy = pltpu.make_async_copy(source, target, sems.at[5 + i])
        copy.start()
        other_copies.append(copy)

    keep_copy.wait()
    shape = (rows * 2 * kept, LON * rows)
    line = lax.broadcasted_iota(jnp.int32, shape, 0)
    column = lax.broadcasted_iota(jnp.int32, shape, 1)
    frequency = jnp.zeros(shape, jnp.int32)
    for j in range(kept):
        frequency = jnp.where(line % kept == j, keep[j], frequency)
    turn = jnp.where((line // kept) % 2 == 1, LON // 4, 0)
    phase = ((column // rows) * frequency + turn) % LON
    table = jnp.cos(phase.astype(F32) * (2.0 * math.pi / LON))
    wide_table = jnp.where(line // (2 * kept) == column % rows, table, 0.0)
    table = wide_table.astype(BF)
    table_out[...] = wide_table.T.astype(BF)

    own = keep[device]
    scale = jnp.where((own == 0) | (2 * own == LON), 1.0, 2.0)
    for copy in mask_copies:
        copy.wait()

    def gate(t, value):
        return jnp.concatenate(
            [jnp.where(masks[t, :, p, 0, :] > 0, value, 0.0) for p in range(2)], axis=0
        ).astype(BF)

    passed = gate(0, 1.0)
    scaled = gate(1, scale)
    per = table.shape[0]
    owners = [owner_of(group, b) for b in range(BLOCKS)]
    for b in range(BLOCKS):
        out[owners[b], 2 * per :, 0:BS] = passed[:, b * BS : (b + 1) * BS]
        beside = [scaled[:, b * BS + g * THIRD : b * BS + (g + 1) * THIRD] for g in range(3)]
        out[owners[b], :, BS:] = jnp.concatenate(beside, axis=0)

    for t in range(2):
        field_copies[t].wait()
        wide = jnp.concatenate(
            [
                field[t, :, :, columns[k]].reshape(LON * rows, LANES) for k in range(tiles)
            ],
            axis=1,
        )
        lines = dot(table, wide, 1, 0).astype(BF)
        for b in range(BLOCKS):
            out[owners[b], t * per : (t + 1) * per, 0:BS] = lines[:, b * BS : (b + 1) * BS]
    for copy in other_copies:
        copy.wait()


def block_adjoint(operand, matrix):
    half = operand.shape[0] // 2
    both = dot(operand, matrix, 1, 0)
    real, imag = both[:, :LANES], both[:, LANES:]
    return jnp.concatenate([real[:half] + imag[half:], real[half:] - imag[:half]], axis=0)


def spectral_kernel(
    pieces,
    first_wide,
    second_wide,
    bias_wide,
    lat,
    terms,
    grad_pre_out,
    first_out,
    *,
    ortho_scale,
    rows,
    kept,
):
    device = lax.axis_index("space")
    _, offset = window_of(block_of(lax.axis_index("dp"), device))
    parts = pieces.shape[0]
    per = rows * 2 * kept
    half = parts * per // 2
    modes = half // kept
    spare = jnp.zeros((LANES - BS, LANES), F32)
    place = lax.broadcasted_iota(jnp.int32, (2 * LANES, LANES), 1)
    chosen = (lax.broadcasted_iota(jnp.int32, (2 * LANES, LANES), 0) == place + offset) & (
        place < BS
    )
    chosen = jnp.where(chosen, 1.0, 0.0).astype(BF)

    def matrices(wide):
        found = dot(wide[...].reshape(2 * BS, 2 * LANES), chosen, 1, 0)
        return [jnp.concatenate([found[p * BS : (p + 1) * BS], spare], axis=0) for p in range(2)]

    first, second = matrices(first_wide), matrices(second_wide)
    across = jnp.concatenate(first, axis=0).astype(BF)
    first_out[...] = jnp.concatenate(first, axis=1).astype(BF)
    second = jnp.concatenate(second, axis=1).astype(BF)
    bias = pltpu.roll(bias_wide[...], (2 * LANES - offset) % (2 * LANES), 1)[:, :LANES]
    bias = jnp.where(lax.broadcasted_iota(jnp.int32, bias.shape, 1) < BS, bias, 0.0)

    def mode_rows(found):
        return jnp.concatenate(
            [found[j][p * modes : (p + 1) * modes] for p in range(2) for j in range(kept)], axis=0
        ).astype(F32)

    group = pieces.shape[1] // 3
    passed = mode_rows([pieces[j, 2 * per :, :] for j in range(kept)]) > 0.0
    weight = mode_rows(
        [
            jnp.concatenate(
                [pieces[j, g * group : (g + 1) * group, BS:] for g in range(3)]
                + [jnp.zeros((group, THIRD), BF)],
                axis=1,
            )
            for j in range(kept)
        ]
    )

    stacked = jnp.concatenate(
        [
            jnp.concatenate([pieces[i, t * per : (t + 1) * per, :] for i in range(parts)], axis=0)
            for t in range(2)
        ],
        axis=1,
    )
    spectra = (dot(lat[...], stacked, 1, 0) * ortho_scale).astype(BF)
    spec_act, spec_cot = spectra[:, :LANES], spectra[:, LANES:]
    grad_out = jnp.where(weight > 0.0, weight * spec_cot.astype(F32), 0.0).astype(BF)
    grad_pre = jnp.where(passed, block_adjoint(grad_out, second), 0.0).astype(BF)
    grad_pre_out[...] = grad_pre

    both = dot(spec_act, across, 1, 1)
    by_real, by_imag = both[:, :LANES], both[:, LANES:]
    pre = jnp.concatenate(
        [
            by_real[:half] - by_imag[half:] + bias[0:1],
            by_imag[:half] + by_real[half:] + bias[1:2],
        ],
        axis=0,
    )
    hidden = jnp.where(passed, pre, 0.0).astype(BF)

    at = 3 * BS // 4
    blank = jnp.zeros((terms.shape[2] - at - 1, LANES), F32)
    for a, (left, right) in enumerate(((spec_act, grad_pre), (hidden, grad_out))):
        slot = (a + device) % 2
        wide = right.astype(F32)
        turned = jnp.concatenate([right[half:], -right[:half]], axis=0)
        products = dot(left, jnp.concatenate([right, turned], axis=1), 0, 0)
        for p in range(2):
            summed = jnp.sum(wide[p * half : (p + 1) * half], axis=0, keepdims=True)
            terms[slot, p] = jnp.concatenate(
                [fold(products[:BS, p * LANES : p * LANES + BS]), summed, blank], axis=0
            ).astype(BF)


def grad_lat_kernel(grad_pre, first, lat_t, grad_lat):
    grad_spec = block_adjoint(grad_pre[...], first[...]).astype(BF)
    lines = dot(lat_t[...], grad_spec, 1, 0)
    per = lines.shape[0] // grad_lat.shape[0]
    for i in range(grad_lat.shape[0]):
        grad_lat[i] = fold(lines[i * per : (i + 1) * per, :BS]).astype(BF)


def inverse_lon_kernel(table, pieces, field_hbm, field, sems, *, ortho_scale):
    rows = field.shape[1]
    per = table.shape[1]
    group = lax.axis_index("dp")
    lines = jnp.concatenate(
        [unfold(pieces[owner_of(group, b), 0 : 3 * per // 4, :]) for b in range(BLOCKS)], axis=1
    )
    copies = []
    for i, (start, stop) in enumerate(((0, LON_CUT), (LON_CUT, LON))):
        wide = (dot(table[start * rows : stop * rows], lines, 1, 0) * ortho_scale).astype(BF)
        for k in range(C // LANES):
            lanes = slice(k * LANES, (k + 1) * LANES)
            field[start:stop, :, lanes] = wide[:, lanes].reshape(stop - start, rows, LANES)
        copy = pltpu.make_async_copy(
            field.at[start:stop], field_hbm.at[start:stop], sems.at[i]
        )
        copy.start()
        copies.append(copy)
    for copy in copies:
        copy.wait()


def gathered_kernel(pieces, others, first, second, bias_first, bias_second, *, grad_norm):
    core = lax.axis_index("space") % 2
    per = pieces.shape[1] - others.shape[1]
    at = 3 * BS // 4
    for a, (target, vector) in enumerate(((first, bias_first), (second, bias_second))):
        for k in range(2):
            near, far = 2 * k + a, 4 + 2 * k + a
            own = pieces[near, per:, :].astype(F32) + pieces[far, per:, :].astype(F32)
            other = others[near].astype(F32) + others[far].astype(F32)
            for p in range(2):
                total = jnp.where(core == p, own, other) * grad_norm
                target[p, k * BS : (k + 1) * BS, :] = unfold(total[:at])
                vector[p : p + 1, k * BS : (k + 1) * BS] = total[at : at + 1, :BS]


def whole(memory=pltpu.VMEM):
    return pl.BlockSpec(memory_space=memory)


def by_blocks(
    activations, cotangent, w_first, w_second, b_first, lon_keep, relu_mask, shrink_mask
):
    groups = lax.axis_size("dp")
    parts = lax.axis_size("space")
    rows = activations.shape[1]
    lat_len = rows * parts
    kept = lon_keep.shape[0]
    ortho_scale = 1.0 / math.sqrt(lat_len * LON)
    grad_norm = 1.0 / math.sqrt(groups * lat_len * kept)
    params = pltpu.CompilerParams(vmem_limit_bytes=VMEM_LIMIT)
    tiles = C // LANES
    per = rows * 2 * kept
    height = (2 * per + 4 * lat_len) * 3 // 4
    term_rows = 3 * BS // 4 + 8

    lat = latitude_matrix(lat_len, kept)
    sent, table, *fetched = pl.pallas_call(
        forward_lon_kernel,
        out_shape=(
            pltpu.VMEM((parts, height, LANES), BF),
            pltpu.VMEM((LON * rows, per), BF),
            pltpu.VMEM((2, BS, 2 * LANES), BF),
            pltpu.VMEM((2, BS, 2 * LANES), BF),
            pltpu.VMEM((2, 2 * LANES), F32),
            pltpu.VMEM(lat.shape, BF),
            pltpu.VMEM(lat.shape, BF),
        ),
        in_specs=[whole(pl.ANY)] * 10,
        out_specs=(whole(),) * 7,
        scratch_shapes=[
            pltpu.VMEM((2, LON, rows, C), BF),
            pltpu.VMEM((2, lat_len, 2, 1, C), jnp.int32),
            pltpu.SMEM((kept,), jnp.int32),
            pltpu.SemaphoreType.DMA((10,)),
        ],
        compiler_params=params,
        name="forward_lon",
    )(
        *(
            pltpu.with_memory_space_constraint(array, pltpu.HBM)
            for array in (
                lon_keep,
                activations[0].transpose(1, 0, 2),
                cotangent[0].transpose(1, 0, 2),
                relu_mask[0],
                shrink_mask[0],
                w_first.transpose(0, 2, 1),
                w_second.transpose(0, 2, 1),
                b_first,
                jnp.asarray(lat, BF),
                jnp.asarray(lat.T, BF),
            )
        )
    )
    pieces = lax.all_to_all(sent, "space", 0, 0, tiled=True)

    *fetched, lat_t = fetched
    terms, grad_pre, first_block = pl.pallas_call(
        functools.partial(spectral_kernel, ortho_scale=ortho_scale, rows=rows, kept=kept),
        out_shape=(
            jax.ShapeDtypeStruct((2, 2, term_rows, LANES), BF),
            pltpu.VMEM((lat.shape[0], LANES), BF),
            pltpu.VMEM((LANES, 2 * LANES), BF),
        ),
        in_specs=[whole()] * 5,
        out_specs=(whole(),) * 3,
        compiler_params=params,
        name="spectral",
    )(pieces, *fetched)
    grad_lat = pl.pallas_call(
        grad_lat_kernel,
        out_shape=jax.ShapeDtypeStruct((parts, 3 * per // 4, LANES), BF),
        in_specs=[whole()] * 3,
        out_specs=whole(),
        compiler_params=params,
        cost_estimate=pl.CostEstimate(
            flops=2 * lat.size * BS * 3, bytes_accessed=4 * lat.size, transcendentals=0
        ),
        name="grad_lat",
    )(grad_pre, first_block, lat_t)

    arrived = lax.ppermute(
        terms,
        ("dp", "space"),
        [
            (g * parts + c, (block_of(g, c) // 2) * parts + c)
            for g in range(groups)
            for c in range(parts)
        ],
    )
    other = lax.ppermute(arrived[1], "space", [(c, c ^ 1) for c in range(parts)])
    share = (arrived[0].astype(F32) + other.astype(F32)).astype(BF)
    share = jnp.broadcast_to(share[None], (parts // 2,) + share.shape)
    returned = lax.all_to_all(
        jnp.concatenate([grad_lat, share.reshape(parts, term_rows, LANES)], axis=1),
        "space",
        0,
        0,
        tiled=True,
    )
    others = lax.ppermute(returned[:, 3 * per // 4 :, :], "space", [(c, c ^ 1) for c in range(parts)])

    keep_rows = C // groups
    field = pl.pallas_call(
        functools.partial(inverse_lon_kernel, ortho_scale=ortho_scale),
        out_shape=jax.ShapeDtypeStruct((LON, rows, C), BF),
        in_specs=[whole(), whole()],
        out_specs=whole(pl.ANY),
        scratch_shapes=[
            pltpu.VMEM((LON, rows, C), BF),
            pltpu.SemaphoreType.DMA((2,)),
        ],
        compiler_params=params,
        cost_estimate=pl.CostEstimate(
            flops=2 * per * LON * rows * C, bytes_accessed=8 * LON * rows * C, transcendentals=0
        ),
        name="inverse_lon",
    )(table, returned)
    first, second, bias_first, bias_second = pl.pallas_call(
        functools.partial(gathered_kernel, grad_norm=grad_norm),
        out_shape=(
            jax.ShapeDtypeStruct((2, keep_rows, BS), F32),
            jax.ShapeDtypeStruct((2, keep_rows, BS), F32),
            jax.ShapeDtypeStruct((2, keep_rows), F32),
            jax.ShapeDtypeStruct((2, keep_rows), F32),
        ),
        in_specs=[whole(), whole()],
        out_specs=(whole(),) * 4,
        compiler_params=params,
        name="gathered",
    )(returned, others)
    return field.transpose(1, 0, 2)[None], first, second, bias_first, bias_second


def build_tables(lon_keep, lat_len, lon_len):
    columns = jnp.arange(lon_len, dtype=jnp.int32)
    lon_phase = columns[:, None] * lon_keep[None, :] % lon_len
    lon_angle = lon_phase.astype(jnp.float32) * (2.0 * math.pi / lon_len)
    lon_table = jnp.stack([jnp.cos(lon_angle), -jnp.sin(lon_angle)], axis=1).astype(jnp.bfloat16)
    latitudes = jnp.arange(lat_len, dtype=jnp.int32)
    lat_phase = latitudes[:, None] * latitudes[None, :] % lat_len
    lat_angle = lat_phase.astype(jnp.float32) * (2.0 * math.pi / lat_len)
    cosine = jnp.cos(lat_angle)
    sine_part = jnp.sin(lat_angle)
    lat_table = jnp.stack(
        [jnp.stack([cosine, sine_part], axis=-1), jnp.stack([-sine_part, cosine], axis=-1)], axis=1
    ).astype(jnp.bfloat16)
    return (lon_table, lat_table)


def apply_blocks(operand, matrix):
    return jnp.einsum("smjbc,bcd->smjbd", operand, matrix, preferred_element_type=jnp.float32)


def adjoint(operand, matrix):
    return jnp.einsum("smjbd,bcd->smjbc", operand, matrix, preferred_element_type=jnp.float32)


def outer_sum(operand, other):
    return jnp.einsum("smjbc,smjbd->bcd", operand, other, preferred_element_type=jnp.float32)


def by_frequencies(
    activations, cotangent, w_first, w_second, b_first, lon_keep, relu_mask, shrink_mask
):
    parts = lax.axis_size("space")
    samples_dev = activations.shape[0]
    lat_len = activations.shape[1] * parts
    kept = lon_keep.shape[0]
    owned = kept // parts
    lon_table, lat_table = build_tables(lon_keep, lat_len, LON)
    ortho_scale = 1.0 / math.sqrt(lat_len * LON)
    act_lon = jnp.einsum(
        "shwc,wpk->shpkc", activations, lon_table, preferred_element_type=jnp.float32
    ).astype(jnp.bfloat16)
    cot_lon = jnp.einsum(
        "shwc,wpk->shpkc", cotangent, lon_table, preferred_element_type=jnp.float32
    ).astype(jnp.bfloat16)
    act_modes, cot_modes = (
        lax.all_to_all(act_lon, "space", split_axis=3, concat_axis=1, tiled=True),
        lax.all_to_all(cot_lon, "space", split_axis=3, concat_axis=1, tiled=True),
    )

    def latitude(modes):
        summed = jnp.einsum(
            "mphq,shqjc->smpjc", lat_table, modes, preferred_element_type=jnp.float32
        )
        return (summed * ortho_scale).astype(jnp.bfloat16)

    block_shape = (samples_dev, lat_len, 2, owned, BLOCKS, BS)
    spec_act = latitude(act_modes).reshape(block_shape)
    spec_cot = latitude(cot_modes)
    own_keep = lax.dynamic_slice_in_dim(lon_keep, lax.axis_index("space") * owned, owned)
    doubled = jnp.where((own_keep == 0) | (2 * own_keep == LON), 1.0, 2.0).astype(jnp.float32)
    grad_out = (
        jnp.where(
            shrink_mask > 0, doubled[None, None, None, :, None] * spec_cot.astype(jnp.float32), 0.0
        )
        .astype(jnp.bfloat16)
        .reshape(block_shape)
    )
    relu_gate = relu_mask.reshape(block_shape) > 0
    first_blocks = w_first.reshape(2, BLOCKS, BS, BS)
    second_blocks = w_second.reshape(2, BLOCKS, BS, BS)
    bias_blocks = b_first.reshape(2, BLOCKS, BS)
    act_real = spec_act[:, :, 0]
    act_imag = spec_act[:, :, 1]
    pre_real = (
        apply_blocks(act_real, first_blocks[0])
        - apply_blocks(act_imag, first_blocks[1])
        + bias_blocks[0]
    )
    pre_imag = (
        apply_blocks(act_real, first_blocks[1])
        + apply_blocks(act_imag, first_blocks[0])
        + bias_blocks[1]
    )
    hidden = jnp.where(relu_gate, jnp.stack([pre_real, pre_imag], axis=2), 0.0).astype(jnp.bfloat16)
    out_real = grad_out[:, :, 0]
    out_imag = grad_out[:, :, 1]
    hidden_real = adjoint(out_real, second_blocks[0]) + adjoint(out_imag, second_blocks[1])
    hidden_imag = -adjoint(out_real, second_blocks[1]) + adjoint(out_imag, second_blocks[0])
    grad_pre = jnp.where(relu_gate, jnp.stack([hidden_real, hidden_imag], axis=2), 0.0).astype(
        jnp.bfloat16
    )
    pre_grad_real = grad_pre[:, :, 0]
    pre_grad_imag = grad_pre[:, :, 1]
    spec_real = adjoint(pre_grad_real, first_blocks[0]) + adjoint(pre_grad_imag, first_blocks[1])
    spec_imag = -adjoint(pre_grad_real, first_blocks[1]) + adjoint(pre_grad_imag, first_blocks[0])
    grad_spec = (
        jnp.stack([spec_real, spec_imag], axis=2)
        .astype(jnp.bfloat16)
        .reshape(samples_dev, lat_len, 2, owned, C)
    )
    first_grad = jnp.stack(
        [
            outer_sum(act_real, pre_grad_real) + outer_sum(act_imag, pre_grad_imag),
            outer_sum(act_real, pre_grad_imag) - outer_sum(act_imag, pre_grad_real),
        ]
    ).reshape(2, C, BS)
    hid_real = hidden[:, :, 0]
    hid_imag = hidden[:, :, 1]
    second_grad = jnp.stack(
        [
            outer_sum(hid_real, out_real) + outer_sum(hid_imag, out_imag),
            outer_sum(hid_real, out_imag) - outer_sum(hid_imag, out_real),
        ]
    ).reshape(2, C, BS)
    bias_first = jnp.sum(grad_pre, axis=(0, 1, 3), dtype=jnp.float32).reshape(2, C)
    bias_second = jnp.sum(grad_out, axis=(0, 1, 3), dtype=jnp.float32).reshape(2, C)
    local_terms = (first_grad, second_grad, bias_first, bias_second)
    summed = lax.psum(
        (local_terms[0], local_terms[1], local_terms[2], local_terms[3]), ("dp", "space")
    )
    share_rows = C // lax.axis_size("dp")
    row_start = lax.axis_index("dp") * share_rows

    def take_share(array):
        return lax.dynamic_slice_in_dim(array, row_start, share_rows, 1)

    totals = jax.tree.map(take_share, summed)
    grad_norm = 1.0 / math.sqrt(samples_dev * lax.axis_size("dp") * lat_len * kept)
    grad_lat = jnp.einsum(
        "mqhp,smqjc->shpjc", lat_table, grad_spec, preferred_element_type=jnp.float32
    ).astype(jnp.bfloat16)
    returned = lax.all_to_all(grad_lat, "space", split_axis=1, concat_axis=3, tiled=True)
    grad_field = (
        jnp.einsum("wpk,shpkc->shwc", lon_table, returned, preferred_element_type=jnp.float32)
        * ortho_scale
    ).astype(jnp.bfloat16)
    return (
        grad_field,
        totals[0] * grad_norm,
        totals[1] * grad_norm,
        totals[2] * grad_norm,
        totals[3] * grad_norm,
    )


def solution(mesh):
    groups, parts = mesh.shape["dp"], mesh.shape["space"]

    def per_device(*arrays):
        activations, lon_keep = arrays[0], arrays[5]
        fits = (
            parts == BLOCKS
            and 2 * groups == BLOCKS
            and activations.shape[:2] == (1, 2)
            and lon_keep.shape[0] == parts
        )
        return by_blocks(*arrays) if fits else by_frequencies(*arrays)

    return jax.shard_map(
        per_device,
        mesh=mesh,
        in_specs=(
            P("dp", "space", None, None),
            P("dp", "space", None, None),
            P(),
            P(),
            P(),
            P(),
            P("dp", None, None, "space", None),
            P("dp", None, None, "space", None),
        ),
        out_specs=(
            P("dp", "space", None, None),
            P(None, "dp", None),
            P(None, "dp", None),
            P(None, "dp"),
            P(None, "dp"),
        ),
        check_vma=False,
    )
```
